32 devices in a mesh: seq: 16 (over z, y, core), head: 2 (over x).
Axes of the slice: x: 2, y: 2, z: 4, core: 2. Of those that a mesh axis runs over, the one named last changes fastest.
Arguments:
- query: bfloat16 [8192, 32, 128], P('seq', 'head'), may hold values from -6 to 6
- key: bfloat16 [8192, 16, 128], P('seq', 'head'), may hold values from -6 to 6
- value: bfloat16 [8192, 16, 128], P('seq', 'head'), may hold values from -6 to 6
- grad_out: bfloat16 [8192, 32, 128], P('seq', 'head'), may hold values from -25 to 25
- q_gain: float32 [128], replicated, may hold values from 0.1 to 1.9
- k_gain: float32 [128], replicated, may hold values from 0.1 to 1.9
Outputs:
- grad_query: bfloat16 [8192, 32, 128], P('seq', 'head')
- grad_key: bfloat16 [8192, 16, 128], P('seq', 'head')
- grad_value: bfloat16 [8192, 16, 128], P('seq', 'head')
- grad_q_gain: float32 [128], replicated
- grad_k_gain: float32 [128], replicated
The draws below stay inside these ranges and needn't reach their ends.
All inputs are finite; a program needn't handle non-finite values.
Results may differ from the reference program's by a relative error of at most 0.0099.
Values may be sent and summed in bfloat16 or wider, within the bound.
No kernel may reach another device: no remote copies, remote signals or barrier semaphores. Data moves between devices by JAX's collectives and lax.ppermute only.
A program may use at most 128 MiB of HBM per device.

```python
import jax
import jax.numpy as jnp
from jax import lax

QUERY_HEADS = 32
KEY_VALUE_HEADS = 16
HEAD_SIZE = 128
WINDOW = 1024
TOKENS_PER_SHARD = 512
DOCUMENT_TOKENS = 8192


def draw_grad_out(key, part):
    first_key = jax.random.fold_in(jax.random.fold_in(key, 7), 0)
    array_shape = (DOCUMENT_TOKENS, QUERY_HEADS, HEAD_SIZE)
    ramp_pos = jnp.arange(DOCUMENT_TOKENS, dtype=jnp.float32) / (DOCUMENT_TOKENS - 1)
    ramp_scale = jnp.power(3.0, ramp_pos)
    base_part = jnp.clip(jax.random.normal(first_key, array_shape, jnp.float32), -4.0, 4.0)
    return (base_part * ramp_scale[:, None, None]).astype(jnp.bfloat16)


def shard_levels(stream_key, shape, pieces, low, largest):
    factor_of = 1.0
    for position, blocks in pieces:
        heights = jax.random.uniform(jax.random.fold_in(jax.random.fold_in(stream_key, 6), position), (blocks,), jnp.float32, low / len(pieces), largest / len(pieces))
        factor_of = factor_of * jnp.repeat(jnp.exp(heights), shape[position] // blocks).reshape((-1,) + (1,) * (len(shape) - 1 - position))
    return factor_of


def gaussian(own_key, extent, scale, most, shards=(), held_as=jnp.bfloat16):
    array = scale * jax.random.normal(own_key, extent, jnp.float32)
    if shards:
        array = array * shard_levels(own_key, extent, shards, -0.22, 0.18)
    return jnp.clip(array, -most, most).astype(held_as)


def setup_inputs(seed: int = 0) -> dict:
    key_list = jax.random.split(jax.random.key(seed), 7)
    query = gaussian(key_list[0], (DOCUMENT_TOKENS, QUERY_HEADS, HEAD_SIZE), 1.0, 6.0, ((0, 16), (1, 2)))
    key = gaussian(key_list[1], (DOCUMENT_TOKENS, KEY_VALUE_HEADS, HEAD_SIZE), 1.0, 6.0, ((0, 16), (1, 2)))
    value = gaussian(key_list[2], (DOCUMENT_TOKENS, KEY_VALUE_HEADS, HEAD_SIZE), 1.0, 6.0, ((0, 16), (1, 2)))
    grad_out = draw_grad_out(jax.random.fold_in(key_list[6], 71), 0)
    q_gain = jnp.clip(1.0 + 0.18 * jax.random.normal(key_list[4], (HEAD_SIZE,), jnp.float32), 0.1, 1.9)
    k_gain = jnp.clip(1.0 + 0.18 * jax.random.normal(key_list[5], (HEAD_SIZE,), jnp.float32), 0.1, 1.9)
    return {"query": query, "key": key, "value": value, "grad_out": grad_out, "q_gain": q_gain, "k_gain": k_gain}


score_scale = 168.0 ** (-0.5)
norm_eps = 1e-06

def normalize(inputs_raw, gain_vec):
    as_float = inputs_raw.astype(jnp.float32)
    inverse_rms = lax.rsqrt(lax.optimization_barrier(jnp.mean(as_float * as_float, axis=-1, keepdims=True)) + norm_eps)
    unit_rows = as_float * inverse_rms
    return (unit_rows * gain_vec, unit_rows, inverse_rms)

def norm_back(d_normed, unit_rows, inverse_rms, gain_vec):
    d_unit = d_normed * gain_vec
    d_inputs = inverse_rms * (d_unit - unit_rows * lax.optimization_barrier(jnp.mean(d_unit * unit_rows, axis=-1, keepdims=True)))
    d_gain = lax.optimization_barrier(jnp.sum(d_normed * unit_rows, axis=(0, 1)))
    return (d_inputs, d_gain)

def reference(query, key, value, grad_out, q_gain, k_gain):
    reach_total = (WINDOW + TOKENS_PER_SHARD - 1) // TOKENS_PER_SHARD
    key_span = (reach_total + 1) * TOKENS_PER_SHARD
    heads_per_group = QUERY_HEADS // KEY_VALUE_HEADS
    q_normed, q_unit, q_inverse = normalize(query, q_gain)
    k_normed, k_unit, k_inverse = normalize(key, k_gain)
    query_low = q_normed.astype(jnp.bfloat16)
    key_low = k_normed.astype(jnp.bfloat16)
    pad_amount = jnp.zeros((reach_total * TOKENS_PER_SHARD, KEY_VALUE_HEADS, HEAD_SIZE), jnp.bfloat16)
    key_pad = jnp.concatenate([pad_amount, key_low], axis=0)
    value_pad = jnp.concatenate([pad_amount, value], axis=0)
    row_ids = jnp.arange(TOKENS_PER_SHARD, dtype=jnp.int32)[:, None]
    col_ids = jnp.arange(key_span, dtype=jnp.int32)[None, :]
    distance_grid = row_ids + reach_total * TOKENS_PER_SHARD - col_ids
    base_allowed = (distance_grid >= 0) & (distance_grid < WINDOW)

    def block_step(totals, block_id):
        key_total, value_total = totals
        start_row = block_id * TOKENS_PER_SHARD
        query_block = lax.dynamic_slice_in_dim(query_low, start_row, TOKENS_PER_SHARD, 0)
        incoming_gradient = lax.dynamic_slice_in_dim(grad_out, start_row, TOKENS_PER_SHARD, 0)
        key_blk = lax.dynamic_slice_in_dim(key_pad, start_row, key_span, 0)
        value_blk = lax.dynamic_slice_in_dim(value_pad, start_row, key_span, 0)
        allowed = base_allowed & (col_ids + start_row >= reach_total * TOKENS_PER_SHARD)
        query_float32 = query_block.reshape(TOKENS_PER_SHARD, KEY_VALUE_HEADS, heads_per_group, HEAD_SIZE).astype(jnp.float32)
        incoming_gradient_float32 = incoming_gradient.reshape(TOKENS_PER_SHARD, KEY_VALUE_HEADS, heads_per_group, HEAD_SIZE).astype(jnp.float32)
        key_f32 = key_blk.astype(jnp.float32)
        value_f32 = value_blk.astype(jnp.float32)
        scores = score_scale * jnp.einsum('tkgd,skd->kgts', query_float32, key_f32)
        exp_scores = jnp.where(allowed[None, None], jnp.exp(scores), 0.0)
        attn_probs = exp_scores / lax.optimization_barrier(jnp.sum(exp_scores, axis=-1, keepdims=True))
        probs_low = lax.optimization_barrier(attn_probs.astype(jnp.bfloat16)).astype(jnp.float32)
        attended = jnp.einsum('kgts,skd->tkgd', probs_low, value_f32)
        offset = jnp.einsum('tkgd,tkgd->kgt', incoming_gradient_float32, attended)[..., None]
        d_probs = jnp.einsum('tkgd,skd->kgts', incoming_gradient_float32, value_f32)
        d_scores = lax.optimization_barrier((attn_probs * (d_probs - offset)).astype(jnp.bfloat16)).astype(jnp.float32)
        value_grad = jnp.einsum('kgts,tkgd->skd', probs_low, incoming_gradient_float32)
        query_grad = score_scale * jnp.einsum('kgts,skd->tkgd', d_scores, key_f32)
        key_grad = score_scale * jnp.einsum('kgts,tkgd->skd', d_scores, query_float32)
        key_total = lax.dynamic_update_slice_in_dim(key_total, lax.dynamic_slice_in_dim(key_total, start_row, key_span, 0) + key_grad, start_row, 0)
        value_total = lax.dynamic_update_slice_in_dim(value_total, lax.dynamic_slice_in_dim(value_total, start_row, key_span, 0) + value_grad, start_row, 0)
        return ((key_total, value_total), query_grad.reshape(TOKENS_PER_SHARD, QUERY_HEADS, HEAD_SIZE))
    blank_array = jnp.zeros((DOCUMENT_TOKENS + reach_total * TOKENS_PER_SHARD, KEY_VALUE_HEADS, HEAD_SIZE), jnp.float32)
    (key_total, value_total), query_parts = lax.scan(block_step, (blank_array, blank_array), jnp.arange(DOCUMENT_TOKENS // TOKENS_PER_SHARD, dtype=jnp.int32))
    query_grad_n = query_parts.reshape(DOCUMENT_TOKENS, QUERY_HEADS, HEAD_SIZE)
    key_grad_n = key_total[reach_total * TOKENS_PER_SHARD:]
    grad_value = value_total[reach_total * TOKENS_PER_SHARD:].astype(jnp.bfloat16)
    grad_query, grad_q_gain = norm_back(query_grad_n, q_unit, q_inverse, q_gain)
    grad_key, grad_k_gain = norm_back(key_grad_n, k_unit, k_inverse, k_gain)
    return (grad_query.astype(jnp.bfloat16), grad_key.astype(jnp.bfloat16), grad_value, grad_q_gain, grad_k_gain)
```

```python
import functools

import jax
import jax.numpy as jnp
from jax import lax
from jax.experimental import pallas as pl
from jax.experimental.pallas import tpu as pltpu
from jax.sharding import PartitionSpec as P

WINDOW = 1024
TILE = 128

score_scale = 168.0 ** (-0.5)
norm_eps = 1e-06
exp2_scale = score_scale * 1.4426950408889634

NT = (((1,), (1,)), ((), ()))


def inverse_rms_of(as_float):
    return lax.rsqrt(jnp.mean(as_float * as_float, axis=-1, keepdims=True) + norm_eps)


def norm_back(d_normed, raw, inverse_rms, gain_vec):
    unit_rows = raw * inverse_rms
    d_unit = d_normed * gain_vec
    return inverse_rms * (
        d_unit - unit_rows * jnp.mean(d_unit * unit_rows, axis=-1, keepdims=True)
    )


def heads_kernel(
    shard_ref, q_ref, g_ref, own_ref, near_ref, far_ref, q_gain_ref, k_gain_ref,
    dq_ref, d_own_ref, d_near_ref, d_far_ref, gains_ref,
    k_low, k_low_t, values, q_low, probs_all, d_scores_all,
):
    rows = own_ref.shape[2]
    group = q_ref.shape[1] // rows
    lanes = TILE * group
    blocks = rows // TILE
    tiles = WINDOW // TILE
    q_gain, k_gain = q_gain_ref[...], k_gain_ref[...]
    far_ok = jnp.where(shard_ref[0] >= 2, 1.0, 0.0)
    near_ok = jnp.where(shard_ref[0] >= 1, 1.0, 0.0)
    key_refs = (far_ref, near_ref, own_ref)

    @pl.when(pl.program_id(0) == 0)
    def _():
        gains_ref[...] = jnp.zeros_like(gains_ref)

    for place, ref in enumerate(key_refs):
        raw = ref[0, 0].astype(jnp.float32)
        here = slice(place * rows, (place + 1) * rows)
        k_low[here, :] = (raw * inverse_rms_of(raw) * k_gain).astype(jnp.bfloat16)
        values[here, :] = ref[0, 1]
    k_low_t[...] = k_low[...].T
    raw_q = q_ref[0].astype(jnp.float32)
    q_low[...] = (raw_q * inverse_rms_of(raw_q) * q_gain).astype(jnp.bfloat16)

    key_ids = lax.broadcasted_iota(jnp.int32, (TILE, lanes), 0)
    token_ids = lax.broadcasted_iota(jnp.int32, (TILE, lanes), 1) // group
    late = key_ids <= token_ids
    edge_ok = jnp.where(late, 1.0, far_ok)
    q_gain_sum = jnp.zeros_like(q_gain)

    for block in range(blocks):
        span = slice(block * TILE, block * TILE + WINDOW + TILE)
        mine = slice(block * lanes, (block + 1) * lanes)
        scores = lax.dot_general(
            k_low[span, :], q_low[mine, :], NT, preferred_element_type=jnp.float32
        )
        scores = jnp.concatenate(
            [jnp.where(late, scores[WINDOW:], scores[:TILE]), scores[TILE:WINDOW]], axis=0
        )
        exp_scores = jnp.exp2(scores * exp2_scale)
        edge = exp_scores[:TILE] * edge_ok
        first_near = (blocks - block) * TILE
        first_own = first_near + rows
        total = jnp.sum(edge, axis=0, keepdims=True)
        for low, high, ok in (
            (TILE, first_near, far_ok),
            (first_near, min(first_own, WINDOW), near_ok),
            (first_own, WINDOW, None),
        ):
            if low < high:
                part = jnp.sum(exp_scores[low:high], axis=0, keepdims=True)
                total = total + (part if ok is None else part * ok)
        inverse = 1.0 / total
        probs = jnp.concatenate([edge, exp_scores[TILE:]], axis=0) * inverse
        d_probs = lax.dot_general(
            values[span, :], g_ref[0, mine, :], NT, preferred_element_type=jnp.float32
        )
        d_probs = jnp.concatenate(
            [jnp.where(late, d_probs[WINDOW:], d_probs[:TILE]), d_probs[TILE:WINDOW]], axis=0
        )
        offset = jnp.sum(probs * d_probs, axis=0, keepdims=True)
        d_scores = probs * (d_probs - offset)
        for whole, held in ((probs, probs_all), (d_scores, d_scores_all)):
            start = block * TILE
            held[start : start + TILE, mine] = jnp.where(late, 0.0, whole[:TILE]).astype(
                jnp.bfloat16
            )
            held[start + TILE : start + WINDOW, mine] = whole[TILE:].astype(jnp.bfloat16)
            held[start + WINDOW : start + WINDOW + TILE, mine] = jnp.where(
                late, whole[:TILE], 0.0
            ).astype(jnp.bfloat16)
        query_grad = score_scale * jnp.dot(
            k_low_t[:, span], d_scores_all[span, mine], preferred_element_type=jnp.float32
        ).T
        raw = q_ref[0, mine, :].astype(jnp.float32)
        inverse_rms = inverse_rms_of(raw)
        q_gain_sum = q_gain_sum + jnp.sum(query_grad * (raw * inverse_rms), axis=0, keepdims=True)
        dq_ref[0, mine, :] = norm_back(query_grad, raw, inverse_rms, q_gain).astype(dq_ref.dtype)

    pieces = [(tile, tile + 1, 0, tile + 1) for tile in range(blocks - 1)]
    pieces += [(blocks - 1, tiles + 1, 0, blocks)]
    pieces += [(tiles + block, tiles + block + 1, block, blocks) for block in range(1, blocks)]
    k_gain_sum = jnp.zeros_like(k_gain)
    for first, last, low, high in pieces:
        meets = slice(low * lanes, high * lanes)
        keys = slice(first * TILE, last * TILE)
        value_grad = jnp.dot(
            probs_all[keys, meets], g_ref[0, meets, :], preferred_element_type=jnp.float32
        )
        key_grad = score_scale * jnp.dot(
            d_scores_all[keys, meets], q_low[meets, :], preferred_element_type=jnp.float32
        )
        for place, (ref, out) in enumerate(
            ((far_ref, d_far_ref), (near_ref, d_near_ref), (own_ref, d_own_ref))
        ):
            start = max(first * TILE, place * rows)
            stop = min(last * TILE, (place + 1) * rows)
            if start >= stop:
                continue
            inside = slice(start - place * rows, stop - place * rows)
            here = slice(start - first * TILE, stop - first * TILE)
            raw = ref[0, 0, inside, :].astype(jnp.float32)
            k_gain_sum = k_gain_sum + jnp.sum(
                key_grad[here] * (raw * inverse_rms_of(raw)), axis=0, keepdims=True
            )
            out[0, 0, inside, :] = key_grad[here].astype(out.dtype)
            out[0, 1, inside, :] = value_grad[here].astype(out.dtype)
    gains_ref[0:1, :] += q_gain_sum
    gains_ref[1:2, :] += k_gain_sum


def group_grads(shard, first, queries, grads, own, near, far, q_gain, k_gain):
    count, _, rows, width = near.shape
    query_rows = queries.shape[1]
    span = WINDOW + rows
    whole_q = pl.BlockSpec((1, query_rows, width), lambda head: (first + head, 0, 0))
    part = pl.BlockSpec((1, 2, rows, width), lambda head: (head, 0, 0, 0))
    gain = pl.BlockSpec((1, width), lambda head: (0, 0))
    flops = 2 * 5 * count * query_rows * (WINDOW + TILE) * width
    return pl.pallas_call(
        heads_kernel,
        grid=(count,),
        in_specs=[
            pl.BlockSpec(memory_space=pltpu.SMEM),
            whole_q,
            whole_q,
            pl.BlockSpec((1, 2, rows, width), lambda head: (first + head, 0, 0, 0)),
            part,
            part,
            gain,
            gain,
        ],
        out_specs=[
            pl.BlockSpec((1, query_rows, width), lambda head: (head, 0, 0)),
            part,
            part,
            part,
            pl.BlockSpec((2, width), lambda head: (0, 0)),
        ],
        out_shape=[
            jax.ShapeDtypeStruct((count, query_rows, width), jnp.bfloat16),
            jax.ShapeDtypeStruct(near.shape, jnp.float32),
            jax.ShapeDtypeStruct(near.shape, jnp.bfloat16),
            jax.ShapeDtypeStruct(near.shape, jnp.bfloat16),
            jax.ShapeDtypeStruct((2, width), jnp.float32),
        ],
        scratch_shapes=[
            pltpu.VMEM((span, width), jnp.bfloat16),
            pltpu.VMEM((width, span), jnp.bfloat16),
            pltpu.VMEM((span, width), jnp.bfloat16),
            pltpu.VMEM((query_rows, width), jnp.bfloat16),
            pltpu.VMEM((span, query_rows), jnp.bfloat16),
            pltpu.VMEM((span, query_rows), jnp.bfloat16),
        ],
        compiler_params=pltpu.CompilerParams(vmem_limit_bytes=40 * 1024 * 1024),
        cost_estimate=pl.CostEstimate(
            flops=2 * flops,
            bytes_accessed=count * (6 * query_rows + 20 * rows) * width,
            transcendentals=count * query_rows * WINDOW,
        ),
    )(shard, queries, grads, own, near, far, q_gain, k_gain)


def group_sizes(kv_dev):
    half = (kv_dev + 1) // 2
    return [size for size in (half, kv_dev - half) if size]


def per_device(query, key, value, grad_out, q_gain, k_gain):
    rows, heads, width = query.shape
    kv_dev = key.shape[1]
    group = heads // kv_dev
    count = lax.axis_size("seq")
    assert 2 * rows == WINDOW and rows % TILE == 0 and count % 2 == 0
    shard = lax.axis_index("seq")
    odd = shard % 2 == 1
    ahead = [(source, source + 2) for source in range(count - 2)]
    back = [(source + 2, source) for source in range(count - 2)]
    swap = [(source, source ^ 1) for source in range(count)]

    def by_head(array):
        split = array.reshape(rows, kv_dev, group, width)
        return jnp.transpose(split, (1, 0, 2, 3)).reshape(kv_dev, rows * group, width)

    own = jnp.transpose(jnp.stack([key, value]), (2, 0, 1, 3))
    sizes = group_sizes(kv_dev)
    starts = [sum(sizes[:place]) for place in range(len(sizes))]
    fars = [
        lax.ppermute(own[first : first + size], "seq", ahead)
        for first, size in zip(starts, sizes, strict=True)
    ]
    queries, grads = by_head(query), by_head(grad_out)
    scalar = shard.astype(jnp.int32).reshape(1)
    gains_2d = (q_gain.reshape(1, width), k_gain.reshape(1, width))
    dq_parts, key_parts, value_parts, gain_sum = [], [], [], 0.0
    for first, size, far in zip(starts, sizes, fars, strict=True):
        mine = own[first : first + size]
        near = lax.ppermute(jnp.where(odd, far, mine), "seq", swap)
        dq, d_own, d_near, d_far, gains = group_grads(
            scalar, first, queries, grads, own, near, far, *gains_2d
        )
        swapped = lax.ppermute(d_near, "seq", swap).astype(jnp.float32)
        relayed = (d_far.astype(jnp.float32) + jnp.where(odd, swapped, 0.0)).astype(jnp.bfloat16)
        returned = lax.ppermute(relayed, "seq", back).astype(jnp.float32)
        total = d_own + returned + jnp.where(odd, 0.0, swapped)
        raw = mine[:, 0].astype(jnp.float32)
        key_grad = norm_back(total[:, 0], raw, inverse_rms_of(raw), k_gain)
        dq_parts.append(dq)
        key_parts.append(key_grad.astype(jnp.bfloat16))
        value_parts.append(total[:, 1].astype(jnp.bfloat16))
        gain_sum = gain_sum + gains
    gain_sum = jnp.sum(lax.all_gather(gain_sum, ("seq", "head")), axis=0)
    grad_query = jnp.concatenate(dq_parts).reshape(kv_dev, rows, group, width)
    grad_query = jnp.transpose(grad_query, (1, 0, 2, 3)).reshape(rows, heads, width)
    grad_key = jnp.transpose(jnp.concatenate(key_parts), (1, 0, 2))
    grad_value = jnp.transpose(jnp.concatenate(value_parts), (1, 0, 2))
    return (grad_query, grad_key, grad_value, gain_sum[0], gain_sum[1])


def solution(mesh):
    split, whole = P("seq", "head", None), P()
    return jax.shard_map(
        per_device,
        mesh=mesh,
        in_specs=(split, split, split, split, whole, whole),
        out_specs=(split, split, split, whole, whole),
        check_vma=False,
    )
```

```python
import functools

import jax
import jax.numpy as jnp
from jax import lax
from jax.experimental import pallas as pl
from jax.experimental.pallas import tpu as pltpu
from jax.sharding import PartitionSpec as P

WINDOW = 1024
TILE = 128

score_scale = 168.0 ** (-0.5)
norm_eps = 1e-06
exp2_scale = score_scale * 1.4426950408889634

GROUPS = 3

NT = (((1,), (1,)), ((), ()))


def inverse_rms_of(as_float):
    return lax.rsqrt(jnp.mean(as_float * as_float, axis=-1, keepdims=True) + norm_eps)


def norm_back(d_normed, raw, inverse_rms, gain_vec):
    unit_rows = raw * inverse_rms
    d_unit = d_normed * gain_vec
    return inverse_rms * (
        d_unit - unit_rows * jnp.mean(d_unit * unit_rows, axis=-1, keepdims=True)
    )


def heads_kernel(
    shard_ref, q_ref, g_ref, own_ref, near_ref, far_ref, q_gain_ref, k_gain_ref,
    dq_ref, d_own_ref, d_near_ref, d_far_ref, gains_ref,
    k_low, k_low_t, values, q_low, probs_all, d_scores_all,
):
    rows = own_ref.shape[2]
    group = q_ref.shape[1] // rows
    lanes = TILE * group
    blocks = rows // TILE
    tiles = WINDOW // TILE
    q_gain, k_gain = q_gain_ref[...], k_gain_ref[...]
    far_ok = jnp.where(shard_ref[0] >= 2, 1.0, 0.0)
    near_ok = jnp.where(shard_ref[0] >= 1, 1.0, 0.0)
    key_refs = (far_ref, near_ref, own_ref)

    @pl.when(pl.program_id(0) == 0)
    def _():
        gains_ref[...] = jnp.zeros_like(gains_ref)

    for place, ref in enumerate(key_refs):
        raw = ref[0, 0].astype(jnp.float32)
        here = slice(place * rows, (place + 1) * rows)
        k_low[here, :] = (raw * inverse_rms_of(raw) * k_gain).astype(jnp.bfloat16)
        values[here, :] = ref[1, 0]
    k_low_t[...] = k_low[...].T
    raw_q = q_ref[0].astype(jnp.float32)
    q_low[...] = (raw_q * inverse_rms_of(raw_q) * q_gain).astype(jnp.bfloat16)

    key_ids = lax.broadcasted_iota(jnp.int32, (TILE, lanes), 0)
    token_ids = lax.broadcasted_iota(jnp.int32, (TILE, lanes), 1) // group
    late = key_ids <= token_ids
    edge_ok = jnp.where(late, 1.0, far_ok)
    q_gain_sum = jnp.zeros_like(q_gain)

    for block in range(blocks):
        span = slice(block * TILE, block * TILE + WINDOW + TILE)
        mine = slice(block * lanes, (block + 1) * lanes)
        scores = lax.dot_general(
            k_low[span, :], q_low[mine, :], NT, preferred_element_type=jnp.float32
        )
        scores = jnp.concatenate(
            [jnp.where(late, scores[WINDOW:], scores[:TILE]), scores[TILE:WINDOW]], axis=0
        )
        exp_scores = jnp.exp2(scores * exp2_scale)
        edge = exp_scores[:TILE] * edge_ok
        first_near = (blocks - block) * TILE
        first_own = first_near + rows
        total = jnp.sum(edge, axis=0, keepdims=True)
        for low, high, ok in (
            (TILE, first_near, far_ok),
            (first_near, min(first_own, WINDOW), near_ok),
            (first_own, WINDOW, None),
        ):
            if low < high:
                part = jnp.sum(exp_scores[low:high], axis=0, keepdims=True)
                total = total + (part if ok is None else part * ok)
        inverse = 1.0 / total
        probs = jnp.concatenate([edge, exp_scores[TILE:]], axis=0) * inverse
        d_probs = lax.dot_general(
            values[span, :], g_ref[0, mine, :], NT, preferred_element_type=jnp.float32
        )
        d_probs = jnp.concatenate(
            [jnp.where(late, d_probs[WINDOW:], d_probs[:TILE]), d_probs[TILE:WINDOW]], axis=0
        )
        offset = jnp.sum(probs * d_probs, axis=0, keepdims=True)
        d_scores = probs * (d_probs - offset)
        for whole, held in ((probs, probs_all), (d_scores, d_scores_all)):
            start = block * TILE
            held[start : start + TILE, mine] = jnp.where(late, 0.0, whole[:TILE]).astype(
                jnp.bfloat16
            )
            held[start + TILE : start + WINDOW, mine] = whole[TILE:].astype(jnp.bfloat16)
            held[start + WINDOW : start + WINDOW + TILE, mine] = jnp.where(
                late, whole[:TILE], 0.0
            ).astype(jnp.bfloat16)
        query_grad = score_scale * jnp.dot(
            k_low_t[:, span], d_scores_all[span, mine], preferred_element_type=jnp.float32
        ).T
        raw = q_ref[0, mine, :].astype(jnp.float32)
        inverse_rms = inverse_rms_of(raw)
        q_gain_sum = q_gain_sum + jnp.sum(query_grad * (raw * inverse_rms), axis=0, keepdims=True)
        dq_ref[0, mine, :] = norm_back(query_grad, raw, inverse_rms, q_gain).astype(dq_ref.dtype)

    pieces = [(tile, tile + 1, 0, tile + 1) for tile in range(blocks - 1)]
    pieces += [(blocks - 1, tiles + 1, 0, blocks)]
    pieces += [(tiles + block, tiles + block + 1, block, blocks) for block in range(1, blocks)]
    k_gain_sum = jnp.zeros_like(k_gain)
    for first, last, low, high in pieces:
        meets = slice(low * lanes, high * lanes)
        keys = slice(first * TILE, last * TILE)
        value_grad = jnp.dot(
            probs_all[keys, meets], g_ref[0, meets, :], preferred_element_type=jnp.float32
        )
        key_grad = score_scale * jnp.dot(
            d_scores_all[keys, meets], q_low[meets, :], preferred_element_type=jnp.float32
        )
        for place, (ref, out) in enumerate(
            ((far_ref, d_far_ref), (near_ref, d_near_ref), (own_ref, d_own_ref))
        ):
            start = max(first * TILE, place * rows)
            stop = min(last * TILE, (place + 1) * rows)
            if start >= stop:
                continue
            inside = slice(start - place * rows, stop - place * rows)
            here = slice(start - first * TILE, stop - first * TILE)
            raw = ref[0, 0, inside, :].astype(jnp.float32)
            k_gain_sum = k_gain_sum + jnp.sum(
                key_grad[here] * (raw * inverse_rms_of(raw)), axis=0, keepdims=True
            )
            out[0, 0, inside, :] = key_grad[here].astype(out.dtype)
            out[1, 0, inside, :] = value_grad[here].astype(out.dtype)
    gains_ref[0:1, :] += q_gain_sum
    gains_ref[1:2, :] += k_gain_sum


def closed(own, returned, swapped, keep, head):
    return [
        own[kind, head]
        + returned[kind, head].astype(jnp.float32)
        + keep * swapped[kind, head].astype(jnp.float32)
        for kind in range(2)
    ]


def close_kernel(shard_ref, own, returned, swapped, raw_ref, k_gain_ref, out):
    keep = jnp.where(shard_ref[0] % 2 == 1, 0.0, 1.0)
    key_grad, value_grad = closed(own, returned, swapped, keep, 0)
    raw = raw_ref[0, 0].astype(jnp.float32)
    key_grad = norm_back(key_grad, raw, inverse_rms_of(raw), k_gain_ref[...])
    out[0, 0] = key_grad.astype(out.dtype)
    out[1, 0] = value_grad.astype(out.dtype)


def finish_kernel(low, shard_ref, own, returned, swapped, raw_ref, k_gain_ref, *rest):
    *done, key_out, value_out, by_token = rest
    keep = jnp.where(shard_ref[0] % 2 == 1, 0.0, 1.0)
    before = [(part, head) for part in done for head in range(part.shape[1])]
    for kind, out in ((0, key_out), (1, value_out)):
        for place, (part, head) in enumerate(before):
            by_token[:, place, :] = part[kind, head].astype(jnp.float32)
        for head in range(own.shape[1]):
            grad = closed(own, returned, swapped, keep, head)[kind]
            if kind == 0:
                raw = raw_ref[0, low + head].astype(jnp.float32)
                grad = norm_back(grad, raw, inverse_rms_of(raw), k_gain_ref[...])
            by_token[:, len(before) + head, :] = grad
        out[...] = by_token[...].astype(out.dtype)


def group_grads(shard, first, here, count, queries, grads, own, near, far, q_gain, k_gain):
    _, _, rows, width = near.shape
    query_rows = queries.shape[1]
    span = WINDOW + rows
    whole_q = pl.BlockSpec((1, query_rows, width), lambda head: (first + head, 0, 0))
    held = pl.BlockSpec((2, 1, rows, width), lambda head: (0, here + head, 0, 0))
    part = pl.BlockSpec((2, 1, rows, width), lambda head: (0, head, 0, 0))
    gain = pl.BlockSpec((1, width), lambda head: (0, 0))
    shape = (2, count, rows, width)
    return pl.pallas_call(
        heads_kernel,
        grid=(count,),
        in_specs=[
            pl.BlockSpec(memory_space=pltpu.SMEM), whole_q, whole_q, held, held, held, gain, gain,
        ],
        out_specs=[
            pl.BlockSpec((1, query_rows, width), lambda head: (head, 0, 0)),
            part,
            part,
            part,
            pl.BlockSpec((2, width), lambda head: (0, 0)),
        ],
        out_shape=[
            jax.ShapeDtypeStruct((count, query_rows, width), jnp.bfloat16),
            jax.ShapeDtypeStruct(shape, jnp.float32),
            jax.ShapeDtypeStruct(shape, jnp.bfloat16),
            jax.ShapeDtypeStruct(shape, jnp.bfloat16),
            jax.ShapeDtypeStruct((2, width), jnp.float32),
        ],
        scratch_shapes=[
            pltpu.VMEM((span, width), jnp.bfloat16),
            pltpu.VMEM((width, span), jnp.bfloat16),
            pltpu.VMEM((span, width), jnp.bfloat16),
            pltpu.VMEM((query_rows, width), jnp.bfloat16),
            pltpu.VMEM((span, query_rows), jnp.bfloat16),
            pltpu.VMEM((span, query_rows), jnp.bfloat16),
        ],
        compiler_params=pltpu.CompilerParams(vmem_limit_bytes=40 * 1024 * 1024),
        cost_estimate=pl.CostEstimate(flops=1000, bytes_accessed=1000, transcendentals=0),
    )(shard, queries, grads, own, near, far, q_gain, k_gain)


def close_group(shard, own, returned, swapped, raw, low, k_gain):
    _, count, rows, width = own.shape
    part = pl.BlockSpec((2, 1, rows, width), lambda head: (0, head, 0, 0))
    return pl.pallas_call(
        close_kernel,
        grid=(count,),
        in_specs=[
            pl.BlockSpec(memory_space=pltpu.SMEM), part, part, part,
            pl.BlockSpec((2, 1, rows, width), lambda head: (0, low + head, 0, 0)),
            pl.BlockSpec((1, width), lambda head: (0, 0)),
        ],
        out_specs=part,
        out_shape=jax.ShapeDtypeStruct(own.shape, jnp.bfloat16),
    )(shard, own, returned, swapped, raw, k_gain)


def finish(shard, own, returned, swapped, raw, low, k_gain, done):
    _, count, rows, width = own.shape
    kv_dev = count + sum(part.shape[1] for part in done)
    shape = (rows, kv_dev, width)
    vmem = pl.BlockSpec(memory_space=pltpu.VMEM)
    return pl.pallas_call(
        functools.partial(finish_kernel, low),
        in_specs=[pl.BlockSpec(memory_space=pltpu.SMEM)] + [vmem] * (5 + len(done)),
        out_specs=[vmem, vmem],
        out_shape=[jax.ShapeDtypeStruct(shape, jnp.bfloat16)] * 2,
        scratch_shapes=[pltpu.VMEM(shape, jnp.float32)],
        compiler_params=pltpu.CompilerParams(vmem_limit_bytes=40 * 1024 * 1024),
    )(shard, own, returned, swapped, raw, k_gain, *done)


def group_sizes(kv_dev):
    count = min(GROUPS, kv_dev)
    return [(kv_dev + count - 1 - place) // count for place in range(count)]


def summed(value, axis):
    count = lax.axis_size(axis)
    if count & (count - 1):
        return lax.psum(value, axis)
    step = 1
    while step < count:
        pairs = [(source, source ^ step) for source in range(count)]
        value = value + lax.ppermute(value, axis, pairs)
        step *= 2
    return value


def per_device(query, key, value, grad_out, q_gain, k_gain):
    rows, heads, width = query.shape
    kv_dev = key.shape[1]
    group = heads // kv_dev
    count = lax.axis_size("seq")
    assert 2 * rows == WINDOW and rows % TILE == 0 and count % 2 == 0
    shard = lax.axis_index("seq")
    odd = shard % 2 == 1
    ahead = [(source, source + 2) for source in range(count - 2)]
    back = [(source + 2, source) for source in range(count - 2)]
    swap = [(source, source ^ 1) for source in range(count)]

    def by_head(array):
        split = array.reshape(rows, kv_dev, group, width)
        return jnp.transpose(split, (1, 0, 2, 3)).reshape(kv_dev, rows * group, width)

    sizes = group_sizes(kv_dev)
    starts = [sum(sizes[:place]) for place in range(len(sizes))]
    cuts = [(0, sizes[0])] + ([(sizes[0], kv_dev)] if len(sizes) > 1 else [])
    owns = [
        jnp.transpose(jnp.stack([key[:, low:high], value[:, low:high]]), (0, 2, 1, 3))
        for low, high in cuts
    ]
    fars = [lax.ppermute(own, "seq", ahead) for own in owns]
    queries, grads = by_head(query), by_head(grad_out)
    scalar = shard.astype(jnp.int32).reshape(1)
    q_gain_2d, k_gain_2d = q_gain.reshape(1, width), k_gain.reshape(1, width)

    def near_of(own, far):
        return lax.ppermute(jnp.where(odd, far, own), "seq", swap)

    dq_parts, done, gains, waiting, relayed = [], [], [], None, None
    for place, (first, size) in enumerate(zip(starts, sizes, strict=True)):
        if place < 2:
            own, far, base = owns[place], fars[place], cuts[place][0]
            if place:
                far, relayed = lax.optimization_barrier((far, relayed))
            else:
                far, *_ = lax.optimization_barrier((far, *owns[1:]))
            near = near_of(own, far)
        else:
            near, relayed, done[-1], gains[-1] = lax.optimization_barrier(
                (near, relayed, done[-1], gains[-1])
            )
        dq, d_own, d_near, d_far, gain = group_grads(
            scalar, first, first - base, size, queries, grads, own, near, far, q_gain_2d, k_gain_2d
        )
        dq_parts.append(dq)
        gains.append(gain)
        if waiting is not None:
            d_own_before, swapped, own_before, low = waiting
            returned = lax.ppermute(relayed, "seq", back)
            done.append(
                close_group(scalar, d_own_before, returned, swapped, own_before, low, k_gain_2d)
            )
        swapped = lax.ppermute(d_near, "seq", swap)
        relayed = d_far.astype(jnp.float32) + jnp.where(odd, swapped.astype(jnp.float32), 0.0)
        relayed = relayed.astype(jnp.bfloat16)
        waiting = (d_own, swapped, own, first - base)
    d_own, swapped, own, low = waiting
    if done:
        relayed, done[-1] = lax.optimization_barrier((relayed, done[-1]))
    returned = lax.ppermute(relayed, "seq", back)
    grad_key, grad_value = finish(scalar, d_own, returned, swapped, own, low, k_gain_2d, done)
    gain_sum = sum(gains[1:], gains[0])
    gain_sum = summed(summed(gain_sum, "seq"), "head")
    grad_query = jnp.concatenate(dq_parts).reshape(kv_dev, rows, group, width)
    grad_query = jnp.transpose(grad_query, (1, 0, 2, 3)).reshape(rows, heads, width)
    return (grad_query, grad_key, grad_value, gain_sum[0], gain_sum[1])


def solution(mesh):
    split, whole = P("seq", "head", None), P()
    return jax.shard_map(
        per_device,
        mesh=mesh,
        in_specs=(split, split, split, split, whole, whole),
        out_specs=(split, split, split, whole, whole),
        check_vma=False,
    )
```

```python
import functools

import jax
import jax.numpy as jnp
from jax import lax
from jax.experimental import pallas as pl
from jax.experimental.pallas import tpu as pltpu
from jax.sharding import PartitionSpec as P

WINDOW = 1024
TILE = 128

score_scale = 168.0 ** (-0.5)
norm_eps = 1e-06
exp2_scale = score_scale * 1.4426950408889634

GROUPS = 3
HEAVY = pl.CostEstimate(flops=10**11, bytes_accessed=10**8, transcendentals=0)
LIGHT = pl.CostEstimate(flops=1000, bytes_accessed=1000, transcendentals=0)

NT = (((1,), (1,)), ((), ()))


def inverse_rms_of(as_float):
    return lax.rsqrt(jnp.mean(as_float * as_float, axis=-1, keepdims=True) + norm_eps)


def norm_back(d_normed, raw, inverse_rms, gain_vec):
    unit_rows = raw * inverse_rms
    d_unit = d_normed * gain_vec
    return inverse_rms * (
        d_unit - unit_rows * jnp.mean(d_unit * unit_rows, axis=-1, keepdims=True)
    )


def heads_kernel(
    shard_ref, q_ref, g_ref, own_ref, near_k_ref, near_v_ref, far_ref, q_gain_ref, k_gain_ref,
    dq_ref, d_own_ref, d_near_k_ref, d_near_v_ref, d_far_ref, gains_ref,
    k_low, k_low_t, values, q_low, probs_all, d_scores_all,
):
    rows = own_ref.shape[2]
    group = q_ref.shape[1] // rows
    lanes = TILE * group
    blocks = rows // TILE
    tiles = WINDOW // TILE
    q_gain, k_gain = q_gain_ref[...], k_gain_ref[...]
    far_ok = jnp.where(shard_ref[0] >= 2, 1.0, 0.0)
    near_ok = jnp.where(shard_ref[0] >= 1, 1.0, 0.0)
    pairs = ((far_ref.at[0], far_ref.at[1]), (near_k_ref, near_v_ref), (own_ref.at[0], own_ref.at[1]))
    outs = (
        (d_far_ref.at[0], d_far_ref.at[1]),
        (d_near_k_ref, d_near_v_ref),
        (d_own_ref.at[0], d_own_ref.at[1]),
    )

    @pl.when(pl.program_id(0) == 0)
    def _():
        gains_ref[...] = jnp.zeros_like(gains_ref)

    for place, (key_ref, value_ref) in enumerate(pairs):
        raw = key_ref[0].astype(jnp.float32)
        here = slice(place * rows, (place + 1) * rows)
        k_low[here, :] = (raw * inverse_rms_of(raw) * k_gain).astype(jnp.bfloat16)
        values[here, :] = value_ref[0]
    k_low_t[...] = k_low[...].T
    raw_q = q_ref[0].astype(jnp.float32)
    q_low[...] = (raw_q * inverse_rms_of(raw_q) * q_gain).astype(jnp.bfloat16)

    key_ids = lax.broadcasted_iota(jnp.int32, (TILE, lanes), 0)
    token_ids = lax.broadcasted_iota(jnp.int32, (TILE, lanes), 1) // group
    late = key_ids <= token_ids
    edge_ok = jnp.where(late, 1.0, far_ok)
    q_gain_sum = jnp.zeros_like(q_gain)

    for block in range(blocks):
        span = slice(block * TILE, block * TILE + WINDOW + TILE)
        mine = slice(block * lanes, (block + 1) * lanes)
        scores = lax.dot_general(
            k_low[span, :], q_low[mine, :], NT, preferred_element_type=jnp.float32
        )
        scores = jnp.concatenate(
            [jnp.where(late, scores[WINDOW:], scores[:TILE]), scores[TILE:WINDOW]], axis=0
        )
        exp_scores = jnp.exp2(scores * exp2_scale)
        edge = exp_scores[:TILE] * edge_ok
        first_near = (blocks - block) * TILE
        first_own = first_near + rows
        total = jnp.sum(edge, axis=0, keepdims=True)
        for low, high, ok in (
            (TILE, first_near, far_ok),
            (first_near, min(first_own, WINDOW), near_ok),
            (first_own, WINDOW, None),
        ):
            if low < high:
                part = jnp.sum(exp_scores[low:high], axis=0, keepdims=True)
                total = total + (part if ok is None else part * ok)
        inverse = 1.0 / total
        probs = jnp.concatenate([edge, exp_scores[TILE:]], axis=0) * inverse
        d_probs = lax.dot_general(
            values[span, :], g_ref[0, mine, :], NT, preferred_element_type=jnp.float32
        )
        d_probs = jnp.concatenate(
            [jnp.where(late, d_probs[WINDOW:], d_probs[:TILE]), d_probs[TILE:WINDOW]], axis=0
        )
        offset = jnp.sum(probs * d_probs, axis=0, keepdims=True)
        d_scores = probs * (d_probs - offset)
        for whole, held in ((probs, probs_all), (d_scores, d_scores_all)):
            start = block * TILE
            held[start : start + TILE, mine] = jnp.where(late, 0.0, whole[:TILE]).astype(
                jnp.bfloat16
            )
            held[start + TILE : start + WINDOW, mine] = whole[TILE:].astype(jnp.bfloat16)
            held[start + WINDOW : start + WINDOW + TILE, mine] = jnp.where(
                late, whole[:TILE], 0.0
            ).astype(jnp.bfloat16)
        query_grad = score_scale * jnp.dot(
            k_low_t[:, span], d_scores_all[span, mine], preferred_element_type=jnp.float32
        ).T
        raw = q_ref[0, mine, :].astype(jnp.float32)
        inverse_rms = inverse_rms_of(raw)
        q_gain_sum = q_gain_sum + jnp.sum(query_grad * (raw * inverse_rms), axis=0, keepdims=True)
        dq_ref[0, mine, :] = norm_back(query_grad, raw, inverse_rms, q_gain).astype(dq_ref.dtype)

    pieces = [(tile, tile + 1, 0, tile + 1) for tile in range(blocks - 1)]
    pieces += [(blocks - 1, tiles + 1, 0, blocks)]
    pieces += [(tiles + block, tiles + block + 1, block, blocks) for block in range(1, blocks)]
    k_gain_sum = jnp.zeros_like(k_gain)
    for first, last, low, high in pieces:
        meets = slice(low * lanes, high * lanes)
        keys = slice(first * TILE, last * TILE)
        value_grad = jnp.dot(
            probs_all[keys, meets], g_ref[0, meets, :], preferred_element_type=jnp.float32
        )
        key_grad = score_scale * jnp.dot(
            d_scores_all[keys, meets], q_low[meets, :], preferred_element_type=jnp.float32
        )
        for place, (key_out, value_out) in enumerate(outs):
            start = max(first * TILE, place * rows)
            stop = min(last * TILE, (place + 1) * rows)
            if start >= stop:
                continue
            inside = slice(start - place * rows, stop - place * rows)
            here = slice(start - first * TILE, stop - first * TILE)
            raw = pairs[place][0][0, inside, :].astype(jnp.float32)
            k_gain_sum = k_gain_sum + jnp.sum(
                key_grad[here] * (raw * inverse_rms_of(raw)), axis=0, keepdims=True
            )
            key_out[0, inside, :] = key_grad[here].astype(key_out.dtype)
            value_out[0, inside, :] = value_grad[here].astype(value_out.dtype)
    gains_ref[0:1, :] += q_gain_sum
    gains_ref[1:2, :] += k_gain_sum


def closed(own, returned, swapped, keep, head):
    return [
        own[kind, head]
        + returned[kind, head].astype(jnp.float32)
        + keep * swapped[kind][head].astype(jnp.float32)
        for kind in range(2)
    ]


def close_kernel(shard_ref, own, returned, swapped_k, swapped_v, raw_ref, k_gain_ref, out):
    keep = jnp.where(shard_ref[0] % 2 == 1, 0.0, 1.0)
    key_grad, value_grad = closed(own, returned, (swapped_k, swapped_v), keep, 0)
    raw = raw_ref[0, 0].astype(jnp.float32)
    key_grad = norm_back(key_grad, raw, inverse_rms_of(raw), k_gain_ref[...])
    out[0, 0] = key_grad.astype(out.dtype)
    out[1, 0] = value_grad.astype(out.dtype)


def finish_kernel(low, shard_ref, own, returned, swapped_k, swapped_v, raw_ref, k_gain_ref, *rest):
    *done, key_out, value_out, by_token = rest
    keep = jnp.where(shard_ref[0] % 2 == 1, 0.0, 1.0)
    before = [(part, head) for part in done for head in range(part.shape[1])]
    for kind, out in ((0, key_out), (1, value_out)):
        for place, (part, head) in enumerate(before):
            by_token[:, place, :] = part[kind, head].astype(jnp.float32)
        for head in range(own.shape[1]):
            grad = closed(own, returned, (swapped_k, swapped_v), keep, head)[kind]
            if kind == 0:
                raw = raw_ref[0, low + head].astype(jnp.float32)
                grad = norm_back(grad, raw, inverse_rms_of(raw), k_gain_ref[...])
            by_token[:, len(before) + head, :] = grad
        out[...] = by_token[...].astype(out.dtype)


def choose_kernel(shard_ref, far_ref, own_ref, key_out, value_out):
    odd = shard_ref[0] % 2 == 1

    @pl.when(odd)
    def _():
        key_out[...], value_out[...] = far_ref[0], far_ref[1]

    @pl.when(jnp.logical_not(odd))
    def _():
        key_out[...], value_out[...] = own_ref[0], own_ref[1]


def relay_kernel(shard_ref, far_ref, swapped_k_ref, swapped_v_ref, out_ref):
    odd = jnp.where(shard_ref[0] % 2 == 1, 1.0, 0.0)
    for kind, swapped_ref in enumerate((swapped_k_ref, swapped_v_ref)):
        total = far_ref[kind].astype(jnp.float32) + odd * swapped_ref[...].astype(jnp.float32)
        out_ref[kind] = total.astype(out_ref.dtype)


def choose(shard, far, own):
    vmem = pl.BlockSpec(memory_space=pltpu.VMEM)
    return pl.pallas_call(
        choose_kernel,
        in_specs=[pl.BlockSpec(memory_space=pltpu.SMEM), vmem, vmem],
        out_specs=[vmem, vmem],
        out_shape=[jax.ShapeDtypeStruct(far.shape[1:], far.dtype)] * 2,
        cost_estimate=LIGHT,
    )(shard, far, own)


def relay(shard, d_far, swapped):
    vmem = pl.BlockSpec(memory_space=pltpu.VMEM)
    return pl.pallas_call(
        relay_kernel,
        in_specs=[pl.BlockSpec(memory_space=pltpu.SMEM), vmem, vmem, vmem],
        out_specs=vmem,
        out_shape=jax.ShapeDtypeStruct(d_far.shape, d_far.dtype),
        cost_estimate=LIGHT,
    )(shard, d_far, *swapped)


def group_grads(shard, first, here, count, queries, grads, own, near, far, q_gain, k_gain):
    _, _, rows, width = own.shape
    query_rows = queries.shape[1]
    span = WINDOW + rows
    whole_q = pl.BlockSpec((1, query_rows, width), lambda head: (first + head, 0, 0))
    part = pl.BlockSpec((2, 1, rows, width), lambda head: (0, head, 0, 0))
    half = pl.BlockSpec((1, rows, width), lambda head: (head, 0, 0))
    held = pl.BlockSpec((2, 1, rows, width), lambda head: (0, here + head, 0, 0))
    held_half = pl.BlockSpec((1, rows, width), lambda head: (here + head, 0, 0))
    gain = pl.BlockSpec((1, width), lambda head: (0, 0))
    shape = (2, count, rows, width)
    return pl.pallas_call(
        heads_kernel,
        grid=(count,),
        in_specs=[
            pl.BlockSpec(memory_space=pltpu.SMEM), whole_q, whole_q, held, held_half,
            held_half, held, gain, gain,
        ],
        out_specs=[
            pl.BlockSpec((1, query_rows, width), lambda head: (head, 0, 0)),
            part,
            half,
            half,
            part,
            pl.BlockSpec((2, width), lambda head: (0, 0)),
        ],
        out_shape=[
            jax.ShapeDtypeStruct((count, query_rows, width), jnp.bfloat16),
            jax.ShapeDtypeStruct(shape, jnp.float32),
            jax.ShapeDtypeStruct(shape[1:], jnp.bfloat16),
            jax.ShapeDtypeStruct(shape[1:], jnp.bfloat16),
            jax.ShapeDtypeStruct(shape, jnp.bfloat16),
            jax.ShapeDtypeStruct((2, width), jnp.float32),
        ],
        scratch_shapes=[
            pltpu.VMEM((span, width), jnp.bfloat16),
            pltpu.VMEM((width, span), jnp.bfloat16),
            pltpu.VMEM((span, width), jnp.bfloat16),
            pltpu.VMEM((query_rows, width), jnp.bfloat16),
            pltpu.VMEM((span, query_rows), jnp.bfloat16),
            pltpu.VMEM((span, query_rows), jnp.bfloat16),
        ],
        compiler_params=pltpu.CompilerParams(vmem_limit_bytes=24 * 1024 * 1024),
        cost_estimate=LIGHT,
    )(shard, queries, grads, own, *near, far, q_gain, k_gain)


def close_group(cost, shard, own, returned, swapped, raw, low, k_gain):
    _, count, rows, width = own.shape
    part = pl.BlockSpec((2, 1, rows, width), lambda head: (0, head, 0, 0))
    half = pl.BlockSpec((1, rows, width), lambda head: (head, 0, 0))
    return pl.pallas_call(
        close_kernel,
        grid=(count,),
        in_specs=[
            pl.BlockSpec(memory_space=pltpu.SMEM), part, part, half, half,
            pl.BlockSpec((2, 1, rows, width), lambda head: (0, low + head, 0, 0)),
            pl.BlockSpec((1, width), lambda head: (0, 0)),
        ],
        out_specs=part,
        out_shape=jax.ShapeDtypeStruct(own.shape, jnp.bfloat16),
        cost_estimate=cost,
    )(shard, own, returned, *swapped, raw, k_gain)


def finish(shard, own, returned, swapped, raw, low, k_gain, done):
    _, count, rows, width = own.shape
    kv_dev = count + sum(part.shape[1] for part in done)
    shape = (rows, kv_dev, width)
    vmem = pl.BlockSpec(memory_space=pltpu.VMEM)
    return pl.pallas_call(
        functools.partial(finish_kernel, low),
        in_specs=[pl.BlockSpec(memory_space=pltpu.SMEM)] + [vmem] * (6 + len(done)),
        out_specs=[vmem, vmem],
        out_shape=[jax.ShapeDtypeStruct(shape, jnp.bfloat16)] * 2,
        scratch_shapes=[pltpu.VMEM(shape, jnp.float32)],
        compiler_params=pltpu.CompilerParams(vmem_limit_bytes=40 * 1024 * 1024),
    )(shard, own, returned, *swapped, raw, k_gain, *done)


def group_sizes(kv_dev):
    count = min(GROUPS, kv_dev)
    return [(kv_dev + count - 1 - place) // count for place in range(count)]


def summed(value, axis):
    count = lax.axis_size(axis)
    if count & (count - 1):
        return lax.psum(value, axis)
    step = 1
    while step < count:
        pairs = [(source, source ^ step) for source in range(count)]
        value = value + lax.ppermute(value, axis, pairs)
        step *= 2
    return value


def per_device(query, key, value, grad_out, q_gain, k_gain):
    rows, heads, width = query.shape
    kv_dev = key.shape[1]
    group = heads // kv_dev
    count = lax.axis_size("seq")
    assert 2 * rows == WINDOW and rows % TILE == 0 and count % 2 == 0
    shard = lax.axis_index("seq")
    odd = shard % 2 == 1
    ahead = [(source, source + 2) for source in range(count - 2)]
    back = [(source + 2, source) for source in range(count - 2)]
    swap = [(source, source ^ 1) for source in range(count)]

    def by_head(array):
        split = array.reshape(rows, kv_dev, group, width)
        return jnp.transpose(split, (1, 0, 2, 3)).reshape(kv_dev, rows * group, width)

    sizes = group_sizes(kv_dev)
    starts = [sum(sizes[:place]) for place in range(len(sizes))]
    cuts = [(0, sizes[0])] + ([(sizes[0], kv_dev)] if len(sizes) > 1 else [])
    owns = [
        jnp.transpose(jnp.stack([key[:, low:high], value[:, low:high]]), (0, 2, 1, 3))
        for low, high in cuts
    ]
    fars = [lax.ppermute(own, "seq", ahead) for own in owns]
    queries, grads = by_head(query), by_head(grad_out)
    scalar = shard.astype(jnp.int32).reshape(1)
    q_gain_2d, k_gain_2d = q_gain.reshape(1, width), k_gain.reshape(1, width)

    dq_parts, gains, kept, done = [], [], [], []
    waiting = None
    for place, (first, size) in enumerate(zip(starts, sizes, strict=True)):
        if waiting is not None:
            d_own, d_near, d_far, before, low = waiting
            swapped = [lax.ppermute(half, "seq", swap) for half in d_near]
            relayed = relay(scalar, d_far, swapped)
        if place < 2:
            own, far, base = owns[place], fars[place], cuts[place][0]
            if place:
                far, relayed = lax.optimization_barrier((far, relayed))
            else:
                far, *_ = lax.optimization_barrier((far, *owns[1:]))
            near = [lax.ppermute(half, "seq", swap) for half in choose(scalar, far, own)]
        if waiting is not None:
            if kept:
                done.append(close_group(HEAVY, scalar, *kept.pop(), k_gain_2d))
                near, done = lax.optimization_barrier((near, done))
            kept.append((d_own, lax.ppermute(relayed, "seq", back), swapped, before, low))
        dq, d_own, *d_near, d_far, gain = group_grads(
            scalar, first, first - base, size, queries, grads, own, near, far, q_gain_2d, k_gain_2d
        )
        waiting = (d_own, d_near, d_far, own, first - base)
        dq_parts.append(dq)
        gains.append(gain)
    d_own, d_near, d_far, before, low = waiting
    swapped = [lax.ppermute(half, "seq", swap) for half in d_near]
    relayed = relay(scalar, d_far, swapped)
    if kept:
        returns = [parts[1] for parts in kept]
        relayed, returns = lax.optimization_barrier((relayed, returns))
        kept = [(own, ret, *rest) for (own, _, *rest), ret in zip(kept, returns, strict=True)]
    returned = lax.ppermute(relayed, "seq", back)
    done += [close_group(LIGHT, scalar, *parts, k_gain_2d) for parts in kept]
    grad_key, grad_value = finish(scalar, d_own, returned, swapped, before, low, k_gain_2d, done)
    gain_sum = sum(gains[1:], gains[0])
    gain_sum = summed(summed(gain_sum, "head"), "seq")
    grad_query = jnp.concatenate(dq_parts).reshape(kv_dev, rows, group, width)
    grad_query = jnp.transpose(grad_query, (1, 0, 2, 3)).reshape(rows, heads, width)
    return (grad_query, grad_key, grad_value, gain_sum[0], gain_sum[1])


def solution(mesh):
    split, whole = P("seq", "head", None), P()
    return jax.shard_map(
        per_device,
        mesh=mesh,
        in_specs=(split, split, split, split, whole, whole),
        out_specs=(split, split, split, whole, whole),
        check_vma=False,
    )
```

```python
import functools

import jax
import jax.numpy as jnp
from jax import lax
from jax.experimental import pallas as pl
from jax.experimental.pallas import tpu as pltpu
from jax.sharding import PartitionSpec as P

WINDOW = 1024
TILE = 128

score_scale = 168.0 ** (-0.5)
norm_eps = 1e-06
exp2_scale = score_scale * 1.4426950408889634

GROUPS = 3
HEAVY = pl.CostEstimate(flops=10**11, bytes_accessed=10**8, transcendentals=0)
LIGHT = pl.CostEstimate(flops=1000, bytes_accessed=1000, transcendentals=0)

NT = (((1,), (1,)), ((), ()))


def inverse_rms_of(as_float):
    return lax.rsqrt(jnp.mean(as_float * as_float, axis=-1, keepdims=True) + norm_eps)


def norm_back(d_normed, raw, inverse_rms, gain_vec):
    unit_rows = raw * inverse_rms
    d_unit = d_normed * gain_vec
    return inverse_rms * (
        d_unit - unit_rows * jnp.mean(d_unit * unit_rows, axis=-1, keepdims=True)
    )


def heads_kernel(
    shard_ref, q_ref, g_ref, own_ref, near_ref, far_ref, q_gain_ref, k_gain_ref,
    dq_ref, d_own_ref, d_near_ref, d_far_ref, gains_ref,
    k_low, k_low_t, values, q_low, probs_all, d_scores_all,
):
    rows = own_ref.shape[2]
    group = q_ref.shape[1] // rows
    lanes = TILE * group
    blocks = rows // TILE
    tiles = WINDOW // TILE
    q_gain, k_gain = q_gain_ref[...], k_gain_ref[...]
    far_ok = jnp.where(shard_ref[0] >= 2, 1.0, 0.0)
    near_ok = jnp.where(shard_ref[0] >= 1, 1.0, 0.0)
    key_refs = (far_ref, near_ref, own_ref)

    @pl.when(pl.program_id(0) == 0)
    def _():
        gains_ref[...] = jnp.zeros_like(gains_ref)

    for place, ref in enumerate(key_refs):
        raw = ref[0, 0].astype(jnp.float32)
        here = slice(place * rows, (place + 1) * rows)
        k_low[here, :] = (raw * inverse_rms_of(raw) * k_gain).astype(jnp.bfloat16)
        values[here, :] = ref[1, 0]
    k_low_t[...] = k_low[...].T
    raw_q = q_ref[0].astype(jnp.float32)
    q_low[...] = (raw_q * inverse_rms_of(raw_q) * q_gain).astype(jnp.bfloat16)

    key_ids = lax.broadcasted_iota(jnp.int32, (TILE, lanes), 0)
    token_ids = lax.broadcasted_iota(jnp.int32, (TILE, lanes), 1) // group
    late = key_ids <= token_ids
    edge_ok = jnp.where(late, 1.0, far_ok)
    q_gain_sum = jnp.zeros_like(q_gain)

    for block in range(blocks):
        span = slice(block * TILE, block * TILE + WINDOW + TILE)
        mine = slice(block * lanes, (block + 1) * lanes)
        scores = lax.dot_general(
            k_low[span, :], q_low[mine, :], NT, preferred_element_type=jnp.float32
        )
        scores = jnp.concatenate(
            [jnp.where(late, scores[WINDOW:], scores[:TILE]), scores[TILE:WINDOW]], axis=0
        )
        exp_scores = jnp.exp2(scores * exp2_scale)
        edge = exp_scores[:TILE] * edge_ok
        first_near = (blocks - block) * TILE
        first_own = first_near + rows
        total = jnp.sum(edge, axis=0, keepdims=True)
        for low, high, ok in (
            (TILE, first_near, far_ok),
            (first_near, min(first_own, WINDOW), near_ok),
            (first_own, WINDOW, None),
        ):
            if low < high:
                part = jnp.sum(exp_scores[low:high], axis=0, keepdims=True)
                total = total + (part if ok is None else part * ok)
        inverse = 1.0 / total
        probs = jnp.concatenate([edge, exp_scores[TILE:]], axis=0) * inverse
        d_probs = lax.dot_general(
            values[span, :], g_ref[0, mine, :], NT, preferred_element_type=jnp.float32
        )
        d_probs = jnp.concatenate(
            [jnp.where(late, d_probs[WINDOW:], d_probs[:TILE]), d_probs[TILE:WINDOW]], axis=0
        )
        offset = jnp.sum(probs * d_probs, axis=0, keepdims=True)
        d_scores = probs * (d_probs - offset)
        for whole, held in ((probs, probs_all), (d_scores, d_scores_all)):
            start = block * TILE
            held[start : start + TILE, mine] = jnp.where(late, 0.0, whole[:TILE]).astype(
                jnp.bfloat16
            )
            held[start + TILE : start + WINDOW, mine] = whole[TILE:].astype(jnp.bfloat16)
            held[start + WINDOW : start + WINDOW + TILE, mine] = jnp.where(
                late, whole[:TILE], 0.0
            ).astype(jnp.bfloat16)
        query_grad = score_scale * jnp.dot(
            k_low_t[:, span], d_scores_all[span, mine], preferred_element_type=jnp.float32
        ).T
        raw = q_ref[0, mine, :].astype(jnp.float32)
        inverse_rms = inverse_rms_of(raw)
        q_gain_sum = q_gain_sum + jnp.sum(query_grad * (raw * inverse_rms), axis=0, keepdims=True)
        dq_ref[0, mine, :] = norm_back(query_grad, raw, inverse_rms, q_gain).astype(dq_ref.dtype)

    pieces = [(tile, tile + 1, 0, tile + 1) for tile in range(blocks - 1)]
    pieces += [(blocks - 1, tiles + 1, 0, blocks)]
    pieces += [(tiles + block, tiles + block + 1, block, blocks) for block in range(1, blocks)]
    k_gain_sum = jnp.zeros_like(k_gain)
    for first, last, low, high in pieces:
        meets = slice(low * lanes, high * lanes)
        keys = slice(first * TILE, last * TILE)
        value_grad = jnp.dot(
            probs_all[keys, meets], g_ref[0, meets, :], preferred_element_type=jnp.float32
        )
        key_grad = score_scale * jnp.dot(
            d_scores_all[keys, meets], q_low[meets, :], preferred_element_type=jnp.float32
        )
        for place, (ref, out) in enumerate(
            zip(key_refs, (d_far_ref, d_near_ref, d_own_ref), strict=True)
        ):
            start = max(first * TILE, place * rows)
            stop = min(last * TILE, (place + 1) * rows)
            if start >= stop:
                continue
            inside = slice(start - place * rows, stop - place * rows)
            here = slice(start - first * TILE, stop - first * TILE)
            raw = ref[0, 0, inside, :].astype(jnp.float32)
            k_gain_sum = k_gain_sum + jnp.sum(
                key_grad[here] * (raw * inverse_rms_of(raw)), axis=0, keepdims=True
            )
            out[0, 0, inside, :] = key_grad[here].astype(out.dtype)
            out[1, 0, inside, :] = value_grad[here].astype(out.dtype)
    gains_ref[0:1, :] += q_gain_sum
    gains_ref[1:2, :] += k_gain_sum


def close_kernel(base, returned, raw_ref, k_gain_ref, out):
    for head in range(base.shape[1]):
        grad = base[0, head].astype(jnp.float32) + returned[0, head].astype(jnp.float32)
        raw = raw_ref[0, head].astype(jnp.float32)
        grad = norm_back(grad, raw, inverse_rms_of(raw), k_gain_ref[...])
        out[0, head] = grad.astype(out.dtype)
        grad = base[1, head].astype(jnp.float32) + returned[1, head].astype(jnp.float32)
        out[1, head] = grad.astype(out.dtype)


def finish_kernel(base, returned, raw_ref, k_gain_ref, *rest):
    *done, key_out, value_out, by_token = rest
    before = [(part, head) for part in done for head in range(part.shape[1])]
    for kind, out in ((0, key_out), (1, value_out)):
        for place, (part, head) in enumerate(before):
            by_token[:, place, :] = part[kind, head].astype(jnp.float32)
        for head in range(base.shape[1]):
            grad = base[kind, head].astype(jnp.float32) + returned[kind, head].astype(jnp.float32)
            if kind == 0:
                raw = raw_ref[0, head].astype(jnp.float32)
                grad = norm_back(grad, raw, inverse_rms_of(raw), k_gain_ref[...])
            by_token[:, len(before) + head, :] = grad
        out[...] = by_token[...].astype(out.dtype)


def later_kernel(*refs):
    pass


def later(array):
    anywhere = pl.BlockSpec(memory_space=pl.ANY)
    return pl.pallas_call(
        later_kernel,
        in_specs=[anywhere],
        out_specs=anywhere,
        out_shape=jax.ShapeDtypeStruct(array.shape, array.dtype),
        input_output_aliases={0: 0},
        cost_estimate=HEAVY,
    )(array)


def group_grads(shard, first, here, count, queries, grads, own, near, far, q_gain, k_gain):
    _, _, rows, width = own.shape
    query_rows = queries.shape[1]
    span = WINDOW + rows
    whole_q = pl.BlockSpec((1, query_rows, width), lambda head: (first + head, 0, 0))
    part = pl.BlockSpec((2, 1, rows, width), lambda head: (0, head, 0, 0))
    held = pl.BlockSpec((2, 1, rows, width), lambda head: (0, here + head, 0, 0))
    gain = pl.BlockSpec((1, width), lambda head: (0, 0))
    shape = (2, count, rows, width)
    return pl.pallas_call(
        heads_kernel,
        grid=(count,),
        in_specs=[
            pl.BlockSpec(memory_space=pltpu.SMEM), whole_q, whole_q, held, held, held, gain, gain,
        ],
        out_specs=[
            pl.BlockSpec((1, query_rows, width), lambda head: (head, 0, 0)),
            part,
            part,
            part,
            pl.BlockSpec((2, width), lambda head: (0, 0)),
        ],
        out_shape=[
            jax.ShapeDtypeStruct((count, query_rows, width), jnp.bfloat16),
            jax.ShapeDtypeStruct(shape, jnp.bfloat16),
            jax.ShapeDtypeStruct(shape, jnp.bfloat16),
            jax.ShapeDtypeStruct(shape, jnp.bfloat16),
            jax.ShapeDtypeStruct((2, width), jnp.float32),
        ],
        scratch_shapes=[
            pltpu.VMEM((span, width), jnp.bfloat16),
            pltpu.VMEM((width, span), jnp.bfloat16),
            pltpu.VMEM((span, width), jnp.bfloat16),
            pltpu.VMEM((query_rows, width), jnp.bfloat16),
            pltpu.VMEM((span, query_rows), jnp.bfloat16),
            pltpu.VMEM((span, query_rows), jnp.bfloat16),
        ],
        compiler_params=pltpu.CompilerParams(vmem_limit_bytes=60 * 1024 * 1024),
        cost_estimate=LIGHT,
    )(shard, queries, grads, own, near, far, q_gain, k_gain)


def close_group(base, returned, raw, k_gain):
    vmem = pl.BlockSpec(memory_space=pltpu.VMEM)
    return pl.pallas_call(
        close_kernel,
        in_specs=[vmem] * 4,
        out_specs=vmem,
        out_shape=jax.ShapeDtypeStruct(base.shape, jnp.bfloat16),
        cost_estimate=LIGHT,
    )(base, returned, raw, k_gain)


def finish(base, returned, raw, k_gain, done):
    _, count, rows, width = base.shape
    kv_dev = count + sum(part.shape[1] for part in done)
    shape = (rows, kv_dev, width)
    vmem = pl.BlockSpec(memory_space=pltpu.VMEM)
    return pl.pallas_call(
        finish_kernel,
        in_specs=[vmem] * (4 + len(done)),
        out_specs=[vmem, vmem],
        out_shape=[jax.ShapeDtypeStruct(shape, jnp.bfloat16)] * 2,
        scratch_shapes=[pltpu.VMEM(shape, jnp.float32)],
        compiler_params=pltpu.CompilerParams(vmem_limit_bytes=40 * 1024 * 1024),
    )(base, returned, raw, k_gain, *done)


def group_sizes(kv_dev):
    count = min(GROUPS, kv_dev)
    return [(kv_dev + count - 1 - place) // count for place in range(count)]


def summed(value, axis, step, stop=None):
    count = lax.axis_size(axis)
    assert count & (count - 1) == 0
    while step < (stop or count):
        pairs = [(source, source ^ step) for source in range(count)]
        value = value + lax.ppermute(value, axis, pairs)
        step *= 2
    return value


def per_device(query, key, value, grad_out, q_gain, k_gain):
    rows, heads, width = query.shape
    kv_dev = key.shape[1]
    group = heads // kv_dev
    count = lax.axis_size("seq")
    assert 2 * rows == WINDOW and rows % TILE == 0 and count % 2 == 0
    shard = lax.axis_index("seq")
    odd = shard % 2 == 1
    ahead = [(source, source + 2) for source in range(count - 2)]
    back = [(source + 2, source) for source in range(count - 2)]
    swap = [(source, source ^ 1) for source in range(count)]

    def by_head(array):
        split = array.reshape(rows, kv_dev, group, width)
        return jnp.transpose(split, (1, 0, 2, 3)).reshape(kv_dev, rows * group, width)

    sizes = group_sizes(kv_dev)
    starts = [sum(sizes[:place]) for place in range(len(sizes))]
    cuts = [(0, sizes[0])] + ([(sizes[0], kv_dev)] if len(sizes) > 1 else [])
    owns = [
        jnp.transpose(jnp.stack([key[:, low:high], value[:, low:high]]), (0, 2, 1, 3))
        for low, high in cuts
    ]
    fars = [lax.ppermute(own, "seq", ahead) for own in owns]
    queries, grads = by_head(query), by_head(grad_out)
    scalar = shard.astype(jnp.int32).reshape(1)
    q_gain_2d, k_gain_2d = q_gain.reshape(1, width), k_gain.reshape(1, width)

    def split(d_own, d_near, d_far, raw):
        swapped = lax.ppermute(d_near, "seq", swap).astype(jnp.float32)
        relayed = d_far.astype(jnp.float32) + jnp.where(odd, swapped, 0.0)
        base = d_own.astype(jnp.float32) + jnp.where(odd, 0.0, swapped)
        return relayed.astype(jnp.bfloat16), base.astype(jnp.bfloat16), raw

    dq_parts, gains, kept, done = [], [], [], []
    grads_out = None
    for place, (first, size) in enumerate(zip(starts, sizes, strict=True)):
        if grads_out is not None:
            relayed, base, raw = split(*grads_out)
        if place < 2:
            own, far, start = owns[place], fars[place], cuts[place][0]
            if place:
                far, relayed = lax.optimization_barrier((later(far), relayed))
            else:
                far, *_ = lax.optimization_barrier((far, *owns[1:]))
            near = lax.ppermute(jnp.where(odd, far, own), "seq", swap)
        if grads_out is not None:
            if kept:
                before, returned, key_before = kept.pop()
                near, returned, relayed = lax.optimization_barrier((near, later(returned), relayed))
                done.append(close_group(before, returned, key_before, k_gain_2d))
            kept.append((base, lax.ppermute(relayed, "seq", back), raw))
        here = slice(first - start, first - start + size)
        dq, *grads_out, gain = group_grads(
            scalar, first, first - start, size, queries, grads, own, near, far, q_gain_2d, k_gain_2d
        )
        grads_out.append(own[:1, here])
        dq_parts.append(dq)
        gains.append(gain)
    relayed, base, raw = split(*grads_out)
    gain_sum = summed(sum(gains[1:], gains[0]), "seq", 2)
    if kept:
        before, returned, key_before = kept.pop()
        relayed, returned, gain_sum = lax.optimization_barrier(
            (relayed, later(returned), gain_sum)
        )
        done.append(close_group(before, returned, key_before, k_gain_2d))
    returned = lax.ppermute(relayed, "seq", back)
    gain_sum = summed(gain_sum, "seq", 1, 2)
    gain_sum = summed(gain_sum, "head", 1)
    grad_key, grad_value = finish(base, returned, raw, k_gain_2d, done)
    grad_query = jnp.concatenate(dq_parts).reshape(kv_dev, rows, group, width)
    grad_query = jnp.transpose(grad_query, (1, 0, 2, 3)).reshape(rows, heads, width)
    return (grad_query, grad_key, grad_value, gain_sum[0], gain_sum[1])


def solution(mesh):
    split, whole = P("seq", "head", None), P()
    return jax.shard_map(
        per_device,
        mesh=mesh,
        in_specs=(split, split, split, split, whole, whole),
        out_specs=(split, split, split, whole, whole),
        check_vma=False,
    )
```

```python
import functools

import jax
import jax.numpy as jnp
from jax import lax
from jax.experimental import pallas as pl
from jax.experimental.pallas import tpu as pltpu
from jax.sharding import PartitionSpec as P

WINDOW = 1024
TILE = 128

score_scale = 168.0 ** (-0.5)
norm_eps = 1e-06
exp2_scale = score_scale * 1.4426950408889634

GROUPS = 3
HEAVY = pl.CostEstimate(flops=10**11, bytes_accessed=10**8, transcendentals=0)
LIGHT = pl.CostEstimate(flops=1000, bytes_accessed=1000, transcendentals=0)

NT = (((1,), (1,)), ((), ()))


def inverse_rms_of(as_float):
    return lax.rsqrt(jnp.mean(as_float * as_float, axis=-1, keepdims=True) + norm_eps)


def norm_back(d_normed, raw, inverse_rms, gain_vec):
    unit_rows = raw * inverse_rms
    d_unit = d_normed * gain_vec
    return inverse_rms * (
        d_unit - unit_rows * jnp.mean(d_unit * unit_rows, axis=-1, keepdims=True)
    )


def heads_kernel(
    shard_ref, q_ref, g_ref, own_ref, near_ref, far_ref, q_gain_ref, k_gain_ref,
    dq_ref, d_own_ref, d_near_ref, d_far_ref, gains_ref,
    k_low, k_low_t, values, q_low, probs_all, d_scores_all,
):
    rows = own_ref.shape[2]
    group = q_ref.shape[1] // rows
    lanes = TILE * group
    blocks = rows // TILE
    tiles = WINDOW // TILE
    q_gain, k_gain = q_gain_ref[...], k_gain_ref[...]
    far_ok = jnp.where(shard_ref[0] >= 2, 1.0, 0.0)
    near_ok = jnp.where(shard_ref[0] >= 1, 1.0, 0.0)
    key_refs = (far_ref, near_ref, own_ref)

    @pl.when(pl.program_id(0) == 0)
    def _():
        gains_ref[...] = jnp.zeros_like(gains_ref)

    for place, ref in enumerate(key_refs):
        raw = ref[0, 0].astype(jnp.float32)
        here = slice(place * rows, (place + 1) * rows)
        k_low[here, :] = (raw * inverse_rms_of(raw) * k_gain).astype(jnp.bfloat16)
        values[here, :] = ref[1, 0]
    k_low_t[...] = k_low[...].T
    raw_q = q_ref[0].astype(jnp.float32)
    q_low[...] = (raw_q * inverse_rms_of(raw_q) * q_gain).astype(jnp.bfloat16)

    key_ids = lax.broadcasted_iota(jnp.int32, (TILE, lanes), 0)
    token_ids = lax.broadcasted_iota(jnp.int32, (TILE, lanes), 1) // group
    late = key_ids <= token_ids
    edge_ok = jnp.where(late, 1.0, far_ok)
    q_gain_sum = jnp.zeros_like(q_gain)

    for block in range(blocks):
        span = slice(block * TILE, block * TILE + WINDOW + TILE)
        mine = slice(block * lanes, (block + 1) * lanes)
        scores = lax.dot_general(
            k_low[span, :], q_low[mine, :], NT, preferred_element_type=jnp.float32
        )
        scores = jnp.concatenate(
            [jnp.where(late, scores[WINDOW:], scores[:TILE]), scores[TILE:WINDOW]], axis=0
        )
        exp_scores = jnp.exp2(scores * exp2_scale)
        edge = exp_scores[:TILE] * edge_ok
        first_near = (blocks - block) * TILE
        first_own = first_near + rows
        total = jnp.sum(edge, axis=0, keepdims=True)
        for low, high, ok in (
            (TILE, first_near, far_ok),
            (first_near, min(first_own, WINDOW), near_ok),
            (first_own, WINDOW, None),
        ):
            if low < high:
                part = jnp.sum(exp_scores[low:high], axis=0, keepdims=True)
                total = total + (part if ok is None else part * ok)
        inverse = 1.0 / total
        probs = jnp.concatenate([edge, exp_scores[TILE:]], axis=0) * inverse
        d_probs = lax.dot_general(
            values[span, :], g_ref[0, mine, :], NT, preferred_element_type=jnp.float32
        )
        d_probs = jnp.concatenate(
            [jnp.where(late, d_probs[WINDOW:], d_probs[:TILE]), d_probs[TILE:WINDOW]], axis=0
        )
        offset = jnp.sum(probs * d_probs, axis=0, keepdims=True)
        d_scores = probs * (d_probs - offset)
        for whole, held in ((probs, probs_all), (d_scores, d_scores_all)):
            start = block * TILE
            held[start : start + TILE, mine] = jnp.where(late, 0.0, whole[:TILE]).astype(
                jnp.bfloat16
            )
            held[start + TILE : start + WINDOW, mine] = whole[TILE:].astype(jnp.bfloat16)
            held[start + WINDOW : start + WINDOW + TILE, mine] = jnp.where(
                late, whole[:TILE], 0.0
            ).astype(jnp.bfloat16)
        query_grad = score_scale * jnp.dot(
            k_low_t[:, span], d_scores_all[span, mine], preferred_element_type=jnp.float32
        ).T
        raw = q_ref[0, mine, :].astype(jnp.float32)
        inverse_rms = inverse_rms_of(raw)
        q_gain_sum = q_gain_sum + jnp.sum(query_grad * (raw * inverse_rms), axis=0, keepdims=True)
        dq_ref[0, mine, :] = norm_back(query_grad, raw, inverse_rms, q_gain).astype(dq_ref.dtype)

    pieces = [(tile, tile + 1, 0, tile + 1) for tile in range(blocks - 1)]
    pieces += [(blocks - 1, tiles + 1, 0, blocks)]
    pieces += [(tiles + block, tiles + block + 1, block, blocks) for block in range(1, blocks)]
    k_gain_sum = jnp.zeros_like(k_gain)
    for first, last, low, high in pieces:
        meets = slice(low * lanes, high * lanes)
        keys = slice(first * TILE, last * TILE)
        value_grad = jnp.dot(
            probs_all[keys, meets], g_ref[0, meets, :], preferred_element_type=jnp.float32
        )
        key_grad = score_scale * jnp.dot(
            d_scores_all[keys, meets], q_low[meets, :], preferred_element_type=jnp.float32
        )
        for place, (ref, out) in enumerate(
            zip(key_refs, (d_far_ref, d_near_ref, d_own_ref), strict=True)
        ):
            start = max(first * TILE, place * rows)
            stop = min(last * TILE, (place + 1) * rows)
            if start >= stop:
                continue
            inside = slice(start - place * rows, stop - place * rows)
            here = slice(start - first * TILE, stop - first * TILE)
            raw = ref[0, 0, inside, :].astype(jnp.float32)
            k_gain_sum = k_gain_sum + jnp.sum(
                key_grad[here] * (raw * inverse_rms_of(raw)), axis=0, keepdims=True
            )
            out[0, 0, inside, :] = key_grad[here].astype(out.dtype)
            out[1, 0, inside, :] = value_grad[here].astype(out.dtype)
    gains_ref[0:1, :] += q_gain_sum
    gains_ref[1:2, :] += k_gain_sum


def closed(shard_ref, own, returned, swapped, kind, head):
    keep = jnp.where(shard_ref[0] % 2 == 1, 0.0, 1.0)
    own, returned, swapped = (
        part[kind, head].astype(jnp.float32) for part in (own, returned, swapped)
    )
    return own + returned + keep * swapped


def close_kernel(shard_ref, own, returned, swapped, raw_ref, k_gain_ref, out):
    for head in range(own.shape[1]):
        grad = closed(shard_ref, own, returned, swapped, 0, head)
        raw = raw_ref[0, head].astype(jnp.float32)
        grad = norm_back(grad, raw, inverse_rms_of(raw), k_gain_ref[...])
        out[0, head] = grad.astype(out.dtype)
        out[1, head] = closed(shard_ref, own, returned, swapped, 1, head).astype(out.dtype)


def finish_kernel(shard_ref, own, returned, swapped, raw_ref, k_gain_ref, *rest):
    *done, key_out, value_out, by_token = rest
    before = [(part, head) for part in done for head in range(part.shape[1])]
    for kind, out in ((0, key_out), (1, value_out)):
        for place, (part, head) in enumerate(before):
            by_token[:, place, :] = part[kind, head].astype(jnp.float32)
        for head in range(own.shape[1]):
            grad = closed(shard_ref, own, returned, swapped, kind, head)
            if kind == 0:
                raw = raw_ref[0, head].astype(jnp.float32)
                grad = norm_back(grad, raw, inverse_rms_of(raw), k_gain_ref[...])
            by_token[:, len(before) + head, :] = grad
        out[...] = by_token[...].astype(out.dtype)


def later_kernel(*refs):
    pass


def later(array):
    anywhere = pl.BlockSpec(memory_space=pl.ANY)
    return pl.pallas_call(
        later_kernel,
        in_specs=[anywhere],
        out_specs=anywhere,
        out_shape=jax.ShapeDtypeStruct(array.shape, array.dtype),
        input_output_aliases={0: 0},
        cost_estimate=HEAVY,
    )(array)


def group_grads(shard, first, here, count, queries, grads, own, near, far, q_gain, k_gain):
    _, _, rows, width = own.shape
    query_rows = queries.shape[1]
    span = WINDOW + rows
    whole_q = pl.BlockSpec((1, query_rows, width), lambda head: (first + head, 0, 0))
    part = pl.BlockSpec((2, 1, rows, width), lambda head: (0, head, 0, 0))
    held = pl.BlockSpec((2, 1, rows, width), lambda head: (0, here + head, 0, 0))
    gain = pl.BlockSpec((1, width), lambda head: (0, 0))
    shape = (2, count, rows, width)
    return pl.pallas_call(
        heads_kernel,
        grid=(count,),
        in_specs=[
            pl.BlockSpec(memory_space=pltpu.SMEM), whole_q, whole_q, held, held, held, gain, gain,
        ],
        out_specs=[
            pl.BlockSpec((1, query_rows, width), lambda head: (head, 0, 0)),
            part,
            part,
            part,
            pl.BlockSpec((2, width), lambda head: (0, 0)),
        ],
        out_shape=[
            jax.ShapeDtypeStruct((count, query_rows, width), jnp.bfloat16),
            jax.ShapeDtypeStruct(shape, jnp.bfloat16),
            jax.ShapeDtypeStruct(shape, jnp.bfloat16),
            jax.ShapeDtypeStruct(shape, jnp.bfloat16),
            jax.ShapeDtypeStruct((2, width), jnp.float32),
        ],
        scratch_shapes=[
            pltpu.VMEM((span, width), jnp.bfloat16),
            pltpu.VMEM((width, span), jnp.bfloat16),
            pltpu.VMEM((span, width), jnp.bfloat16),
            pltpu.VMEM((query_rows, width), jnp.bfloat16),
            pltpu.VMEM((span, query_rows), jnp.bfloat16),
            pltpu.VMEM((span, query_rows), jnp.bfloat16),
        ],
        compiler_params=pltpu.CompilerParams(vmem_limit_bytes=60 * 1024 * 1024),
        cost_estimate=LIGHT,
    )(shard, queries, grads, own, near, far, q_gain, k_gain)


def close_group(shard, own, returned, swapped, raw, k_gain):
    smem, vmem = (pl.BlockSpec(memory_space=space) for space in (pltpu.SMEM, pltpu.VMEM))
    return pl.pallas_call(
        close_kernel,
        in_specs=[smem] + [vmem] * 5,
        out_specs=vmem,
        out_shape=jax.ShapeDtypeStruct(own.shape, jnp.bfloat16),
        cost_estimate=LIGHT,
    )(shard, own, returned, swapped, raw, k_gain)


def finish(shard, own, returned, swapped, raw, k_gain, done):
    _, count, rows, width = own.shape
    kv_dev = count + sum(part.shape[1] for part in done)
    shape = (rows, kv_dev, width)
    smem, vmem = (pl.BlockSpec(memory_space=space) for space in (pltpu.SMEM, pltpu.VMEM))
    return pl.pallas_call(
        finish_kernel,
        in_specs=[smem] + [vmem] * (5 + len(done)),
        out_specs=[vmem, vmem],
        out_shape=[jax.ShapeDtypeStruct(shape, jnp.bfloat16)] * 2,
        scratch_shapes=[pltpu.VMEM(shape, jnp.float32)],
        compiler_params=pltpu.CompilerParams(vmem_limit_bytes=40 * 1024 * 1024),
    )(shard, own, returned, swapped, raw, k_gain, *done)


def group_sizes(kv_dev):
    count = min(GROUPS, kv_dev)
    return [(kv_dev + count - 1 - place) // count for place in range(count)]


def summed(value, axis, step, stop=None):
    count = lax.axis_size(axis)
    assert count & (count - 1) == 0
    while step < (stop or count):
        pairs = [(source, source ^ step) for source in range(count)]
        value = value + lax.ppermute(value, axis, pairs)
        step *= 2
    return value


def per_device(query, key, value, grad_out, q_gain, k_gain):
    rows, heads, width = query.shape
    kv_dev = key.shape[1]
    group = heads // kv_dev
    count = lax.axis_size("seq")
    assert 2 * rows == WINDOW and rows % TILE == 0 and count % 2 == 0
    shard = lax.axis_index("seq")
    odd = shard % 2 == 1
    ahead = [(source, source + 2) for source in range(count - 2)]
    back = [(source + 2, source) for source in range(count - 2)]
    swap = [(source, source ^ 1) for source in range(count)]

    def by_head(array):
        split = array.reshape(rows, kv_dev, group, width)
        return jnp.transpose(split, (1, 0, 2, 3)).reshape(kv_dev, rows * group, width)

    sizes = group_sizes(kv_dev)
    starts = [sum(sizes[:place]) for place in range(len(sizes))]
    cuts = [(0, sizes[0])] + ([(sizes[0], kv_dev)] if len(sizes) > 1 else [])
    by_kind = lax.optimization_barrier([jnp.transpose(kind, (1, 0, 2)) for kind in (key, value)])
    owns = [jnp.stack([kind[low:high] for kind in by_kind]) for low, high in cuts]
    fars = [lax.ppermute(own, "seq", ahead) for own in owns]
    queries, grads = by_head(query), by_head(grad_out)
    scalar = shard.astype(jnp.int32).reshape(1)
    q_gain_2d, k_gain_2d = q_gain.reshape(1, width), k_gain.reshape(1, width)

    def split(d_own, d_near, d_far, raw):
        swapped = lax.ppermute(d_near, "seq", swap)
        from_pair = jnp.where(odd, swapped.astype(jnp.float32), 0.0)
        relayed = (d_far.astype(jnp.float32) + from_pair).astype(jnp.bfloat16)
        return relayed, (d_own, swapped, raw)

    def close(stays, returned):
        d_own, swapped, raw = stays
        return close_group(scalar, d_own, returned, swapped, raw, k_gain_2d)

    dq_parts, gains, kept, done = [], [], [], []
    grads_out = None
    for place, (first, size) in enumerate(zip(starts, sizes, strict=True)):
        if grads_out is not None:
            relayed, stays = split(*grads_out)
        if place < 2:
            own, far, start = owns[place], fars[place], cuts[place][0]
            if place:
                far, relayed = lax.optimization_barrier((later(far), relayed))
            else:
                far, queries, grads, *_ = lax.optimization_barrier(
                    (far, queries, grads, *owns[1:])
                )
            near = lax.ppermute(jnp.where(odd, far, own), "seq", swap)
        if grads_out is not None:
            if kept:
                before, returned = kept.pop()
                near, returned, relayed = lax.optimization_barrier((near, later(returned), relayed))
                done.append(close(before, returned))
            kept.append((stays, lax.ppermute(relayed, "seq", back)))
        here = slice(first - start, first - start + size)
        dq, *grads_out, gain = group_grads(
            scalar, first, first - start, size, queries, grads, own, near, far, q_gain_2d, k_gain_2d
        )
        grads_out.append(own[:1, here])
        dq_parts.append(dq)
        gains.append(gain)
    relayed, stays = split(*grads_out)
    gain_sum = sum(gains[1:], gains[0])
    if kept:
        before, returned = kept.pop()
        returned, gain_sum = lax.optimization_barrier((later(returned), gain_sum))
        done.append(close(before, returned))
    gain_sum = summed(gain_sum, "seq", 2)
    relayed, gain_sum = lax.optimization_barrier((relayed, gain_sum))
    returned = lax.ppermute(relayed, "seq", back)
    gain_sum = summed(gain_sum, "seq", 1, 2)
    gain_sum = summed(gain_sum, "head", 1)
    d_own, swapped, raw = stays
    grad_key, grad_value = finish(scalar, d_own, returned, swapped, raw, k_gain_2d, done)
    grad_query = jnp.concatenate(dq_parts).reshape(kv_dev, rows, group, width)
    grad_query = jnp.transpose(grad_query, (1, 0, 2, 3)).reshape(rows, heads, width)
    return (grad_query, grad_key, grad_value, gain_sum[0], gain_sum[1])


def solution(mesh):
    split, whole = P("seq", "head", None), P()
    return jax.shard_map(
        per_device,
        mesh=mesh,
        in_specs=(split, split, split, split, whole, whole),
        out_specs=(split, split, split, whole, whole),
        check_vma=False,
    )
```

```python
import functools

import jax
import jax.numpy as jnp
from jax import lax
from jax.experimental import pallas as pl
from jax.experimental.pallas import tpu as pltpu
from jax.sharding import PartitionSpec as P

WINDOW = 1024
TILE = 128

score_scale = 168.0 ** (-0.5)
norm_eps = 1e-06
exp2_scale = score_scale * 1.4426950408889634

GROUPS = 3
HEAVY = pl.CostEstimate(flops=10**11, bytes_accessed=10**8, transcendentals=0)
LIGHT = pl.CostEstimate(flops=1000, bytes_accessed=1000, transcendentals=0)

NT = (((1,), (1,)), ((), ()))


def inverse_rms_of(as_float):
    return lax.rsqrt(jnp.mean(as_float * as_float, axis=-1, keepdims=True) + norm_eps)


def norm_back(d_normed, raw, inverse_rms, gain_vec):
    unit_rows = raw * inverse_rms
    d_unit = d_normed * gain_vec
    return inverse_rms * (
        d_unit - unit_rows * jnp.mean(d_unit * unit_rows, axis=-1, keepdims=True)
    )


def heads_kernel(
    shard_ref, q_ref, g_ref, own_ref, near_ref, far_ref, q_gain_ref, k_gain_ref,
    dq_ref, d_own_ref, d_near_ref, d_far_ref, gains_ref,
    k_low, k_low_t, k_rms, values, values_t, q_low, q_rms, g_low, exps, d_scores,
):
    rows = own_ref.shape[2]
    group = q_ref.shape[1] // rows
    lanes = TILE * group
    blocks = rows // TILE
    tiles = WINDOW // TILE
    q_gain, k_gain = q_gain_ref[...], k_gain_ref[...]
    far_ok = jnp.where(shard_ref[0] >= 2, 1.0, 0.0)
    near_ok = jnp.where(shard_ref[0] >= 1, 1.0, 0.0)
    key_refs = (far_ref, near_ref, own_ref)

    @pl.when(pl.program_id(0) == 0)
    def _():
        gains_ref[...] = jnp.zeros_like(gains_ref)

    for place, ref in enumerate(key_refs):
        raw = ref[0, 0].astype(jnp.float32)
        here = slice(place * rows, (place + 1) * rows)
        inverse_rms = jnp.broadcast_to(inverse_rms_of(raw), raw.shape)
        k_rms[here, :] = inverse_rms
        k_low[here, :] = (raw * inverse_rms * k_gain).astype(jnp.bfloat16)
        values[here, :] = ref[1, 0]
    k_low_t[...] = k_low[...].T
    values_t[...] = values[...].T
    raw_q = q_ref[0].astype(jnp.float32)
    inverse_rms = jnp.broadcast_to(inverse_rms_of(raw_q), raw_q.shape)
    q_rms[...] = inverse_rms
    q_low[...] = (raw_q * inverse_rms * q_gain).astype(jnp.bfloat16)

    key_ids = lax.broadcasted_iota(jnp.int32, (TILE, lanes), 0)
    token_ids = lax.broadcasted_iota(jnp.int32, (TILE, lanes), 1) // group
    late = key_ids <= token_ids
    edge_ok = jnp.where(late, 1.0, far_ok)
    q_gain_sum = jnp.zeros_like(q_gain)

    for block in range(blocks):
        start = block * TILE
        span = slice(start, start + WINDOW + TILE)
        mine = slice(block * lanes, (block + 1) * lanes)
        scores = lax.dot_general(
            k_low[span, :], q_low[mine, :], NT, preferred_element_type=jnp.float32
        )
        edge = jnp.where(late, scores[WINDOW:], scores[:TILE])
        edge = jnp.exp2(edge * exp2_scale) * edge_ok
        middle = jnp.exp2(scores[TILE:WINDOW] * exp2_scale)
        exps[start : start + TILE, mine] = jnp.where(late, 0.0, edge).astype(jnp.bfloat16)
        exps[start + TILE : start + WINDOW, mine] = middle.astype(jnp.bfloat16)
        exps[start + WINDOW : start + WINDOW + TILE, mine] = jnp.where(late, edge, 0.0).astype(
            jnp.bfloat16
        )
        first_near = (blocks - block) * TILE
        first_own = first_near + rows
        total = jnp.sum(edge, axis=0, keepdims=True)
        for low, high, ok in (
            (TILE, first_near, far_ok),
            (first_near, min(first_own, WINDOW), near_ok),
            (first_own, WINDOW, None),
        ):
            if low < high:
                part = jnp.sum(middle[low - TILE : high - TILE], axis=0, keepdims=True)
                total = total + (part if ok is None else part * ok)
        inverse = 1.0 / total
        scaled_t = (g_ref[0, mine, :].astype(jnp.float32).T * inverse).astype(jnp.bfloat16)
        g_low[mine, :] = scaled_t.T
        attended_t = jnp.dot(values_t[:, span], exps[span, mine], preferred_element_type=jnp.float32)
        offset = inverse * jnp.sum(
            scaled_t.astype(jnp.float32) * attended_t, axis=0, keepdims=True
        )
        d_probs = jnp.dot(values[span, :], scaled_t, preferred_element_type=jnp.float32)
        d_scores[span, mine] = (
            exps[span, mine].astype(jnp.float32) * (d_probs - offset)
        ).astype(jnp.bfloat16)
        query_grad = score_scale * jnp.dot(
            k_low_t[:, span], d_scores[span, mine], preferred_element_type=jnp.float32
        ).T
        raw = q_ref[0, mine, :].astype(jnp.float32)
        inverse_rms = q_rms[mine, :]
        q_gain_sum = q_gain_sum + jnp.sum(query_grad * (raw * inverse_rms), axis=0, keepdims=True)
        dq_ref[0, mine, :] = norm_back(query_grad, raw, inverse_rms, q_gain).astype(dq_ref.dtype)

    pieces = [(tile, tile + 1, 0, tile + 1) for tile in range(blocks - 1)]
    pieces += [(blocks - 1, tiles + 1, 0, blocks)]
    pieces += [(tiles + block, tiles + block + 1, block, blocks) for block in range(1, blocks)]
    k_gain_sum = jnp.zeros_like(k_gain)
    for first, last, low, high in pieces:
        meets = slice(low * lanes, high * lanes)
        keys = slice(first * TILE, last * TILE)
        value_grad = jnp.dot(
            exps[keys, meets], g_low[meets, :], preferred_element_type=jnp.float32
        )
        key_grad = score_scale * jnp.dot(
            d_scores[keys, meets], q_low[meets, :], preferred_element_type=jnp.float32
        )
        for place, (ref, out) in enumerate(
            zip(key_refs, (d_far_ref, d_near_ref, d_own_ref), strict=True)
        ):
            start = max(first * TILE, place * rows)
            stop = min(last * TILE, (place + 1) * rows)
            if start >= stop:
                continue
            inside = slice(start - place * rows, stop - place * rows)
            here = slice(start - first * TILE, stop - first * TILE)
            unit = ref[0, 0, inside, :].astype(jnp.float32) * k_rms[start:stop, :]
            k_gain_sum = k_gain_sum + jnp.sum(key_grad[here] * unit, axis=0, keepdims=True)
            out[0, 0, inside, :] = key_grad[here].astype(out.dtype)
            out[1, 0, inside, :] = value_grad[here].astype(out.dtype)
    gains_ref[0:1, :] += q_gain_sum
    gains_ref[1:2, :] += k_gain_sum


def closed(shard_ref, own, returned, swapped, kind, head):
    keep = jnp.where(shard_ref[0] % 2 == 1, 0.0, 1.0)
    own, returned, swapped = (
        part[kind, head].astype(jnp.float32) for part in (own, returned, swapped)
    )
    return own + returned + keep * swapped


def close_kernel(shard_ref, own, returned, swapped, raw_ref, k_gain_ref, out):
    for head in range(own.shape[1]):
        grad = closed(shard_ref, own, returned, swapped, 0, head)
        raw = raw_ref[0, head].astype(jnp.float32)
        grad = norm_back(grad, raw, inverse_rms_of(raw), k_gain_ref[...])
        out[0, head] = grad.astype(out.dtype)
        out[1, head] = closed(shard_ref, own, returned, swapped, 1, head).astype(out.dtype)


def finish_kernel(shard_ref, own, returned, swapped, raw_ref, k_gain_ref, *rest):
    *done, key_out, value_out, by_token = rest
    before = [(part, head) for part in done for head in range(part.shape[1])]
    for kind, out in ((0, key_out), (1, value_out)):
        for place, (part, head) in enumerate(before):
            by_token[:, place, :] = part[kind, head].astype(jnp.float32)
        for head in range(own.shape[1]):
            grad = closed(shard_ref, own, returned, swapped, kind, head)
            if kind == 0:
                raw = raw_ref[0, head].astype(jnp.float32)
                grad = norm_back(grad, raw, inverse_rms_of(raw), k_gain_ref[...])
            by_token[:, len(before) + head, :] = grad
        out[...] = by_token[...].astype(out.dtype)


def later_kernel(*refs):
    pass


def later(array):
    anywhere = pl.BlockSpec(memory_space=pl.ANY)
    return pl.pallas_call(
        later_kernel,
        in_specs=[anywhere],
        out_specs=anywhere,
        out_shape=jax.ShapeDtypeStruct(array.shape, array.dtype),
        input_output_aliases={0: 0},
        cost_estimate=HEAVY,
    )(array)


def group_grads(shard, first, here, count, queries, grads, own, near, far, q_gain, k_gain):
    _, _, rows, width = own.shape
    query_rows = queries.shape[1]
    span = WINDOW + rows
    whole_q = pl.BlockSpec((1, query_rows, width), lambda head: (first + head, 0, 0))
    part = pl.BlockSpec((2, 1, rows, width), lambda head: (0, head, 0, 0))
    held = pl.BlockSpec((2, 1, rows, width), lambda head: (0, here + head, 0, 0))
    gain = pl.BlockSpec((1, width), lambda head: (0, 0))
    shape = (2, count, rows, width)
    return pl.pallas_call(
        heads_kernel,
        grid=(count,),
        in_specs=[
            pl.BlockSpec(memory_space=pltpu.SMEM), whole_q, whole_q, held, held, held, gain, gain,
        ],
        out_specs=[
            pl.BlockSpec((1, query_rows, width), lambda head: (head, 0, 0)),
            part,
            part,
            part,
            pl.BlockSpec((2, width), lambda head: (0, 0)),
        ],
        out_shape=[
            jax.ShapeDtypeStruct((count, query_rows, width), jnp.bfloat16),
            jax.ShapeDtypeStruct(shape, jnp.bfloat16),
            jax.ShapeDtypeStruct(shape, jnp.bfloat16),
            jax.ShapeDtypeStruct(shape, jnp.bfloat16),
            jax.ShapeDtypeStruct((2, width), jnp.float32),
        ],
        scratch_shapes=[
            pltpu.VMEM((span, width), jnp.bfloat16),
            pltpu.VMEM((width, span), jnp.bfloat16),
            pltpu.VMEM((span, width), jnp.float32),
            pltpu.VMEM((span, width), jnp.bfloat16),
            pltpu.VMEM((width, span), jnp.bfloat16),
            pltpu.VMEM((query_rows, width), jnp.bfloat16),
            pltpu.VMEM((query_rows, width), jnp.float32),
            pltpu.VMEM((query_rows, width), jnp.bfloat16),
            pltpu.VMEM((span, query_rows), jnp.bfloat16),
            pltpu.VMEM((span, query_rows), jnp.bfloat16),
        ],
        compiler_params=pltpu.CompilerParams(vmem_limit_bytes=60 * 1024 * 1024),
        cost_estimate=LIGHT,
    )(shard, queries, grads, own, near, far, q_gain, k_gain)


def close_group(shard, own, returned, swapped, raw, k_gain):
    smem, vmem = (pl.BlockSpec(memory_space=space) for space in (pltpu.SMEM, pltpu.VMEM))
    return pl.pallas_call(
        close_kernel,
        in_specs=[smem] + [vmem] * 5,
        out_specs=vmem,
        out_shape=jax.ShapeDtypeStruct(own.shape, jnp.bfloat16),
        cost_estimate=LIGHT,
    )(shard, own, returned, swapped, raw, k_gain)


def finish(shard, own, returned, swapped, raw, k_gain, done):
    _, count, rows, width = own.shape
    kv_dev = count + sum(part.shape[1] for part in done)
    shape = (rows, kv_dev, width)
    smem, vmem = (pl.BlockSpec(memory_space=space) for space in (pltpu.SMEM, pltpu.VMEM))
    return pl.pallas_call(
        finish_kernel,
        in_specs=[smem] + [vmem] * (5 + len(done)),
        out_specs=[vmem, vmem],
        out_shape=[jax.ShapeDtypeStruct(shape, jnp.bfloat16)] * 2,
        scratch_shapes=[pltpu.VMEM(shape, jnp.float32)],
        compiler_params=pltpu.CompilerParams(vmem_limit_bytes=40 * 1024 * 1024),
    )(shard, own, returned, swapped, raw, k_gain, *done)


def group_sizes(kv_dev):
    count = min(GROUPS, kv_dev)
    return [(kv_dev + count - 1 - place) // count for place in range(count)]


def summed(value, axis, step, stop=None):
    count = lax.axis_size(axis)
    assert count & (count - 1) == 0
    while step < (stop or count):
        pairs = [(source, source ^ step) for source in range(count)]
        value = value + lax.ppermute(value, axis, pairs)
        step *= 2
    return value


def per_device(query, key, value, grad_out, q_gain, k_gain):
    rows, heads, width = query.shape
    kv_dev = key.shape[1]
    group = heads // kv_dev
    count = lax.axis_size("seq")
    assert 2 * rows == WINDOW and rows % TILE == 0 and count % 2 == 0
    shard = lax.axis_index("seq")
    odd = shard % 2 == 1
    ahead = [(source, source + 2) for source in range(count - 2)]
    back = [(source + 2, source) for source in range(count - 2)]
    swap = [(source, source ^ 1) for source in range(count)]

    def by_head(array):
        split = array.reshape(rows, kv_dev, group, width)
        return jnp.transpose(split, (1, 0, 2, 3)).reshape(kv_dev, rows * group, width)

    sizes = group_sizes(kv_dev)
    starts = [sum(sizes[:place]) for place in range(len(sizes))]
    cuts = [(0, sizes[0])] + ([(sizes[0], kv_dev)] if len(sizes) > 1 else [])
    by_kind = lax.optimization_barrier([jnp.transpose(kind, (1, 0, 2)) for kind in (key, value)])
    owns = [jnp.stack([kind[low:high] for kind in by_kind]) for low, high in cuts]
    fars = [lax.ppermute(own, "seq", ahead) for own in owns]
    queries, grads = by_head(query), by_head(grad_out)
    scalar = shard.astype(jnp.int32).reshape(1)
    q_gain_2d, k_gain_2d = q_gain.reshape(1, width), k_gain.reshape(1, width)

    def split(d_own, d_near, d_far, raw):
        swapped = lax.ppermute(d_near, "seq", swap)
        from_pair = jnp.where(odd, swapped.astype(jnp.float32), 0.0)
        relayed = (d_far.astype(jnp.float32) + from_pair).astype(jnp.bfloat16)
        return relayed, (d_own, swapped, raw)

    def close(stays, returned):
        d_own, swapped, raw = stays
        return close_group(scalar, d_own, returned, swapped, raw, k_gain_2d)

    dq_parts, gains, kept, done = [], [], [], []
    grads_out = None
    for place, (first, size) in enumerate(zip(starts, sizes, strict=True)):
        if grads_out is not None:
            relayed, stays = split(*grads_out)
        if place < 2:
            own, far, start = owns[place], fars[place], cuts[place][0]
            if place:
                far, relayed = lax.optimization_barrier((later(far), relayed))
            else:
                far, queries, grads, *_ = lax.optimization_barrier(
                    (far, queries, grads, *owns[1:])
                )
            near = lax.ppermute(jnp.where(odd, far, own), "seq", swap)
        if grads_out is not None:
            if kept:
                before, returned = kept.pop()
                near, returned, relayed = lax.optimization_barrier((near, later(returned), relayed))
                done.append(close(before, returned))
            kept.append((stays, lax.ppermute(relayed, "seq", back)))
        here = slice(first - start, first - start + size)
        dq, *grads_out, gain = group_grads(
            scalar, first, first - start, size, queries, grads, own, near, far, q_gain_2d, k_gain_2d
        )
        grads_out.append(own[:1, here])
        dq_parts.append(dq)
        gains.append(gain)
    relayed, stays = split(*grads_out)
    gain_sum = sum(gains[1:], gains[0])
    if kept:
        before, returned = kept.pop()
        returned, done = lax.optimization_barrier((returned, done))
        returned, gain_sum = lax.optimization_barrier((later(returned), gain_sum))
        done.append(close(before, returned))
    gain_sum = summed(gain_sum, "seq", 2)
    relayed, gain_sum = lax.optimization_barrier((relayed, gain_sum))
    returned = lax.ppermute(relayed, "seq", back)
    gain_sum = summed(gain_sum, "seq", 1, 2)
    gain_sum = summed(gain_sum, "head", 1)
    d_own, swapped, raw = stays
    grad_key, grad_value = finish(scalar, d_own, returned, swapped, raw, k_gain_2d, done)
    grad_query = jnp.concatenate(dq_parts).reshape(kv_dev, rows, group, width)
    grad_query = jnp.transpose(grad_query, (1, 0, 2, 3)).reshape(rows, heads, width)
    return (grad_query, grad_key, grad_value, gain_sum[0], gain_sum[1])


def solution(mesh):
    split, whole = P("seq", "head", None), P()
    return jax.shard_map(
        per_device,
        mesh=mesh,
        in_specs=(split, split, split, split, whole, whole),
        out_specs=(split, split, split, whole, whole),
        check_vma=False,
    )
```

```python
import functools

import jax
import jax.numpy as jnp
from jax import lax
from jax.experimental import pallas as pl
from jax.experimental.pallas import tpu as pltpu
from jax.sharding import PartitionSpec as P

WINDOW = 1024
TILE = 128

score_scale = 168.0 ** (-0.5)
norm_eps = 1e-06
exp2_scale = score_scale * 1.4426950408889634

GROUPS = 3
HEAVY = pl.CostEstimate(flops=10**11, bytes_accessed=10**8, transcendentals=0)
LIGHT = pl.CostEstimate(flops=1000, bytes_accessed=1000, transcendentals=0)

NT = (((1,), (1,)), ((), ()))


def inverse_rms_of(as_float):
    return lax.rsqrt(jnp.mean(as_float * as_float, axis=-1, keepdims=True) + norm_eps)


def norm_back(d_normed, raw, inverse_rms, gain_vec):
    unit_rows = raw * inverse_rms
    d_unit = d_normed * gain_vec
    return inverse_rms * (
        d_unit - unit_rows * jnp.mean(d_unit * unit_rows, axis=-1, keepdims=True)
    )


def heads_kernel(
    shard_ref, q_ref, g_ref, own_ref, near_ref, far_ref, q_gain_ref, k_gain_ref,
    dq_ref, d_own_ref, d_near_ref, d_far_ref, gains_ref,
    k_low, k_low_t, values, q_low, probs_all, d_scores_all,
):
    rows = own_ref.shape[2]
    group = q_ref.shape[1] // rows
    lanes = TILE * group
    blocks = rows // TILE
    tiles = WINDOW // TILE
    q_gain, k_gain = q_gain_ref[...], k_gain_ref[...]
    far_ok = jnp.where(shard_ref[0] >= 2, 1.0, 0.0)
    near_ok = jnp.where(shard_ref[0] >= 1, 1.0, 0.0)
    key_refs = (far_ref, near_ref, own_ref)

    @pl.when(pl.program_id(0) == 0)
    def _():
        gains_ref[...] = jnp.zeros_like(gains_ref)

    for place, ref in enumerate(key_refs):
        raw = ref[0, 0].astype(jnp.float32)
        here = slice(place * rows, (place + 1) * rows)
        k_low[here, :] = (raw * inverse_rms_of(raw) * k_gain).astype(jnp.bfloat16)
        values[here, :] = ref[1, 0]
    k_low_t[...] = k_low[...].T
    raw_q = q_ref[0].astype(jnp.float32)
    q_low[...] = (raw_q * inverse_rms_of(raw_q) * q_gain).astype(jnp.bfloat16)

    key_ids = lax.broadcasted_iota(jnp.int32, (TILE, lanes), 0)
    token_ids = lax.broadcasted_iota(jnp.int32, (TILE, lanes), 1) // group
    late = key_ids <= token_ids
    edge_ok = jnp.where(late, 1.0, far_ok)
    q_gain_sum = jnp.zeros_like(q_gain)

    for block in range(blocks):
        span = slice(block * TILE, block * TILE + WINDOW + TILE)
        mine = slice(block * lanes, (block + 1) * lanes)
        scores = lax.dot_general(
            k_low[span, :], q_low[mine, :], NT, preferred_element_type=jnp.float32
        )
        scores = jnp.concatenate(
            [jnp.where(late, scores[WINDOW:], scores[:TILE]), scores[TILE:WINDOW]], axis=0
        )
        exp_scores = jnp.exp2(scores * exp2_scale)
        edge = exp_scores[:TILE] * edge_ok
        first_near = (blocks - block) * TILE
        first_own = first_near + rows
        total = jnp.sum(edge, axis=0, keepdims=True)
        for low, high, ok in (
            (TILE, first_near, far_ok),
            (first_near, min(first_own, WINDOW), near_ok),
            (first_own, WINDOW, None),
        ):
            if low < high:
                part = jnp.sum(exp_scores[low:high], axis=0, keepdims=True)
                total = total + (part if ok is None else part * ok)
        inverse = 1.0 / total
        probs = jnp.concatenate([edge, exp_scores[TILE:]], axis=0) * inverse
        d_probs = lax.dot_general(
            values[span, :], g_ref[0, mine, :], NT, preferred_element_type=jnp.float32
        )
        d_probs = jnp.concatenate(
            [jnp.where(late, d_probs[WINDOW:], d_probs[:TILE]), d_probs[TILE:WINDOW]], axis=0
        )
        offset = jnp.sum(probs * d_probs, axis=0, keepdims=True)
        d_scores = probs * (d_probs - offset)
        for whole, held in ((probs, probs_all), (d_scores, d_scores_all)):
            start = block * TILE
            held[start : start + TILE, mine] = jnp.where(late, 0.0, whole[:TILE]).astype(
                jnp.bfloat16
            )
            held[start + TILE : start + WINDOW, mine] = whole[TILE:].astype(jnp.bfloat16)
            held[start + WINDOW : start + WINDOW + TILE, mine] = jnp.where(
                late, whole[:TILE], 0.0
            ).astype(jnp.bfloat16)
        query_grad = score_scale * jnp.dot(
            k_low_t[:, span], d_scores_all[span, mine], preferred_element_type=jnp.float32
        ).T
        raw = q_ref[0, mine, :].astype(jnp.float32)
        inverse_rms = inverse_rms_of(raw)
        q_gain_sum = q_gain_sum + jnp.sum(query_grad * (raw * inverse_rms), axis=0, keepdims=True)
        dq_ref[0, mine, :] = norm_back(query_grad, raw, inverse_rms, q_gain).astype(dq_ref.dtype)

    pieces = [(tile, tile + 1, 0, tile + 1) for tile in range(blocks - 1)]
    pieces += [(blocks - 1, tiles + 1, 0, blocks)]
    pieces += [(tiles + block, tiles + block + 1, block, blocks) for block in range(1, blocks)]
    k_gain_sum = jnp.zeros_like(k_gain)
    for first, last, low, high in pieces:
        meets = slice(low * lanes, high * lanes)
        keys = slice(first * TILE, last * TILE)
        value_grad = jnp.dot(
            probs_all[keys, meets], g_ref[0, meets, :], preferred_element_type=jnp.float32
        )
        key_grad = score_scale * jnp.dot(
            d_scores_all[keys, meets], q_low[meets, :], preferred_element_type=jnp.float32
        )
        for place, (ref, out) in enumerate(
            zip(key_refs, (d_far_ref, d_near_ref, d_own_ref), strict=True)
        ):
            start = max(first * TILE, place * rows)
            stop = min(last * TILE, (place + 1) * rows)
            if start >= stop:
                continue
            inside = slice(start - place * rows, stop - place * rows)
            here = slice(start - first * TILE, stop - first * TILE)
            raw = ref[0, 0, inside, :].astype(jnp.float32)
            k_gain_sum = k_gain_sum + jnp.sum(
                key_grad[here] * (raw * inverse_rms_of(raw)), axis=0, keepdims=True
            )
            out[0, 0, inside, :] = key_grad[here].astype(out.dtype)
            out[1, 0, inside, :] = value_grad[here].astype(out.dtype)
    gains_ref[0:1, :] += q_gain_sum
    gains_ref[1:2, :] += k_gain_sum


def closed(shard_ref, own, returned, swapped, kind, head):
    keep = jnp.where(shard_ref[0] % 2 == 1, 0.0, 1.0)
    own, returned, swapped = (
        part[kind, head].astype(jnp.float32) for part in (own, returned, swapped)
    )
    return own + returned + keep * swapped


def close_kernel(shard_ref, own, returned, swapped, raw_ref, k_gain_ref, out):
    for head in range(own.shape[1]):
        grad = closed(shard_ref, own, returned, swapped, 0, head)
        raw = raw_ref[0, head].astype(jnp.float32)
        grad = norm_back(grad, raw, inverse_rms_of(raw), k_gain_ref[...])
        out[0, head] = grad.astype(out.dtype)
        out[1, head] = closed(shard_ref, own, returned, swapped, 1, head).astype(out.dtype)


def finish_kernel(shard_ref, own, returned, swapped, raw_ref, k_gain_ref, *rest):
    *done, key_out, value_out, by_token = rest
    before = [(part, head) for part in done for head in range(part.shape[1])]
    for kind, out in ((0, key_out), (1, value_out)):
        for place, (part, head) in enumerate(before):
            by_token[:, place, :] = part[kind, head].astype(jnp.float32)
        for head in range(own.shape[1]):
            grad = closed(shard_ref, own, returned, swapped, kind, head)
            if kind == 0:
                raw = raw_ref[0, head].astype(jnp.float32)
                grad = norm_back(grad, raw, inverse_rms_of(raw), k_gain_ref[...])
            by_token[:, len(before) + head, :] = grad
        out[...] = by_token[...].astype(out.dtype)


def later_kernel(corner_ref, in_ref, out_ref):
    if len(in_ref.shape) == 1:
        out_ref[0] = in_ref[0]
    else:
        out_ref[...] = in_ref[...]


def later(array, small):
    vmem = pl.BlockSpec(memory_space=pltpu.VMEM)
    held = pl.BlockSpec(memory_space=pltpu.SMEM if small.ndim == 1 else pltpu.VMEM)
    return pl.pallas_call(
        later_kernel,
        in_specs=[vmem, held],
        out_specs=held,
        out_shape=jax.ShapeDtypeStruct(small.shape, small.dtype),
        compiler_params=pltpu.CompilerParams(vmem_limit_bytes=1024 * 1024),
        cost_estimate=HEAVY,
    )(array[0, 0, :16], small)


def group_grads(shard, first, here, count, queries, grads, own, near, far, q_gain, k_gain):
    _, _, rows, width = own.shape
    query_rows = queries.shape[1]
    span = WINDOW + rows
    whole_q = pl.BlockSpec((1, query_rows, width), lambda head: (first + head, 0, 0))
    part = pl.BlockSpec((2, 1, rows, width), lambda head: (0, head, 0, 0))
    held = pl.BlockSpec((2, 1, rows, width), lambda head: (0, here + head, 0, 0))
    gain = pl.BlockSpec((1, width), lambda head: (0, 0))
    shape = (2, count, rows, width)
    return pl.pallas_call(
        heads_kernel,
        grid=(count,),
        in_specs=[
            pl.BlockSpec(memory_space=pltpu.SMEM), whole_q, whole_q, held, held, held, gain, gain,
        ],
        out_specs=[
            pl.BlockSpec((1, query_rows, width), lambda head: (head, 0, 0)),
            part,
            part,
            part,
            pl.BlockSpec((2, width), lambda head: (0, 0)),
        ],
        out_shape=[
            jax.ShapeDtypeStruct((count, query_rows, width), jnp.bfloat16),
            jax.ShapeDtypeStruct(shape, jnp.bfloat16),
            jax.ShapeDtypeStruct(shape, jnp.bfloat16),
            jax.ShapeDtypeStruct(shape, jnp.bfloat16),
            jax.ShapeDtypeStruct((2, width), jnp.float32),
        ],
        scratch_shapes=[
            pltpu.VMEM((span, width), jnp.bfloat16),
            pltpu.VMEM((width, span), jnp.bfloat16),
            pltpu.VMEM((span, width), jnp.bfloat16),
            pltpu.VMEM((query_rows, width), jnp.bfloat16),
            pltpu.VMEM((span, query_rows), jnp.bfloat16),
            pltpu.VMEM((span, query_rows), jnp.bfloat16),
        ],
        compiler_params=pltpu.CompilerParams(vmem_limit_bytes=22 * 1024 * 1024),
        cost_estimate=LIGHT,
    )(shard, queries, grads, own, near, far, q_gain, k_gain)


def close_group(shard, own, returned, swapped, raw, k_gain):
    smem, vmem = (pl.BlockSpec(memory_space=space) for space in (pltpu.SMEM, pltpu.VMEM))
    return pl.pallas_call(
        close_kernel,
        in_specs=[smem] + [vmem] * 5,
        out_specs=vmem,
        out_shape=jax.ShapeDtypeStruct(own.shape, jnp.bfloat16),
        compiler_params=pltpu.CompilerParams(vmem_limit_bytes=12 * 1024 * 1024),
        cost_estimate=LIGHT,
    )(shard, own, returned, swapped, raw, k_gain)


def finish(shard, own, returned, swapped, raw, k_gain, done):
    _, count, rows, width = own.shape
    kv_dev = count + sum(part.shape[1] for part in done)
    shape = (rows, kv_dev, width)
    smem, vmem = (pl.BlockSpec(memory_space=space) for space in (pltpu.SMEM, pltpu.VMEM))
    return pl.pallas_call(
        finish_kernel,
        in_specs=[smem] + [vmem] * (5 + len(done)),
        out_specs=[vmem, vmem],
        out_shape=[jax.ShapeDtypeStruct(shape, jnp.bfloat16)] * 2,
        scratch_shapes=[pltpu.VMEM(shape, jnp.float32)],
        compiler_params=pltpu.CompilerParams(vmem_limit_bytes=20 * 1024 * 1024),
    )(shard, own, returned, swapped, raw, k_gain, *done)


def group_sizes(kv_dev):
    count = min(GROUPS, kv_dev)
    return [(kv_dev + count - 1 - place) // count for place in range(count)]


def exchanged(value, axis, step):
    pairs = [(source, source ^ step) for source in range(lax.axis_size(axis))]
    return lax.ppermute(value, axis, pairs)


def steps_of(axis):
    count = lax.axis_size(axis)
    assert count & (count - 1) == 0
    return [(axis, 1 << place) for place in range(count.bit_length() - 1)]


def per_device(query, key, value, grad_out, q_gain, k_gain):
    rows, heads, width = query.shape
    kv_dev = key.shape[1]
    group = heads // kv_dev
    count = lax.axis_size("seq")
    assert 2 * rows == WINDOW and rows % TILE == 0 and count % 2 == 0
    shard = lax.axis_index("seq")
    odd = shard % 2 == 1
    ahead = [(source, source + 2) for source in range(count - 2)]
    back = [(source + 2, source) for source in range(count - 2)]
    swap = [(source, source ^ 1) for source in range(count)]

    def by_head(array):
        split = array.reshape(rows, kv_dev, group, width)
        return jnp.transpose(split, (1, 0, 2, 3)).reshape(kv_dev, rows * group, width)

    sizes = group_sizes(kv_dev)
    starts = [sum(sizes[:place]) for place in range(len(sizes))]
    cuts = [(0, sizes[0])] + ([(sizes[0], kv_dev)] if len(sizes) > 1 else [])
    by_kind = lax.optimization_barrier([jnp.transpose(kind, (1, 0, 2)) for kind in (key, value)])
    owns = [jnp.stack([kind[low:high] for kind in by_kind]) for low, high in cuts]
    fars = [lax.ppermute(own, "seq", ahead) for own in owns]
    queries, grads = by_head(query), by_head(grad_out)
    scalar = shard.astype(jnp.int32).reshape(1)
    q_gain_2d, k_gain_2d = q_gain.reshape(1, width), k_gain.reshape(1, width)

    def split(d_own, d_near, d_far, raw):
        swapped = lax.ppermute(d_near, "seq", swap)
        from_pair = jnp.where(odd, swapped.astype(jnp.float32), 0.0)
        relayed = (d_far.astype(jnp.float32) + from_pair).astype(jnp.bfloat16)
        return relayed, (d_own, swapped, raw)

    def close(stays, returned):
        d_own, swapped, raw = stays
        return close_group(scalar, d_own, returned, swapped, raw, k_gain_2d)

    dq_parts, gains, kept, done = [], [], [], []
    grads_out = None
    for place, (first, size) in enumerate(zip(starts, sizes, strict=True)):
        if grads_out is not None:
            relayed, stays = split(*grads_out)
        if place < 2:
            own, far, start = owns[place], fars[place], cuts[place][0]
            if place:
                far, gains[0] = lax.optimization_barrier((far, gains[0]))
            else:
                far, queries, grads, *_ = lax.optimization_barrier(
                    (far, queries, grads, *owns[1:])
                )
            near = lax.ppermute(jnp.where(odd, far, own), "seq", swap)
        scalar_now = scalar
        if grads_out is not None:
            if kept:
                before, returned = kept.pop()
                scalar_now = later(returned, scalar)
                done.append(close(before, returned))
            near, relayed, scalar_now = lax.optimization_barrier((near, relayed, scalar_now))
            kept.append((stays, lax.ppermute(relayed, "seq", back)))
        here = slice(first - start, first - start + size)
        dq, *grads_out, gain = group_grads(
            scalar_now, first, first - start, size, queries, grads, own, near, far, q_gain_2d, k_gain_2d
        )
        grads_out.append(own[:1, here])
        dq_parts.append(dq)
        gains.append(gain)
    relayed, stays = split(*grads_out)
    gain_sum = sum(gains[1:], gains[0])
    if kept:
        before, returned = kept.pop()
        returned, done = lax.optimization_barrier((returned, done))
        gain_sum = later(returned, gain_sum)
        done.append(close(before, returned))
    core, *chips = steps_of("seq")
    gain_sum = gain_sum + exchanged(gain_sum, *chips[0])
    relayed, gain_sum = lax.optimization_barrier((relayed, gain_sum))
    returned = lax.ppermute(relayed, "seq", back)
    grad_query = jnp.concatenate(dq_parts).reshape(kv_dev, rows, group, width)
    grad_query = jnp.transpose(grad_query, (1, 0, 2, 3)).reshape(rows, heads, width)
    *early, last = [core, *steps_of("head"), *chips[1:]]
    for step in early:
        gain_sum = gain_sum + exchanged(gain_sum, *step)
    gain_sum, grad_query, done = lax.optimization_barrier((gain_sum, grad_query, done))
    d_own, swapped, raw = stays
    grad_key, grad_value = finish(scalar, d_own, returned, swapped, raw, k_gain_2d, done)
    other, grad_key = lax.optimization_barrier((exchanged(gain_sum, *last), grad_key))
    gain_sum = gain_sum + other
    return (grad_query, grad_key, grad_value, gain_sum[0], gain_sum[1])


def solution(mesh):
    split, whole = P("seq", "head", None), P()
    return jax.shard_map(
        per_device,
        mesh=mesh,
        in_specs=(split, split, split, split, whole, whole),
        out_specs=(split, split, split, whole, whole),
        check_vma=False,
    )
```

```python
import functools

import jax
import jax.numpy as jnp
from jax import lax
from jax.experimental import pallas as pl
from jax.experimental.pallas import tpu as pltpu
from jax.sharding import PartitionSpec as P

WINDOW = 1024
TILE = 128

score_scale = 168.0 ** (-0.5)
norm_eps = 1e-06
exp2_scale = score_scale * 1.4426950408889634

GROUPS = 3
HEAVY = pl.CostEstimate(flops=10**11, bytes_accessed=10**8, transcendentals=0)
LIGHT = pl.CostEstimate(flops=1000, bytes_accessed=1000, transcendentals=0)

NT = (((1,), (1,)), ((), ()))


def inverse_rms_of(as_float):
    return lax.rsqrt(jnp.mean(as_float * as_float, axis=-1, keepdims=True) + norm_eps)


def norm_back(d_normed, raw, inverse_rms, gain_vec):
    unit_rows = raw * inverse_rms
    d_unit = d_normed * gain_vec
    return inverse_rms * (
        d_unit - unit_rows * jnp.mean(d_unit * unit_rows, axis=-1, keepdims=True)
    )


def heads_kernel(
    shard_ref, q_ref, g_ref, own_ref, near_ref, far_ref, q_gain_ref, k_gain_ref,
    dq_ref, d_own_ref, d_near_ref, d_far_ref, gains_ref,
    k_low, k_low_t, values, q_low, probs_all, d_scores_all,
):
    rows = own_ref.shape[2]
    group = q_ref.shape[1] // rows
    lanes = TILE * group
    blocks = rows // TILE
    tiles = WINDOW // TILE
    q_gain, k_gain = q_gain_ref[...], k_gain_ref[...]
    far_ok = jnp.where(shard_ref[0] >= 2, 1.0, 0.0)
    near_ok = jnp.where(shard_ref[0] >= 1, 1.0, 0.0)
    key_refs = (far_ref, near_ref, own_ref)

    @pl.when(pl.program_id(0) == 0)
    def _():
        gains_ref[...] = jnp.zeros_like(gains_ref)

    for place, ref in enumerate(key_refs):
        raw = ref[0, 0].astype(jnp.float32)
        here = slice(place * rows, (place + 1) * rows)
        k_low[here, :] = (raw * inverse_rms_of(raw) * k_gain).astype(jnp.bfloat16)
        values[here, :] = ref[1, 0]
    k_low_t[...] = k_low[...].T
    raw_q = q_ref[0].astype(jnp.float32)
    q_low[...] = (raw_q * inverse_rms_of(raw_q) * q_gain).astype(jnp.bfloat16)

    key_ids = lax.broadcasted_iota(jnp.int32, (TILE, lanes), 0)
    token_ids = lax.broadcasted_iota(jnp.int32, (TILE, lanes), 1) // group
    late = key_ids <= token_ids
    edge_ok = jnp.where(late, 1.0, far_ok)
    q_gain_sum = jnp.zeros_like(q_gain)

    for block in range(blocks):
        span = slice(block * TILE, block * TILE + WINDOW + TILE)
        mine = slice(block * lanes, (block + 1) * lanes)
        scores = lax.dot_general(
            k_low[span, :], q_low[mine, :], NT, preferred_element_type=jnp.float32
        )
        scores = jnp.concatenate(
            [jnp.where(late, scores[WINDOW:], scores[:TILE]), scores[TILE:WINDOW]], axis=0
        )
        exp_scores = jnp.exp2(scores * exp2_scale)
        edge = exp_scores[:TILE] * edge_ok
        first_near = (blocks - block) * TILE
        first_own = first_near + rows
        total = jnp.sum(edge, axis=0, keepdims=True)
        for low, high, ok in (
            (TILE, first_near, far_ok),
            (first_near, min(first_own, WINDOW), near_ok),
            (first_own, WINDOW, None),
        ):
            if low < high:
                part = jnp.sum(exp_scores[low:high], axis=0, keepdims=True)
                total = total + (part if ok is None else part * ok)
        inverse = 1.0 / total
        probs = jnp.concatenate([edge, exp_scores[TILE:]], axis=0) * inverse
        d_probs = lax.dot_general(
            values[span, :], g_ref[0, mine, :], NT, preferred_element_type=jnp.float32
        )
        d_probs = jnp.concatenate(
            [jnp.where(late, d_probs[WINDOW:], d_probs[:TILE]), d_probs[TILE:WINDOW]], axis=0
        )
        offset = jnp.sum(probs * d_probs, axis=0, keepdims=True)
        d_scores = probs * (d_probs - offset)
        for whole, held in ((probs, probs_all), (d_scores, d_scores_all)):
            start = block * TILE
            held[start : start + TILE, mine] = jnp.where(late, 0.0, whole[:TILE]).astype(
                jnp.bfloat16
            )
            held[start + TILE : start + WINDOW, mine] = whole[TILE:].astype(jnp.bfloat16)
            held[start + WINDOW : start + WINDOW + TILE, mine] = jnp.where(
                late, whole[:TILE], 0.0
            ).astype(jnp.bfloat16)
        query_grad = score_scale * jnp.dot(
            k_low_t[:, span], d_scores_all[span, mine], preferred_element_type=jnp.float32
        ).T
        raw = q_ref[0, mine, :].astype(jnp.float32)
        inverse_rms = inverse_rms_of(raw)
        q_gain_sum = q_gain_sum + jnp.sum(query_grad * (raw * inverse_rms), axis=0, keepdims=True)
        dq_ref[0, mine, :] = norm_back(query_grad, raw, inverse_rms, q_gain).astype(dq_ref.dtype)

    pieces = [(tile, tile + 1, 0, tile + 1) for tile in range(blocks - 1)]
    pieces += [(blocks - 1, tiles + 1, 0, blocks)]
    pieces += [(tiles + block, tiles + block + 1, block, blocks) for block in range(1, blocks)]
    k_gain_sum = jnp.zeros_like(k_gain)
    for first, last, low, high in pieces:
        meets = slice(low * lanes, high * lanes)
        keys = slice(first * TILE, last * TILE)
        value_grad = jnp.dot(
            probs_all[keys, meets], g_ref[0, meets, :], preferred_element_type=jnp.float32
        )
        key_grad = score_scale * jnp.dot(
            d_scores_all[keys, meets], q_low[meets, :], preferred_element_type=jnp.float32
        )
        for place, (ref, out) in enumerate(
            zip(key_refs, (d_far_ref, d_near_ref, d_own_ref), strict=True)
        ):
            start = max(first * TILE, place * rows)
            stop = min(last * TILE, (place + 1) * rows)
            if start >= stop:
                continue
            inside = slice(start - place * rows, stop - place * rows)
            here = slice(start - first * TILE, stop - first * TILE)
            raw = ref[0, 0, inside, :].astype(jnp.float32)
            k_gain_sum = k_gain_sum + jnp.sum(
                key_grad[here] * (raw * inverse_rms_of(raw)), axis=0, keepdims=True
            )
            out[0, 0, inside, :] = key_grad[here].astype(out.dtype)
            out[1, 0, inside, :] = value_grad[here].astype(out.dtype)
    gains_ref[0:1, :] += q_gain_sum
    gains_ref[1:2, :] += k_gain_sum


def closed(shard_ref, own, returned, swapped, kind, head):
    keep = jnp.where(shard_ref[0] % 2 == 1, 0.0, 1.0)
    own, returned, swapped = (
        part[kind, head].astype(jnp.float32) for part in (own, returned, swapped)
    )
    return own + returned + keep * swapped


def close_kernel(shard_ref, own, returned, swapped, raw_ref, k_gain_ref, out):
    for head in range(own.shape[1]):
        grad = closed(shard_ref, own, returned, swapped, 0, head)
        raw = raw_ref[0, head].astype(jnp.float32)
        grad = norm_back(grad, raw, inverse_rms_of(raw), k_gain_ref[...])
        out[0, head] = grad.astype(out.dtype)
        out[1, head] = closed(shard_ref, own, returned, swapped, 1, head).astype(out.dtype)


def finish_kernel(shard_ref, own, returned, swapped, raw_ref, k_gain_ref, *rest):
    *done, key_out, value_out, by_token = rest
    before = [(part, head) for part in done for head in range(part.shape[1])]
    for kind, out in ((0, key_out), (1, value_out)):
        for place, (part, head) in enumerate(before):
            by_token[:, place, :] = part[kind, head].astype(jnp.float32)
        for head in range(own.shape[1]):
            grad = closed(shard_ref, own, returned, swapped, kind, head)
            if kind == 0:
                raw = raw_ref[0, head].astype(jnp.float32)
                grad = norm_back(grad, raw, inverse_rms_of(raw), k_gain_ref[...])
            by_token[:, len(before) + head, :] = grad
        out[...] = by_token[...].astype(out.dtype)


def choose_kernel(shard_ref, far_ref, own_ref, out_ref):
    odd = shard_ref[0] % 2 == 1

    @pl.when(odd)
    def _():
        out_ref[...] = far_ref[...]

    @pl.when(jnp.logical_not(odd))
    def _():
        out_ref[...] = own_ref[...]


def relay_kernel(shard_ref, far_ref, swapped_ref, out_ref):
    odd = jnp.where(shard_ref[0] % 2 == 1, 1.0, 0.0)
    total = far_ref[...].astype(jnp.float32) + odd * swapped_ref[...].astype(jnp.float32)
    out_ref[...] = total.astype(out_ref.dtype)


def small_call(kernel, shard, *arrays):
    smem, vmem = (pl.BlockSpec(memory_space=space) for space in (pltpu.SMEM, pltpu.VMEM))
    return pl.pallas_call(
        kernel,
        in_specs=[smem] + [vmem] * len(arrays),
        out_specs=vmem,
        out_shape=jax.ShapeDtypeStruct(arrays[0].shape, arrays[0].dtype),
        compiler_params=pltpu.CompilerParams(vmem_limit_bytes=12 * 1024 * 1024),
        cost_estimate=LIGHT,
    )(shard, *arrays)


def later_kernel(corner_ref, in_ref, out_ref):
    if len(in_ref.shape) == 1:
        out_ref[0] = in_ref[0]
    else:
        out_ref[...] = in_ref[...]


def later(array, small):
    vmem = pl.BlockSpec(memory_space=pltpu.VMEM)
    held = pl.BlockSpec(memory_space=pltpu.SMEM if small.ndim == 1 else pltpu.VMEM)
    return pl.pallas_call(
        later_kernel,
        in_specs=[vmem, held],
        out_specs=held,
        out_shape=jax.ShapeDtypeStruct(small.shape, small.dtype),
        compiler_params=pltpu.CompilerParams(vmem_limit_bytes=1024 * 1024),
        cost_estimate=HEAVY,
    )(array[0, 0, :16], small)


def group_grads(shard, first, here, count, queries, grads, own, near, far, q_gain, k_gain):
    _, _, rows, width = own.shape
    query_rows = queries.shape[1]
    span = WINDOW + rows
    whole_q = pl.BlockSpec((1, query_rows, width), lambda head: (first + head, 0, 0))
    part = pl.BlockSpec((2, 1, rows, width), lambda head: (0, head, 0, 0))
    held = pl.BlockSpec((2, 1, rows, width), lambda head: (0, here + head, 0, 0))
    gain = pl.BlockSpec((1, width), lambda head: (0, 0))
    shape = (2, count, rows, width)
    return pl.pallas_call(
        heads_kernel,
        grid=(count,),
        in_specs=[
            pl.BlockSpec(memory_space=pltpu.SMEM), whole_q, whole_q, held, held, held, gain, gain,
        ],
        out_specs=[
            pl.BlockSpec((1, query_rows, width), lambda head: (head, 0, 0)),
            part,
            part,
            part,
            pl.BlockSpec((2, width), lambda head: (0, 0)),
        ],
        out_shape=[
            jax.ShapeDtypeStruct((count, query_rows, width), jnp.bfloat16),
            jax.ShapeDtypeStruct(shape, jnp.bfloat16),
            jax.ShapeDtypeStruct(shape, jnp.bfloat16),
            jax.ShapeDtypeStruct(shape, jnp.bfloat16),
            jax.ShapeDtypeStruct((2, width), jnp.float32),
        ],
        scratch_shapes=[
            pltpu.VMEM((span, width), jnp.bfloat16),
            pltpu.VMEM((width, span), jnp.bfloat16),
            pltpu.VMEM((span, width), jnp.bfloat16),
            pltpu.VMEM((query_rows, width), jnp.bfloat16),
            pltpu.VMEM((span, query_rows), jnp.bfloat16),
            pltpu.VMEM((span, query_rows), jnp.bfloat16),
        ],
        compiler_params=pltpu.CompilerParams(vmem_limit_bytes=22 * 1024 * 1024),
        cost_estimate=LIGHT,
    )(shard, queries, grads, own, near, far, q_gain, k_gain)


def close_group(shard, own, returned, swapped, raw, k_gain):
    smem, vmem = (pl.BlockSpec(memory_space=space) for space in (pltpu.SMEM, pltpu.VMEM))
    return pl.pallas_call(
        close_kernel,
        in_specs=[smem] + [vmem] * 5,
        out_specs=vmem,
        out_shape=jax.ShapeDtypeStruct(own.shape, jnp.bfloat16),
        compiler_params=pltpu.CompilerParams(vmem_limit_bytes=12 * 1024 * 1024),
        cost_estimate=LIGHT,
    )(shard, own, returned, swapped, raw, k_gain)


def finish(shard, own, returned, swapped, raw, k_gain, done):
    _, count, rows, width = own.shape
    kv_dev = count + sum(part.shape[1] for part in done)
    shape = (rows, kv_dev, width)
    smem, vmem = (pl.BlockSpec(memory_space=space) for space in (pltpu.SMEM, pltpu.VMEM))
    return pl.pallas_call(
        finish_kernel,
        in_specs=[smem] + [vmem] * (5 + len(done)),
        out_specs=[vmem, vmem],
        out_shape=[jax.ShapeDtypeStruct(shape, jnp.bfloat16)] * 2,
        scratch_shapes=[pltpu.VMEM(shape, jnp.float32)],
        compiler_params=pltpu.CompilerParams(vmem_limit_bytes=20 * 1024 * 1024),
    )(shard, own, returned, swapped, raw, k_gain, *done)


def group_sizes(kv_dev):
    count = min(GROUPS, kv_dev)
    return [(kv_dev + count - 1 - place) // count for place in range(count)]


def exchanged(value, axis, low, high):
    count = lax.axis_size(axis)
    assert count & (count - 1) == 0
    return [
        lax.ppermute(value, axis, [(source, source ^ (mask << low)) for source in range(count)])
        for mask in range(1, 1 << max(high - low, 0))
    ]


def summed(value, axis, low, high):
    for place in range(low, high):
        value = value + exchanged(value, axis, place, place + 1)[0]
    return value


def per_device(query, key, value, grad_out, q_gain, k_gain):
    rows, heads, width = query.shape
    kv_dev = key.shape[1]
    group = heads // kv_dev
    count = lax.axis_size("seq")
    assert 2 * rows == WINDOW and rows % TILE == 0 and count % 2 == 0
    shard = lax.axis_index("seq")
    ahead = [(source, source + 2) for source in range(count - 2)]
    back = [(source + 2, source) for source in range(count - 2)]
    swap = [(source, source ^ 1) for source in range(count)]

    def by_head(array):
        split = array.reshape(rows, kv_dev, group, width)
        return jnp.transpose(split, (1, 0, 2, 3)).reshape(kv_dev, rows * group, width)

    sizes = group_sizes(kv_dev)
    starts = [sum(sizes[:place]) for place in range(len(sizes))]
    cuts = [(0, sizes[0])] + ([(sizes[0], kv_dev)] if len(sizes) > 1 else [])
    by_kind = lax.optimization_barrier([jnp.transpose(kind, (1, 0, 2)) for kind in (key, value)])
    owns = [jnp.stack([kind[low:high] for kind in by_kind]) for low, high in cuts]
    fars = [lax.ppermute(own, "seq", ahead) for own in owns]
    queries, grads = by_head(query), by_head(grad_out)
    scalar = shard.astype(jnp.int32).reshape(1)
    q_gain_2d, k_gain_2d = q_gain.reshape(1, width), k_gain.reshape(1, width)

    def split(d_own, d_near, d_far, raw):
        swapped = lax.ppermute(d_near, "seq", swap)
        relayed = small_call(relay_kernel, scalar, d_far, swapped)
        return relayed, (d_own, swapped, raw)

    def close(stays, returned):
        d_own, swapped, raw = stays
        return close_group(scalar, d_own, returned, swapped, raw, k_gain_2d)

    dq_parts, gains, kept, done = [], [], [], []
    grads_out = None
    for place, (first, size) in enumerate(zip(starts, sizes, strict=True)):
        if grads_out is not None:
            relayed, stays = split(*grads_out)
        if place < 2:
            own, far, start = owns[place], fars[place], cuts[place][0]
            if place:
                far, gains[0] = lax.optimization_barrier((far, gains[0]))
                gains[0] = later(far, gains[0])
                far, gains[0], relayed = lax.optimization_barrier((far, gains[0], relayed))
            else:
                far, queries, grads, *_ = lax.optimization_barrier(
                    (far, queries, grads, *owns[1:])
                )
            near = lax.ppermute(small_call(choose_kernel, scalar, far, own), "seq", swap)
        scalar_now = scalar
        if grads_out is not None:
            if kept:
                before, returned = kept.pop()
                scalar_now = later(returned, scalar)
                done.append(close(before, returned))
            near, relayed, scalar_now = lax.optimization_barrier((near, relayed, scalar_now))
            kept.append((stays, lax.ppermute(relayed, "seq", back)))
        here = slice(first - start, first - start + size)
        dq, *grads_out, gain = group_grads(
            scalar_now, first, first - start, size, queries, grads, own, near, far, q_gain_2d, k_gain_2d
        )
        grads_out.append(own[:1, here])
        dq_parts.append(dq)
        gains.append(gain)
    relayed, stays = split(*grads_out)
    gain_sum = sum(gains[1:], gains[0])
    if kept:
        before, returned = kept.pop()
        returned, done = lax.optimization_barrier((returned, done))
        gain_sum = later(returned, gain_sum)
        done.append(close(before, returned))
    returned = lax.ppermute(relayed, "seq", back)
    grad_query = jnp.concatenate(dq_parts).reshape(kv_dev, rows, group, width)
    grad_query = jnp.transpose(grad_query, (1, 0, 2, 3)).reshape(rows, heads, width)
    seq_bits, head_bits = ((lax.axis_size(axis) - 1).bit_length() for axis in ("seq", "head"))
    gain_sum = summed(gain_sum, "seq", 0, 1)
    gain_sum = summed(gain_sum, "head", 0, head_bits)
    gain_sum = summed(gain_sum, "seq", 1, seq_bits - 2)
    gain_sum, grad_query, done = lax.optimization_barrier((gain_sum, grad_query, done))
    d_own, swapped, raw = stays
    grad_key, grad_value = finish(scalar, d_own, returned, swapped, raw, k_gain_2d, done)
    others, grad_key = lax.optimization_barrier(
        (exchanged(gain_sum, "seq", max(seq_bits - 2, 1), seq_bits), grad_key)
    )
    gain_sum = (gain_sum + others[0]) + (others[1] + others[2]) if len(others) == 3 else sum(
        others, gain_sum
    )
    return (grad_query, grad_key, grad_value, gain_sum[0], gain_sum[1])


def solution(mesh):
    split, whole = P("seq", "head", None), P()
    return jax.shard_map(
        per_device,
        mesh=mesh,
        in_specs=(split, split, split, split, whole, whole),
        out_specs=(split, split, split, whole, whole),
        check_vma=False,
    )
```

```python
import functools

import jax
import jax.numpy as jnp
from jax import lax
from jax.experimental import pallas as pl
from jax.experimental.pallas import tpu as pltpu
from jax.sharding import PartitionSpec as P

WINDOW = 1024
TILE = 128

score_scale = 168.0 ** (-0.5)
norm_eps = 1e-06
exp2_scale = score_scale * 1.4426950408889634

GROUPS = 3
HEAVY = pl.CostEstimate(flops=10**11, bytes_accessed=10**8, transcendentals=0)
LIGHT = pl.CostEstimate(flops=1000, bytes_accessed=1000, transcendentals=0)

NT = (((1,), (1,)), ((), ()))


def inverse_rms_of(as_float):
    return lax.rsqrt(jnp.mean(as_float * as_float, axis=-1, keepdims=True) + norm_eps)


def norm_back(d_normed, raw, inverse_rms, gain_vec):
    unit_rows = raw * inverse_rms
    d_unit = d_normed * gain_vec
    return inverse_rms * (
        d_unit - unit_rows * jnp.mean(d_unit * unit_rows, axis=-1, keepdims=True)
    )


def heads_kernel(
    shard_ref, q_ref, g_ref, own_ref, near_ref, far_ref, q_gain_ref, k_gain_ref,
    dq_ref, d_own_ref, d_near_ref, d_far_ref, gains_ref,
    k_low, k_low_t, k_rms, values, q_low, q_rms, probs_all, d_scores_all,
):
    rows = own_ref.shape[2]
    group = q_ref.shape[1] // rows
    lanes = TILE * group
    blocks = rows // TILE
    tiles = WINDOW // TILE
    q_gain, k_gain = q_gain_ref[...], k_gain_ref[...]
    far_ok = jnp.where(shard_ref[0] >= 2, 1.0, 0.0)
    near_ok = jnp.where(shard_ref[0] >= 1, 1.0, 0.0)
    key_refs = (far_ref, near_ref, own_ref)

    @pl.when(pl.program_id(0) == 0)
    def _():
        gains_ref[...] = jnp.zeros_like(gains_ref)

    for place, ref in enumerate(key_refs):
        raw = ref[0, 0].astype(jnp.float32)
        here = slice(place * rows, (place + 1) * rows)
        inverse_rms = jnp.broadcast_to(inverse_rms_of(raw), raw.shape)
        k_rms[here, :] = inverse_rms
        k_low[here, :] = (raw * inverse_rms * k_gain).astype(jnp.bfloat16)
        values[here, :] = ref[1, 0]
    k_low_t[...] = k_low[...].T
    raw_q = q_ref[0].astype(jnp.float32)
    inverse_rms = jnp.broadcast_to(inverse_rms_of(raw_q), raw_q.shape)
    q_rms[...] = inverse_rms
    q_low[...] = (raw_q * inverse_rms * q_gain).astype(jnp.bfloat16)

    key_ids = lax.broadcasted_iota(jnp.int32, (TILE, lanes), 0)
    token_ids = lax.broadcasted_iota(jnp.int32, (TILE, lanes), 1) // group
    late = key_ids <= token_ids
    edge_ok = jnp.where(late, 1.0, far_ok)
    q_gain_sum = jnp.zeros_like(q_gain)

    for block in range(blocks):
        span = slice(block * TILE, block * TILE + WINDOW + TILE)
        mine = slice(block * lanes, (block + 1) * lanes)
        scores = lax.dot_general(
            k_low[span, :], q_low[mine, :], NT, preferred_element_type=jnp.float32
        )
        scores = jnp.concatenate(
            [jnp.where(late, scores[WINDOW:], scores[:TILE]), scores[TILE:WINDOW]], axis=0
        )
        exp_scores = jnp.exp2(scores * exp2_scale)
        edge = exp_scores[:TILE] * edge_ok
        first_near = (blocks - block) * TILE
        first_own = first_near + rows
        total = jnp.sum(edge, axis=0, keepdims=True)
        for low, high, ok in (
            (TILE, first_near, far_ok),
            (first_near, min(first_own, WINDOW), near_ok),
            (first_own, WINDOW, None),
        ):
            if low < high:
                part = jnp.sum(exp_scores[low:high], axis=0, keepdims=True)
                total = total + (part if ok is None else part * ok)
        inverse = 1.0 / total
        probs = jnp.concatenate([edge, exp_scores[TILE:]], axis=0) * inverse
        d_probs = lax.dot_general(
            values[span, :], g_ref[0, mine, :], NT, preferred_element_type=jnp.float32
        )
        d_probs = jnp.concatenate(
            [jnp.where(late, d_probs[WINDOW:], d_probs[:TILE]), d_probs[TILE:WINDOW]], axis=0
        )
        offset = jnp.sum(probs * d_probs, axis=0, keepdims=True)
        d_scores = probs * (d_probs - offset)
        for whole, held in ((probs, probs_all), (d_scores, d_scores_all)):
            start = block * TILE
            held[start : start + TILE, mine] = jnp.where(late, 0.0, whole[:TILE]).astype(
                jnp.bfloat16
            )
            held[start + TILE : start + WINDOW, mine] = whole[TILE:].astype(jnp.bfloat16)
            held[start + WINDOW : start + WINDOW + TILE, mine] = jnp.where(
                late, whole[:TILE], 0.0
            ).astype(jnp.bfloat16)
        query_grad = score_scale * jnp.dot(
            k_low_t[:, span], d_scores_all[span, mine], preferred_element_type=jnp.float32
        ).T
        raw = q_ref[0, mine, :].astype(jnp.float32)
        inverse_rms = q_rms[mine, :]
        q_gain_sum = q_gain_sum + jnp.sum(query_grad * (raw * inverse_rms), axis=0, keepdims=True)
        dq_ref[0, mine, :] = norm_back(query_grad, raw, inverse_rms, q_gain).astype(dq_ref.dtype)

    pieces = [(tile, tile + 1, 0, tile + 1) for tile in range(blocks - 1)]
    pieces += [(blocks - 1, tiles + 1, 0, blocks)]
    pieces += [(tiles + block, tiles + block + 1, block, blocks) for block in range(1, blocks)]
    k_gain_sum = jnp.zeros_like(k_gain)
    for first, last, low, high in pieces:
        meets = slice(low * lanes, high * lanes)
        keys = slice(first * TILE, last * TILE)
        value_grad = jnp.dot(
            probs_all[keys, meets], g_ref[0, meets, :], preferred_element_type=jnp.float32
        )
        key_grad = score_scale * jnp.dot(
            d_scores_all[keys, meets], q_low[meets, :], preferred_element_type=jnp.float32
        )
        for place, (ref, out) in enumerate(
            zip(key_refs, (d_far_ref, d_near_ref, d_own_ref), strict=True)
        ):
            start = max(first * TILE, place * rows)
            stop = min(last * TILE, (place + 1) * rows)
            if start >= stop:
                continue
            inside = slice(start - place * rows, stop - place * rows)
            here = slice(start - first * TILE, stop - first * TILE)
            unit = ref[0, 0, inside, :].astype(jnp.float32) * k_rms[start:stop, :]
            k_gain_sum = k_gain_sum + jnp.sum(key_grad[here] * unit, axis=0, keepdims=True)
            out[0, 0, inside, :] = key_grad[here].astype(out.dtype)
            out[1, 0, inside, :] = value_grad[here].astype(out.dtype)
    gains_ref[0:1, :] += q_gain_sum
    gains_ref[1:2, :] += k_gain_sum


def closed(shard_ref, own, returned, swapped, kind, head):
    keep = jnp.where(shard_ref[0] % 2 == 1, 0.0, 1.0)
    own, returned, swapped = (
        part[kind, head].astype(jnp.float32) for part in (own, returned, swapped)
    )
    return own + returned + keep * swapped


def close_kernel(shard_ref, own, returned, swapped, raw_ref, k_gain_ref, out):
    for head in range(own.shape[1]):
        grad = closed(shard_ref, own, returned, swapped, 0, head)
        raw = raw_ref[0, head].astype(jnp.float32)
        grad = norm_back(grad, raw, inverse_rms_of(raw), k_gain_ref[...])
        out[0, head] = grad.astype(out.dtype)
        out[1, head] = closed(shard_ref, own, returned, swapped, 1, head).astype(out.dtype)


def finish_kernel(shard_ref, own, returned, swapped, raw_ref, k_gain_ref, *rest):
    *done, key_out, value_out, by_token = rest
    rows, heads, _ = key_out.shape
    before = [(part, head) for part in done for head in range(part.shape[1])]
    for kind, out in ((0, key_out), (1, value_out)):
        for place, (part, head) in enumerate(before):
            by_token[pl.ds(place, rows, stride=heads), :] = part[kind, head].astype(jnp.float32)
        for head in range(own.shape[1]):
            grad = closed(shard_ref, own, returned, swapped, kind, head)
            if kind == 0:
                raw = raw_ref[0, head].astype(jnp.float32)
                grad = norm_back(grad, raw, inverse_rms_of(raw), k_gain_ref[...])
            by_token[pl.ds(len(before) + head, rows, stride=heads), :] = grad
        out[...] = by_token[...].reshape(out.shape).astype(out.dtype)


def choose_kernel(shard_ref, far_ref, own_ref, out_ref):
    odd = shard_ref[0] % 2 == 1

    @pl.when(odd)
    def _():
        out_ref[...] = far_ref[...]

    @pl.when(jnp.logical_not(odd))
    def _():
        out_ref[...] = own_ref[...]


def relay_kernel(shard_ref, far_ref, swapped_ref, out_ref):
    odd = jnp.where(shard_ref[0] % 2 == 1, 1.0, 0.0)
    total = far_ref[...].astype(jnp.float32) + odd * swapped_ref[...].astype(jnp.float32)
    out_ref[...] = total.astype(out_ref.dtype)


def small_call(kernel, shard, *arrays):
    smem, vmem = (pl.BlockSpec(memory_space=space) for space in (pltpu.SMEM, pltpu.VMEM))
    return pl.pallas_call(
        kernel,
        in_specs=[smem] + [vmem] * len(arrays),
        out_specs=vmem,
        out_shape=jax.ShapeDtypeStruct(arrays[0].shape, arrays[0].dtype),
        compiler_params=pltpu.CompilerParams(vmem_limit_bytes=12 * 1024 * 1024),
        cost_estimate=LIGHT,
    )(shard, *arrays)


def later_kernel(corner_ref, in_ref, out_ref):
    if len(in_ref.shape) == 1:
        out_ref[0] = in_ref[0]
    else:
        out_ref[...] = in_ref[...]


def later(array, small):
    vmem = pl.BlockSpec(memory_space=pltpu.VMEM)
    held = pl.BlockSpec(memory_space=pltpu.SMEM if small.ndim == 1 else pltpu.VMEM)
    return pl.pallas_call(
        later_kernel,
        in_specs=[vmem, held],
        out_specs=held,
        out_shape=jax.ShapeDtypeStruct(small.shape, small.dtype),
        compiler_params=pltpu.CompilerParams(vmem_limit_bytes=1024 * 1024),
        cost_estimate=HEAVY,
    )(array[0, 0, :16], small)


def group_grads(shard, first, here, count, queries, grads, own, near, far, q_gain, k_gain):
    _, _, rows, width = own.shape
    query_rows = queries.shape[1]
    span = WINDOW + rows
    whole_q = pl.BlockSpec((1, query_rows, width), lambda head: (first + head, 0, 0))
    part = pl.BlockSpec((2, 1, rows, width), lambda head: (0, head, 0, 0))
    held = pl.BlockSpec((2, 1, rows, width), lambda head: (0, here + head, 0, 0))
    gain = pl.BlockSpec((1, width), lambda head: (0, 0))
    shape = (2, count, rows, width)
    return pl.pallas_call(
        heads_kernel,
        grid=(count,),
        in_specs=[
            pl.BlockSpec(memory_space=pltpu.SMEM), whole_q, whole_q, held, held, held, gain, gain,
        ],
        out_specs=[
            pl.BlockSpec((1, query_rows, width), lambda head: (head, 0, 0)),
            part,
            part,
            part,
            pl.BlockSpec((2, width), lambda head: (0, 0)),
        ],
        out_shape=[
            jax.ShapeDtypeStruct((count, query_rows, width), jnp.bfloat16),
            jax.ShapeDtypeStruct(shape, jnp.bfloat16),
            jax.ShapeDtypeStruct(shape, jnp.bfloat16),
            jax.ShapeDtypeStruct(shape, jnp.bfloat16),
            jax.ShapeDtypeStruct((2, width), jnp.float32),
        ],
        scratch_shapes=[
            pltpu.VMEM((span, width), jnp.bfloat16),
            pltpu.VMEM((width, span), jnp.bfloat16),
            pltpu.VMEM((span, width), jnp.float32),
            pltpu.VMEM((span, width), jnp.bfloat16),
            pltpu.VMEM((query_rows, width), jnp.bfloat16),
            pltpu.VMEM((query_rows, width), jnp.float32),
            pltpu.VMEM((span, query_rows), jnp.bfloat16),
            pltpu.VMEM((span, query_rows), jnp.bfloat16),
        ],
        compiler_params=pltpu.CompilerParams(vmem_limit_bytes=22 * 1024 * 1024),
        cost_estimate=LIGHT,
    )(shard, queries, grads, own, near, far, q_gain, k_gain)


def close_group(shard, own, returned, swapped, raw, k_gain):
    smem, vmem = (pl.BlockSpec(memory_space=space) for space in (pltpu.SMEM, pltpu.VMEM))
    return pl.pallas_call(
        close_kernel,
        in_specs=[smem] + [vmem] * 5,
        out_specs=vmem,
        out_shape=jax.ShapeDtypeStruct(own.shape, jnp.bfloat16),
        compiler_params=pltpu.CompilerParams(vmem_limit_bytes=12 * 1024 * 1024),
        cost_estimate=LIGHT,
    )(shard, own, returned, swapped, raw, k_gain)


def finish(shard, own, returned, swapped, raw, k_gain, done):
    _, count, rows, width = own.shape
    kv_dev = count + sum(part.shape[1] for part in done)
    shape = (rows, kv_dev, width)
    smem, vmem = (pl.BlockSpec(memory_space=space) for space in (pltpu.SMEM, pltpu.VMEM))
    return pl.pallas_call(
        finish_kernel,
        in_specs=[smem] + [vmem] * (5 + len(done)),
        out_specs=[vmem, vmem],
        out_shape=[jax.ShapeDtypeStruct(shape, jnp.bfloat16)] * 2,
        scratch_shapes=[pltpu.VMEM((rows * kv_dev, width), jnp.float32)],
        compiler_params=pltpu.CompilerParams(vmem_limit_bytes=20 * 1024 * 1024),
    )(shard, own, returned, swapped, raw, k_gain, *done)


def group_sizes(kv_dev):
    count = min(GROUPS, kv_dev)
    return [(kv_dev + count - 1 - place) // count for place in range(count)]


def exchanged(value, axis, low, high):
    count = lax.axis_size(axis)
    assert count & (count - 1) == 0
    return [
        lax.ppermute(value, axis, [(source, source ^ (mask << low)) for source in range(count)])
        for mask in range(1, 1 << max(high - low, 0))
    ]


def summed(value, axis, low, high):
    for place in range(low, high):
        value = value + exchanged(value, axis, place, place + 1)[0]
    return value


def per_device(query, key, value, grad_out, q_gain, k_gain):
    rows, heads, width = query.shape
    kv_dev = key.shape[1]
    group = heads // kv_dev
    count = lax.axis_size("seq")
    assert 2 * rows == WINDOW and rows % TILE == 0 and count % 2 == 0
    shard = lax.axis_index("seq")
    ahead = [(source, source + 2) for source in range(count - 2)]
    back = [(source + 2, source) for source in range(count - 2)]
    swap = [(source, source ^ 1) for source in range(count)]

    def by_head(array):
        split = array.reshape(rows, kv_dev, group, width)
        return jnp.transpose(split, (1, 0, 2, 3)).reshape(kv_dev, rows * group, width)

    sizes = group_sizes(kv_dev)
    starts = [sum(sizes[:place]) for place in range(len(sizes))]
    cuts = [(0, sizes[0])] + ([(sizes[0], kv_dev)] if len(sizes) > 1 else [])
    by_kind = lax.optimization_barrier([jnp.transpose(kind, (1, 0, 2)) for kind in (key, value)])
    owns = [jnp.stack([kind[low:high] for kind in by_kind]) for low, high in cuts]
    fars = [lax.ppermute(own, "seq", ahead) for own in owns]
    queries, grads = by_head(query), by_head(grad_out)
    scalar = shard.astype(jnp.int32).reshape(1)
    q_gain_2d, k_gain_2d = q_gain.reshape(1, width), k_gain.reshape(1, width)

    def split(d_own, d_near, d_far, raw):
        swapped = lax.ppermute(d_near, "seq", swap)
        relayed = small_call(relay_kernel, scalar, d_far, swapped)
        return relayed, (d_own, swapped, raw)

    def close(stays, returned):
        d_own, swapped, raw = stays
        return close_group(scalar, d_own, returned, swapped, raw, k_gain_2d)

    dq_parts, gains, kept, done = [], [], [], []
    grads_out = None
    for place, (first, size) in enumerate(zip(starts, sizes, strict=True)):
        if grads_out is not None:
            relayed, stays = split(*grads_out)
        if place < 2:
            own, far, start = owns[place], fars[place], cuts[place][0]
            if place:
                far, gains[0] = lax.optimization_barrier((far, gains[0]))
                gains[0] = later(far, gains[0])
                far, gains[0], relayed = lax.optimization_barrier((far, gains[0], relayed))
            else:
                far, queries, grads, *_ = lax.optimization_barrier(
                    (far, queries, grads, *owns[1:])
                )
            near = lax.ppermute(small_call(choose_kernel, scalar, far, own), "seq", swap)
        scalar_now = scalar
        if grads_out is not None:
            if kept:
                before, returned = kept.pop()
                scalar_now = later(returned, scalar)
                done.append(close(before, returned))
            near, relayed, scalar_now = lax.optimization_barrier((near, relayed, scalar_now))
            kept.append((stays, lax.ppermute(relayed, "seq", back)))
        here = slice(first - start, first - start + size)
        dq, *grads_out, gain = group_grads(
            scalar_now, first, first - start, size, queries, grads, own, near, far, q_gain_2d, k_gain_2d
        )
        grads_out.append(own[:1, here])
        dq_parts.append(dq)
        gains.append(gain)
    relayed, stays = split(*grads_out)
    gain_sum = sum(gains[1:], gains[0])
    if kept:
        before, returned = kept.pop()
        returned, done = lax.optimization_barrier((returned, done))
        gain_sum = later(returned, gain_sum)
        done.append(close(before, returned))
    returned = lax.ppermute(relayed, "seq", back)
    grad_query = jnp.concatenate(dq_parts).reshape(kv_dev, rows, group, width)
    grad_query = jnp.transpose(grad_query, (1, 0, 2, 3)).reshape(rows, heads, width)
    seq_bits, head_bits = ((lax.axis_size(axis) - 1).bit_length() for axis in ("seq", "head"))
    gain_sum = summed(gain_sum, "seq", 0, 1)
    gain_sum = summed(gain_sum, "head", 0, head_bits)
    gain_sum = summed(gain_sum, "seq", 1, seq_bits - 2)
    gain_sum, grad_query, done = lax.optimization_barrier((gain_sum, grad_query, done))
    d_own, swapped, raw = stays
    grad_key, grad_value = finish(scalar, d_own, returned, swapped, raw, k_gain_2d, done)
    others, grad_key = lax.optimization_barrier(
        (exchanged(gain_sum, "seq", max(seq_bits - 2, 1), seq_bits), grad_key)
    )
    gain_sum = (gain_sum + others[0]) + (others[1] + others[2]) if len(others) == 3 else sum(
        others, gain_sum
    )
    return (grad_query, grad_key, grad_value, gain_sum[0], gain_sum[1])


def solution(mesh):
    split, whole = P("seq", "head", None), P()
    return jax.shard_map(
        per_device,
        mesh=mesh,
        in_specs=(split, split, split, split, whole, whole),
        out_specs=(split, split, split, whole, whole),
        check_vma=False,
    )
```

```python
import functools

import jax
import jax.numpy as jnp
from jax import lax
from jax.experimental import pallas as pl
from jax.experimental.pallas import tpu as pltpu
from jax.sharding import PartitionSpec as P

WINDOW = 1024
TILE = 128

score_scale = 168.0 ** (-0.5)
norm_eps = 1e-06
exp2_scale = score_scale * 1.4426950408889634

GROUPS = 3
HEAVY = pl.CostEstimate(flops=10**11, bytes_accessed=10**8, transcendentals=0)
LIGHT = pl.CostEstimate(flops=1000, bytes_accessed=1000, transcendentals=0)

NT = (((1,), (1,)), ((), ()))


def inverse_rms_of(as_float):
    return lax.rsqrt(jnp.mean(as_float * as_float, axis=-1, keepdims=True) + norm_eps)


def norm_back(d_normed, raw, inverse_rms, gain_vec):
    unit_rows = raw * inverse_rms
    d_unit = d_normed * gain_vec
    return inverse_rms * (
        d_unit - unit_rows * jnp.mean(d_unit * unit_rows, axis=-1, keepdims=True)
    )


def by_sublane(tile):
    return jnp.sum(tile.reshape(-1, 8, tile.shape[1]), axis=0)


def heads_kernel(
    shard_ref, q_ref, g_ref, own_ref, near_ref, far_ref, q_gain_ref, k_gain_ref,
    dq_ref, d_own_ref, d_near_ref, d_far_ref, gains_ref,
    k_low, k_low_t, k_rms, values, q_low, q_rms, g_low, exps, d_scores, d_probs_held,
):
    rows = own_ref.shape[2]
    group = q_ref.shape[1] // rows
    lanes = TILE * group
    blocks = rows // TILE
    tiles = WINDOW // TILE
    q_gain, k_gain = q_gain_ref[...], k_gain_ref[...]
    far_ok = jnp.where(shard_ref[0] >= 2, 1.0, 0.0)
    near_ok = jnp.where(shard_ref[0] >= 1, 1.0, 0.0)
    key_refs = (far_ref, near_ref, own_ref)

    @pl.when(pl.program_id(0) == 0)
    def _():
        gains_ref[...] = jnp.zeros_like(gains_ref)

    for place, ref in enumerate(key_refs):
        raw = ref[0, 0].astype(jnp.float32)
        here = slice(place * rows, (place + 1) * rows)
        inverse_rms = jnp.broadcast_to(inverse_rms_of(raw), raw.shape)
        k_rms[here, :] = inverse_rms
        k_low[here, :] = (raw * inverse_rms * k_gain).astype(jnp.bfloat16)
        values[here, :] = ref[1, 0]
    k_low_t[...] = k_low[...].T
    raw_q = q_ref[0].astype(jnp.float32)
    inverse_rms = jnp.broadcast_to(inverse_rms_of(raw_q), raw_q.shape)
    q_rms[...] = inverse_rms
    q_low[...] = (raw_q * inverse_rms * q_gain).astype(jnp.bfloat16)

    key_ids = lax.broadcasted_iota(jnp.int32, (TILE, lanes), 0)
    token_ids = lax.broadcasted_iota(jnp.int32, (TILE, lanes), 1) // group
    late = key_ids <= token_ids
    edge_ok = jnp.where(late, 1.0, far_ok)
    q_gain_sum = jnp.zeros_like(q_gain)

    for block in range(blocks):
        start = block * TILE
        span = slice(start, start + WINDOW + TILE)
        mine = slice(block * lanes, (block + 1) * lanes)
        scores = lax.dot_general(
            k_low[span, :], q_low[mine, :], NT, preferred_element_type=jnp.float32
        )
        edge = jnp.where(late, scores[WINDOW:], scores[:TILE])
        edge = jnp.exp2(edge * exp2_scale) * edge_ok
        exps[start : start + TILE, mine] = jnp.where(late, 0.0, edge).astype(jnp.bfloat16)
        exps[start + WINDOW : start + WINDOW + TILE, mine] = jnp.where(late, edge, 0.0).astype(
            jnp.bfloat16
        )
        totals = {"own": by_sublane(edge)}
        for tile in range(1, tiles):
            part = jnp.exp2(scores[tile * TILE : (tile + 1) * TILE] * exp2_scale)
            at = start + tile * TILE
            exps[at : at + TILE, mine] = part.astype(jnp.bfloat16)
            place = ("far", "near", "own")[min(at // rows, 2)]
            part = by_sublane(part)
            totals[place] = totals[place] + part if place in totals else part
        total = totals["own"]
        if "far" in totals:
            total = total + totals["far"] * far_ok
        if "near" in totals:
            total = total + totals["near"] * near_ok
        inverse = 1.0 / jnp.sum(total, axis=0, keepdims=True)
        scaled_t = (g_ref[0, mine, :].astype(jnp.float32).T * inverse).astype(jnp.bfloat16)
        g_low[mine, :] = scaled_t.T
        d_probs = jnp.dot(values[span, :], scaled_t, preferred_element_type=jnp.float32)
        offset = None
        for tile in range(tiles + 1):
            at = start + tile * TILE
            part = d_probs[tile * TILE : (tile + 1) * TILE]
            d_probs_held[tile * TILE : (tile + 1) * TILE, :] = part
            part = by_sublane(exps[at : at + TILE, mine].astype(jnp.float32) * part)
            offset = part if offset is None else offset + part
        offset = inverse * jnp.sum(offset, axis=0, keepdims=True)
        for tile in range(tiles + 1):
            at = start + tile * TILE
            part = d_probs_held[tile * TILE : (tile + 1) * TILE, :] - offset
            part = exps[at : at + TILE, mine].astype(jnp.float32) * part
            d_scores[at : at + TILE, mine] = part.astype(jnp.bfloat16)
        query_grad = score_scale * jnp.dot(
            k_low_t[:, span], d_scores[span, mine], preferred_element_type=jnp.float32
        ).T
        raw = q_ref[0, mine, :].astype(jnp.float32)
        inverse_rms = q_rms[mine, :]
        q_gain_sum = q_gain_sum + jnp.sum(query_grad * (raw * inverse_rms), axis=0, keepdims=True)
        dq_ref[0, mine, :] = norm_back(query_grad, raw, inverse_rms, q_gain).astype(dq_ref.dtype)

    pieces = [(tile, tile + 1, 0, tile + 1) for tile in range(blocks - 1)]
    pieces += [(blocks - 1, tiles + 1, 0, blocks)]
    pieces += [(tiles + block, tiles + block + 1, block, blocks) for block in range(1, blocks)]
    k_gain_sum = jnp.zeros_like(k_gain)
    for first, last, low, high in pieces:
        meets = slice(low * lanes, high * lanes)
        keys = slice(first * TILE, last * TILE)
        value_grad = jnp.dot(
            exps[keys, meets], g_low[meets, :], preferred_element_type=jnp.float32
        )
        key_grad = score_scale * jnp.dot(
            d_scores[keys, meets], q_low[meets, :], preferred_element_type=jnp.float32
        )
        for place, (ref, out) in enumerate(
            zip(key_refs, (d_far_ref, d_near_ref, d_own_ref), strict=True)
        ):
            start = max(first * TILE, place * rows)
            stop = min(last * TILE, (place + 1) * rows)
            if start >= stop:
                continue
            inside = slice(start - place * rows, stop - place * rows)
            here = slice(start - first * TILE, stop - first * TILE)
            unit = ref[0, 0, inside, :].astype(jnp.float32) * k_rms[start:stop, :]
            k_gain_sum = k_gain_sum + jnp.sum(key_grad[here] * unit, axis=0, keepdims=True)
            out[0, 0, inside, :] = key_grad[here].astype(out.dtype)
            out[1, 0, inside, :] = value_grad[here].astype(out.dtype)
    gains_ref[0:1, :] += q_gain_sum
    gains_ref[1:2, :] += k_gain_sum


def closed(shard_ref, own, returned, swapped, kind, head):
    keep = jnp.where(shard_ref[0] % 2 == 1, 0.0, 1.0)
    own, returned, swapped = (
        part[kind, head].astype(jnp.float32) for part in (own, returned, swapped)
    )
    return own + returned + keep * swapped


def close_kernel(shard_ref, own, returned, swapped, raw_ref, k_gain_ref, out):
    for head in range(own.shape[1]):
        grad = closed(shard_ref, own, returned, swapped, 0, head)
        raw = raw_ref[0, head].astype(jnp.float32)
        grad = norm_back(grad, raw, inverse_rms_of(raw), k_gain_ref[...])
        out[0, head] = grad.astype(out.dtype)
        out[1, head] = closed(shard_ref, own, returned, swapped, 1, head).astype(out.dtype)


def finish_kernel(shard_ref, own, returned, swapped, raw_ref, k_gain_ref, *rest):
    *done, key_out, value_out, by_token = rest
    rows, heads, _ = key_out.shape
    before = [(part, head) for part in done for head in range(part.shape[1])]
    for kind, out in ((0, key_out), (1, value_out)):
        for place, (part, head) in enumerate(before):
            by_token[pl.ds(place, rows, stride=heads), :] = part[kind, head].astype(jnp.float32)
        for head in range(own.shape[1]):
            grad = closed(shard_ref, own, returned, swapped, kind, head)
            if kind == 0:
                raw = raw_ref[0, head].astype(jnp.float32)
                grad = norm_back(grad, raw, inverse_rms_of(raw), k_gain_ref[...])
            by_token[pl.ds(len(before) + head, rows, stride=heads), :] = grad
        out[...] = by_token[...].reshape(out.shape).astype(out.dtype)


def choose_kernel(shard_ref, far_ref, own_ref, out_ref):
    odd = shard_ref[0] % 2 == 1

    @pl.when(odd)
    def _():
        out_ref[...] = far_ref[...]

    @pl.when(jnp.logical_not(odd))
    def _():
        out_ref[...] = own_ref[...]


def relay_kernel(shard_ref, far_ref, swapped_ref, out_ref):
    odd = jnp.where(shard_ref[0] % 2 == 1, 1.0, 0.0)
    total = far_ref[...].astype(jnp.float32) + odd * swapped_ref[...].astype(jnp.float32)
    out_ref[...] = total.astype(out_ref.dtype)


def small_call(kernel, shard, *arrays):
    smem, vmem = (pl.BlockSpec(memory_space=space) for space in (pltpu.SMEM, pltpu.VMEM))
    return pl.pallas_call(
        kernel,
        in_specs=[smem] + [vmem] * len(arrays),
        out_specs=vmem,
        out_shape=jax.ShapeDtypeStruct(arrays[0].shape, arrays[0].dtype),
        compiler_params=pltpu.CompilerParams(vmem_limit_bytes=12 * 1024 * 1024),
        cost_estimate=LIGHT,
    )(shard, *arrays)


def later_kernel(corner_ref, in_ref, out_ref):
    if len(in_ref.shape) == 1:
        out_ref[0] = in_ref[0]
    else:
        out_ref[...] = in_ref[...]


def later(array, small):
    vmem = pl.BlockSpec(memory_space=pltpu.VMEM)
    held = pl.BlockSpec(memory_space=pltpu.SMEM if small.ndim == 1 else pltpu.VMEM)
    return pl.pallas_call(
        later_kernel,
        in_specs=[vmem, held],
        out_specs=held,
        out_shape=jax.ShapeDtypeStruct(small.shape, small.dtype),
        compiler_params=pltpu.CompilerParams(vmem_limit_bytes=1024 * 1024),
        cost_estimate=HEAVY,
    )(array[0, 0, :16], small)


def group_grads(shard, first, here, count, queries, grads, own, near, far, q_gain, k_gain):
    _, _, rows, width = own.shape
    query_rows = queries.shape[1]
    span = WINDOW + rows
    whole_q = pl.BlockSpec((1, query_rows, width), lambda head: (first + head, 0, 0))
    part = pl.BlockSpec((2, 1, rows, width), lambda head: (0, head, 0, 0))
    held = pl.BlockSpec((2, 1, rows, width), lambda head: (0, here + head, 0, 0))
    gain = pl.BlockSpec((1, width), lambda head: (0, 0))
    shape = (2, count, rows, width)
    return pl.pallas_call(
        heads_kernel,
        grid=(count,),
        in_specs=[
            pl.BlockSpec(memory_space=pltpu.SMEM), whole_q, whole_q, held, held, held, gain, gain,
        ],
        out_specs=[
            pl.BlockSpec((1, query_rows, width), lambda head: (head, 0, 0)),
            part,
            part,
            part,
            pl.BlockSpec((2, width), lambda head: (0, 0)),
        ],
        out_shape=[
            jax.ShapeDtypeStruct((count, query_rows, width), jnp.bfloat16),
            jax.ShapeDtypeStruct(shape, jnp.bfloat16),
            jax.ShapeDtypeStruct(shape, jnp.bfloat16),
            jax.ShapeDtypeStruct(shape, jnp.bfloat16),
            jax.ShapeDtypeStruct((2, width), jnp.float32),
        ],
        scratch_shapes=[
            pltpu.VMEM((span, width), jnp.bfloat16),
            pltpu.VMEM((width, span), jnp.bfloat16),
            pltpu.VMEM((span, width), jnp.float32),
            pltpu.VMEM((span, width), jnp.bfloat16),
            pltpu.VMEM((query_rows, width), jnp.bfloat16),
            pltpu.VMEM((query_rows, width), jnp.float32),
            pltpu.VMEM((query_rows, width), jnp.bfloat16),
            pltpu.VMEM((span, query_rows), jnp.bfloat16),
            pltpu.VMEM((span, query_rows), jnp.bfloat16),
            pltpu.VMEM((WINDOW + TILE, TILE * query_rows // rows), jnp.float32),
        ],
        compiler_params=pltpu.CompilerParams(vmem_limit_bytes=22 * 1024 * 1024),
        cost_estimate=LIGHT,
    )(shard, queries, grads, own, near, far, q_gain, k_gain)


def close_group(shard, own, returned, swapped, raw, k_gain):
    smem, vmem = (pl.BlockSpec(memory_space=space) for space in (pltpu.SMEM, pltpu.VMEM))
    return pl.pallas_call(
        close_kernel,
        in_specs=[smem] + [vmem] * 5,
        out_specs=vmem,
        out_shape=jax.ShapeDtypeStruct(own.shape, jnp.bfloat16),
        compiler_params=pltpu.CompilerParams(vmem_limit_bytes=12 * 1024 * 1024),
        cost_estimate=LIGHT,
    )(shard, own, returned, swapped, raw, k_gain)


def finish(shard, own, returned, swapped, raw, k_gain, done):
    _, count, rows, width = own.shape
    kv_dev = count + sum(part.shape[1] for part in done)
    shape = (rows, kv_dev, width)
    smem, vmem = (pl.BlockSpec(memory_space=space) for space in (pltpu.SMEM, pltpu.VMEM))
    return pl.pallas_call(
        finish_kernel,
        in_specs=[smem] + [vmem] * (5 + len(done)),
        out_specs=[vmem, vmem],
        out_shape=[jax.ShapeDtypeStruct(shape, jnp.bfloat16)] * 2,
        scratch_shapes=[pltpu.VMEM((rows * kv_dev, width), jnp.float32)],
        compiler_params=pltpu.CompilerParams(vmem_limit_bytes=20 * 1024 * 1024),
    )(shard, own, returned, swapped, raw, k_gain, *done)


def group_sizes(kv_dev):
    count = min(GROUPS, kv_dev)
    return [(kv_dev + count - 1 - place) // count for place in range(count)]


def exchanged(value, axis, low, high):
    count = lax.axis_size(axis)
    assert count & (count - 1) == 0
    return [
        lax.ppermute(value, axis, [(source, source ^ (mask << low)) for source in range(count)])
        for mask in range(1, 1 << max(high - low, 0))
    ]


def summed(value, axis, low, high):
    for place in range(low, high):
        value = value + exchanged(value, axis, place, place + 1)[0]
    return value


def per_device(query, key, value, grad_out, q_gain, k_gain):
    rows, heads, width = query.shape
    kv_dev = key.shape[1]
    group = heads // kv_dev
    count = lax.axis_size("seq")
    assert 2 * rows == WINDOW and rows % TILE == 0 and count % 2 == 0
    shard = lax.axis_index("seq")
    ahead = [(source, source + 2) for source in range(count - 2)]
    back = [(source + 2, source) for source in range(count - 2)]
    swap = [(source, source ^ 1) for source in range(count)]

    def by_head(array):
        split = array.reshape(rows, kv_dev, group, width)
        return jnp.transpose(split, (1, 0, 2, 3)).reshape(kv_dev, rows * group, width)

    sizes = group_sizes(kv_dev)
    starts = [sum(sizes[:place]) for place in range(len(sizes))]
    cuts = [(0, sizes[0])] + ([(sizes[0], kv_dev)] if len(sizes) > 1 else [])
    by_kind = lax.optimization_barrier([jnp.transpose(kind, (1, 0, 2)) for kind in (key, value)])
    owns = [jnp.stack([kind[low:high] for kind in by_kind]) for low, high in cuts]
    fars = [lax.ppermute(own, "seq", ahead) for own in owns]
    queries, grads = by_head(query), by_head(grad_out)
    scalar = shard.astype(jnp.int32).reshape(1)
    q_gain_2d, k_gain_2d = q_gain.reshape(1, width), k_gain.reshape(1, width)

    def split(d_own, d_near, d_far, raw):
        swapped = lax.ppermute(d_near, "seq", swap)
        relayed = small_call(relay_kernel, scalar, d_far, swapped)
        return relayed, (d_own, swapped, raw)

    def close(stays, returned):
        d_own, swapped, raw = stays
        return close_group(scalar, d_own, returned, swapped, raw, k_gain_2d)

    dq_parts, gains, kept, done = [], [], [], []
    grads_out = None
    for place, (first, size) in enumerate(zip(starts, sizes, strict=True)):
        if grads_out is not None:
            relayed, stays = split(*grads_out)
        if place < 2:
            own, far, start = owns[place], fars[place], cuts[place][0]
            if place:
                far, gains[0] = lax.optimization_barrier((far, gains[0]))
                gains[0] = later(far, gains[0])
                far, gains[0], relayed = lax.optimization_barrier((far, gains[0], relayed))
            else:
                far, queries, grads, *_ = lax.optimization_barrier(
                    (far, queries, grads, *owns[1:])
                )
            near = lax.ppermute(small_call(choose_kernel, scalar, far, own), "seq", swap)
        scalar_now = scalar
        if grads_out is not None:
            if kept:
                before, returned = kept.pop()
                scalar_now = later(returned, scalar)
                done.append(close(before, returned))
            near, relayed, scalar_now = lax.optimization_barrier((near, relayed, scalar_now))
            kept.append((stays, lax.ppermute(relayed, "seq", back)))
        here = slice(first - start, first - start + size)
        dq, *grads_out, gain = group_grads(
            scalar_now, first, first - start, size, queries, grads, own, near, far, q_gain_2d, k_gain_2d
        )
        grads_out.append(own[:1, here])
        dq_parts.append(dq)
        gains.append(gain)
    relayed, stays = split(*grads_out)
    gain_sum = sum(gains[1:], gains[0])
    if kept:
        before, returned = kept.pop()
        returned, done = lax.optimization_barrier((returned, done))
        gain_sum = later(returned, gain_sum)
        done.append(close(before, returned))
    returned = lax.ppermute(relayed, "seq", back)
    grad_query = jnp.concatenate(dq_parts).reshape(kv_dev, rows, group, width)
    grad_query = jnp.transpose(grad_query, (1, 0, 2, 3)).reshape(rows, heads, width)
    seq_bits, head_bits = ((lax.axis_size(axis) - 1).bit_length() for axis in ("seq", "head"))
    gain_sum = summed(gain_sum, "seq", 0, 1)
    gain_sum = summed(gain_sum, "head", 0, head_bits)
    gain_sum = summed(gain_sum, "seq", 1, seq_bits - 2)
    gain_sum, grad_query, done = lax.optimization_barrier((gain_sum, grad_query, done))
    d_own, swapped, raw = stays
    grad_key, grad_value = finish(scalar, d_own, returned, swapped, raw, k_gain_2d, done)
    others, grad_key = lax.optimization_barrier(
        (exchanged(gain_sum, "seq", max(seq_bits - 2, 1), seq_bits), grad_key)
    )
    gain_sum = (gain_sum + others[0]) + (others[1] + others[2]) if len(others) == 3 else sum(
        others, gain_sum
    )
    return (grad_query, grad_key, grad_value, gain_sum[0], gain_sum[1])


def solution(mesh):
    split, whole = P("seq", "head", None), P()
    return jax.shard_map(
        per_device,
        mesh=mesh,
        in_specs=(split, split, split, split, whole, whole),
        out_specs=(split, split, split, whole, whole),
        check_vma=False,
    )
```

```python
import functools

import jax
import jax.numpy as jnp
from jax import lax
from jax.experimental import pallas as pl
from jax.experimental.pallas import tpu as pltpu
from jax.sharding import PartitionSpec as P

WINDOW = 1024
TILE = 256

score_scale = 168.0 ** (-0.5)
norm_eps = 1e-06
exp2_scale = score_scale * 1.4426950408889634

GROUPS = 3
HEAVY = pl.CostEstimate(flops=10**11, bytes_accessed=10**8, transcendentals=0)
LIGHT = pl.CostEstimate(flops=1000, bytes_accessed=1000, transcendentals=0)

NT = (((1,), (1,)), ((), ()))


def inverse_rms_of(as_float):
    return lax.rsqrt(jnp.mean(as_float * as_float, axis=-1, keepdims=True) + norm_eps)


def norm_back(d_normed, raw, inverse_rms, gain_vec):
    unit_rows = raw * inverse_rms
    d_unit = d_normed * gain_vec
    return inverse_rms * (
        d_unit - unit_rows * jnp.mean(d_unit * unit_rows, axis=-1, keepdims=True)
    )


def heads_kernel(
    shard_ref, q_ref, g_ref, own_ref, near_ref, far_ref, q_gain_ref, k_gain_ref,
    dq_ref, d_own_ref, d_near_ref, d_far_ref, gains_ref,
    k_low, k_low_t, k_rms, values, q_low, q_rms, probs_all, d_scores_all,
):
    rows = own_ref.shape[2]
    group = q_ref.shape[1] // rows
    lanes = TILE * group
    blocks = rows // TILE
    tiles = WINDOW // TILE
    q_gain, k_gain = q_gain_ref[...], k_gain_ref[...]
    far_ok = jnp.where(shard_ref[0] >= 2, 1.0, 0.0)
    near_ok = jnp.where(shard_ref[0] >= 1, 1.0, 0.0)
    key_refs = (far_ref, near_ref, own_ref)

    @pl.when(pl.program_id(0) == 0)
    def _():
        gains_ref[...] = jnp.zeros_like(gains_ref)

    for place, ref in enumerate(key_refs):
        raw = ref[0, 0].astype(jnp.float32)
        here = slice(place * rows, (place + 1) * rows)
        inverse_rms = jnp.broadcast_to(inverse_rms_of(raw), raw.shape)
        k_rms[here, :] = inverse_rms
        k_low[here, :] = (raw * inverse_rms * k_gain).astype(jnp.bfloat16)
        values[here, :] = ref[1, 0]
    k_low_t[...] = k_low[...].T
    raw_q = q_ref[0].astype(jnp.float32)
    inverse_rms = jnp.broadcast_to(inverse_rms_of(raw_q), raw_q.shape)
    q_rms[...] = inverse_rms
    q_low[...] = (raw_q * inverse_rms * q_gain).astype(jnp.bfloat16)

    key_ids = lax.broadcasted_iota(jnp.int32, (TILE, lanes), 0)
    token_ids = lax.broadcasted_iota(jnp.int32, (TILE, lanes), 1) // group
    late = key_ids <= token_ids
    edge_ok = jnp.where(late, 1.0, far_ok)
    q_gain_sum = jnp.zeros_like(q_gain)

    for block in range(blocks):
        span = slice(block * TILE, block * TILE + WINDOW + TILE)
        mine = slice(block * lanes, (block + 1) * lanes)
        scores = lax.dot_general(
            k_low[span, :], q_low[mine, :], NT, preferred_element_type=jnp.float32
        )
        scores = jnp.concatenate(
            [jnp.where(late, scores[WINDOW:], scores[:TILE]), scores[TILE:WINDOW]], axis=0
        )
        exp_scores = jnp.exp2(scores * exp2_scale)
        edge = exp_scores[:TILE] * edge_ok
        first_near = (blocks - block) * TILE
        first_own = first_near + rows
        total = jnp.sum(edge, axis=0, keepdims=True)
        for low, high, ok in (
            (TILE, first_near, far_ok),
            (first_near, min(first_own, WINDOW), near_ok),
            (first_own, WINDOW, None),
        ):
            if low < high:
                part = jnp.sum(exp_scores[low:high], axis=0, keepdims=True)
                total = total + (part if ok is None else part * ok)
        inverse = 1.0 / total
        probs = jnp.concatenate([edge, exp_scores[TILE:]], axis=0) * inverse
        d_probs = lax.dot_general(
            values[span, :], g_ref[0, mine, :], NT, preferred_element_type=jnp.float32
        )
        d_probs = jnp.concatenate(
            [jnp.where(late, d_probs[WINDOW:], d_probs[:TILE]), d_probs[TILE:WINDOW]], axis=0
        )
        offset = jnp.sum(probs * d_probs, axis=0, keepdims=True)
        d_scores = probs * (d_probs - offset)
        for whole, held in ((probs, probs_all), (d_scores, d_scores_all)):
            start = block * TILE
            held[start : start + TILE, mine] = jnp.where(late, 0.0, whole[:TILE]).astype(
                jnp.bfloat16
            )
            held[start + TILE : start + WINDOW, mine] = whole[TILE:].astype(jnp.bfloat16)
            held[start + WINDOW : start + WINDOW + TILE, mine] = jnp.where(
                late, whole[:TILE], 0.0
            ).astype(jnp.bfloat16)
        query_grad = score_scale * jnp.dot(
            k_low_t[:, span], d_scores_all[span, mine], preferred_element_type=jnp.float32
        ).T
        raw = q_ref[0, mine, :].astype(jnp.float32)
        inverse_rms = q_rms[mine, :]
        q_gain_sum = q_gain_sum + jnp.sum(query_grad * (raw * inverse_rms), axis=0, keepdims=True)
        dq_ref[0, mine, :] = norm_back(query_grad, raw, inverse_rms, q_gain).astype(dq_ref.dtype)

    pieces = [(tile, tile + 1, 0, tile + 1) for tile in range(blocks - 1)]
    pieces += [(blocks - 1, tiles + 1, 0, blocks)]
    pieces += [(tiles + block, tiles + block + 1, block, blocks) for block in range(1, blocks)]
    k_gain_sum = jnp.zeros_like(k_gain)
    for first, last, low, high in pieces:
        meets = slice(low * lanes, high * lanes)
        keys = slice(first * TILE, last * TILE)
        value_grad = jnp.dot(
            probs_all[keys, meets], g_ref[0, meets, :], preferred_element_type=jnp.float32
        )
        key_grad = score_scale * jnp.dot(
            d_scores_all[keys, meets], q_low[meets, :], preferred_element_type=jnp.float32
        )
        for place, (ref, out) in enumerate(
            zip(key_refs, (d_far_ref, d_near_ref, d_own_ref), strict=True)
        ):
            start = max(first * TILE, place * rows)
            stop = min(last * TILE, (place + 1) * rows)
            if start >= stop:
                continue
            inside = slice(start - place * rows, stop - place * rows)
            here = slice(start - first * TILE, stop - first * TILE)
            unit = ref[0, 0, inside, :].astype(jnp.float32) * k_rms[start:stop, :]
            k_gain_sum = k_gain_sum + jnp.sum(key_grad[here] * unit, axis=0, keepdims=True)
            out[0, 0, inside, :] = key_grad[here].astype(out.dtype)
            out[1, 0, inside, :] = value_grad[here].astype(out.dtype)
    gains_ref[0:1, :] += q_gain_sum
    gains_ref[1:2, :] += k_gain_sum


def closed(shard_ref, own, returned, swapped, kind, head):
    keep = jnp.where(shard_ref[0] % 2 == 1, 0.0, 1.0)
    own, returned, swapped = (
        part[kind, head].astype(jnp.float32) for part in (own, returned, swapped)
    )
    return own + returned + keep * swapped


def close_kernel(shard_ref, own, returned, swapped, raw_ref, k_gain_ref, out):
    for head in range(own.shape[1]):
        grad = closed(shard_ref, own, returned, swapped, 0, head)
        raw = raw_ref[0, head].astype(jnp.float32)
        grad = norm_back(grad, raw, inverse_rms_of(raw), k_gain_ref[...])
        out[0, head] = grad.astype(out.dtype)
        out[1, head] = closed(shard_ref, own, returned, swapped, 1, head).astype(out.dtype)


def finish_kernel(shard_ref, own, returned, swapped, raw_ref, k_gain_ref, *rest):
    *done, key_out, value_out, by_token = rest
    rows, heads, _ = key_out.shape
    before = [(part, head) for part in done for head in range(part.shape[1])]
    for kind, out in ((0, key_out), (1, value_out)):
        for place, (part, head) in enumerate(before):
            by_token[pl.ds(place, rows, stride=heads), :] = part[kind, head].astype(jnp.float32)
        for head in range(own.shape[1]):
            grad = closed(shard_ref, own, returned, swapped, kind, head)
            if kind == 0:
                raw = raw_ref[0, head].astype(jnp.float32)
                grad = norm_back(grad, raw, inverse_rms_of(raw), k_gain_ref[...])
            by_token[pl.ds(len(before) + head, rows, stride=heads), :] = grad
        out[...] = by_token[...].reshape(out.shape).astype(out.dtype)


def choose_kernel(shard_ref, far_ref, own_ref, out_ref):
    odd = shard_ref[0] % 2 == 1

    @pl.when(odd)
    def _():
        out_ref[...] = far_ref[...]

    @pl.when(jnp.logical_not(odd))
    def _():
        out_ref[...] = own_ref[...]


def relay_kernel(shard_ref, far_ref, swapped_ref, out_ref):
    odd = jnp.where(shard_ref[0] % 2 == 1, 1.0, 0.0)
    total = far_ref[...].astype(jnp.float32) + odd * swapped_ref[...].astype(jnp.float32)
    out_ref[...] = total.astype(out_ref.dtype)


def small_call(kernel, shard, *arrays):
    smem, vmem = (pl.BlockSpec(memory_space=space) for space in (pltpu.SMEM, pltpu.VMEM))
    return pl.pallas_call(
        kernel,
        in_specs=[smem] + [vmem] * len(arrays),
        out_specs=vmem,
        out_shape=jax.ShapeDtypeStruct(arrays[0].shape, arrays[0].dtype),
        compiler_params=pltpu.CompilerParams(vmem_limit_bytes=12 * 1024 * 1024),
        cost_estimate=LIGHT,
    )(shard, *arrays)


def later_kernel(corner_ref, in_ref, out_ref):
    if len(in_ref.shape) == 1:
        out_ref[0] = in_ref[0]
    else:
        out_ref[...] = in_ref[...]


def later(array, small):
    vmem = pl.BlockSpec(memory_space=pltpu.VMEM)
    held = pl.BlockSpec(memory_space=pltpu.SMEM if small.ndim == 1 else pltpu.VMEM)
    return pl.pallas_call(
        later_kernel,
        in_specs=[vmem, held],
        out_specs=held,
        out_shape=jax.ShapeDtypeStruct(small.shape, small.dtype),
        compiler_params=pltpu.CompilerParams(vmem_limit_bytes=1024 * 1024),
        cost_estimate=HEAVY,
    )(array[0, 0, :16], small)


def group_grads(shard, first, here, count, queries, grads, own, near, far, q_gain, k_gain):
    _, _, rows, width = own.shape
    query_rows = queries.shape[1]
    span = WINDOW + rows
    whole_q = pl.BlockSpec((1, query_rows, width), lambda head: (first + head, 0, 0))
    part = pl.BlockSpec((2, 1, rows, width), lambda head: (0, head, 0, 0))
    held = pl.BlockSpec((2, 1, rows, width), lambda head: (0, here + head, 0, 0))
    gain = pl.BlockSpec((1, width), lambda head: (0, 0))
    shape = (2, count, rows, width)
    return pl.pallas_call(
        heads_kernel,
        grid=(count,),
        in_specs=[
            pl.BlockSpec(memory_space=pltpu.SMEM), whole_q, whole_q, held, held, held, gain, gain,
        ],
        out_specs=[
            pl.BlockSpec((1, query_rows, width), lambda head: (head, 0, 0)),
            part,
            part,
            part,
            pl.BlockSpec((2, width), lambda head: (0, 0)),
        ],
        out_shape=[
            jax.ShapeDtypeStruct((count, query_rows, width), jnp.bfloat16),
            jax.ShapeDtypeStruct(shape, jnp.bfloat16),
            jax.ShapeDtypeStruct(shape, jnp.bfloat16),
            jax.ShapeDtypeStruct(shape, jnp.bfloat16),
            jax.ShapeDtypeStruct((2, width), jnp.float32),
        ],
        scratch_shapes=[
            pltpu.VMEM((span, width), jnp.bfloat16),
            pltpu.VMEM((width, span), jnp.bfloat16),
            pltpu.VMEM((span, width), jnp.float32),
            pltpu.VMEM((span, width), jnp.bfloat16),
            pltpu.VMEM((query_rows, width), jnp.bfloat16),
            pltpu.VMEM((query_rows, width), jnp.float32),
            pltpu.VMEM((span, query_rows), jnp.bfloat16),
            pltpu.VMEM((span, query_rows), jnp.bfloat16),
        ],
        compiler_params=pltpu.CompilerParams(vmem_limit_bytes=22 * 1024 * 1024),
        cost_estimate=LIGHT,
    )(shard, queries, grads, own, near, far, q_gain, k_gain)


def close_group(shard, own, returned, swapped, raw, k_gain):
    smem, vmem = (pl.BlockSpec(memory_space=space) for space in (pltpu.SMEM, pltpu.VMEM))
    return pl.pallas_call(
        close_kernel,
        in_specs=[smem] + [vmem] * 5,
        out_specs=vmem,
        out_shape=jax.ShapeDtypeStruct(own.shape, jnp.bfloat16),
        compiler_params=pltpu.CompilerParams(vmem_limit_bytes=12 * 1024 * 1024),
        cost_estimate=LIGHT,
    )(shard, own, returned, swapped, raw, k_gain)


def finish(shard, own, returned, swapped, raw, k_gain, done):
    _, count, rows, width = own.shape
    kv_dev = count + sum(part.shape[1] for part in done)
    shape = (rows, kv_dev, width)
    smem, vmem = (pl.BlockSpec(memory_space=space) for space in (pltpu.SMEM, pltpu.VMEM))
    return pl.pallas_call(
        finish_kernel,
        in_specs=[smem] + [vmem] * (5 + len(done)),
        out_specs=[vmem, vmem],
        out_shape=[jax.ShapeDtypeStruct(shape, jnp.bfloat16)] * 2,
        scratch_shapes=[pltpu.VMEM((rows * kv_dev, width), jnp.float32)],
        compiler_params=pltpu.CompilerParams(vmem_limit_bytes=20 * 1024 * 1024),
    )(shard, own, returned, swapped, raw, k_gain, *done)


def group_sizes(kv_dev):
    count = min(GROUPS, kv_dev)
    return [(kv_dev + count - 1 - place) // count for place in range(count)]


def exchanged(value, axis, low, high):
    count = lax.axis_size(axis)
    assert count & (count - 1) == 0
    return [
        lax.ppermute(value, axis, [(source, source ^ (mask << low)) for source in range(count)])
        for mask in range(1, 1 << max(high - low, 0))
    ]


def summed(value, axis, low, high):
    for place in range(low, high):
        value = value + exchanged(value, axis, place, place + 1)[0]
    return value


def per_device(query, key, value, grad_out, q_gain, k_gain):
    rows, heads, width = query.shape
    kv_dev = key.shape[1]
    group = heads // kv_dev
    count = lax.axis_size("seq")
    assert 2 * rows == WINDOW and rows % TILE == 0 and count % 2 == 0
    shard = lax.axis_index("seq")
    ahead = [(source, source + 2) for source in range(count - 2)]
    back = [(source + 2, source) for source in range(count - 2)]
    swap = [(source, source ^ 1) for source in range(count)]

    def by_head(array):
        split = array.reshape(rows, kv_dev, group, width)
        return jnp.transpose(split, (1, 0, 2, 3)).reshape(kv_dev, rows * group, width)

    sizes = group_sizes(kv_dev)
    starts = [sum(sizes[:place]) for place in range(len(sizes))]
    cuts = [(0, sizes[0])] + ([(sizes[0], kv_dev)] if len(sizes) > 1 else [])
    by_kind = lax.optimization_barrier([jnp.transpose(kind, (1, 0, 2)) for kind in (key, value)])
    owns = [jnp.stack([kind[low:high] for kind in by_kind]) for low, high in cuts]
    fars = [lax.ppermute(own, "seq", ahead) for own in owns]
    queries, grads = by_head(query), by_head(grad_out)
    scalar = shard.astype(jnp.int32).reshape(1)
    q_gain_2d, k_gain_2d = q_gain.reshape(1, width), k_gain.reshape(1, width)

    def split(d_own, d_near, d_far, raw):
        swapped = lax.ppermute(d_near, "seq", swap)
        relayed = small_call(relay_kernel, scalar, d_far, swapped)
        return relayed, (d_own, swapped, raw)

    def close(stays, returned):
        d_own, swapped, raw = stays
        return close_group(scalar, d_own, returned, swapped, raw, k_gain_2d)

    dq_parts, gains, kept, done = [], [], [], []
    grads_out = None
    for place, (first, size) in enumerate(zip(starts, sizes, strict=True)):
        if grads_out is not None:
            relayed, stays = split(*grads_out)
        if place < 2:
            own, far, start = owns[place], fars[place], cuts[place][0]
            if place:
                far, gains[0] = lax.optimization_barrier((far, gains[0]))
                gains[0] = later(far, gains[0])
                far, gains[0], relayed = lax.optimization_barrier((far, gains[0], relayed))
            else:
                far, queries, grads, *_ = lax.optimization_barrier(
                    (far, queries, grads, *owns[1:])
                )
            near = lax.ppermute(small_call(choose_kernel, scalar, far, own), "seq", swap)
        scalar_now = scalar
        if grads_out is not None:
            if kept:
                before, returned = kept.pop()
                scalar_now = later(returned, scalar)
                done.append(close(before, returned))
            near, relayed, scalar_now = lax.optimization_barrier((near, relayed, scalar_now))
            kept.append((stays, lax.ppermute(relayed, "seq", back)))
        here = slice(first - start, first - start + size)
        dq, *grads_out, gain = group_grads(
            scalar_now, first, first - start, size, queries, grads, own, near, far, q_gain_2d, k_gain_2d
        )
        grads_out.append(own[:1, here])
        dq_parts.append(dq)
        gains.append(gain)
    relayed, stays = split(*grads_out)
    gain_sum = sum(gains[1:], gains[0])
    if kept:
        before, returned = kept.pop()
        returned, done = lax.optimization_barrier((returned, done))
        gain_sum = later(returned, gain_sum)
        done.append(close(before, returned))
    returned = lax.ppermute(relayed, "seq", back)
    grad_query = jnp.concatenate(dq_parts).reshape(kv_dev, rows, group, width)
    grad_query = jnp.transpose(grad_query, (1, 0, 2, 3)).reshape(rows, heads, width)
    seq_bits, head_bits = ((lax.axis_size(axis) - 1).bit_length() for axis in ("seq", "head"))
    gain_sum = summed(gain_sum, "seq", 0, 1)
    gain_sum = summed(gain_sum, "head", 0, head_bits)
    gain_sum = summed(gain_sum, "seq", 1, seq_bits - 2)
    gain_sum, grad_query, done = lax.optimization_barrier((gain_sum, grad_query, done))
    d_own, swapped, raw = stays
    grad_key, grad_value = finish(scalar, d_own, returned, swapped, raw, k_gain_2d, done)
    others, grad_key = lax.optimization_barrier(
        (exchanged(gain_sum, "seq", max(seq_bits - 2, 1), seq_bits), grad_key)
    )
    gain_sum = (gain_sum + others[0]) + (others[1] + others[2]) if len(others) == 3 else sum(
        others, gain_sum
    )
    return (grad_query, grad_key, grad_value, gain_sum[0], gain_sum[1])


def solution(mesh):
    split, whole = P("seq", "head", None), P()
    return jax.shard_map(
        per_device,
        mesh=mesh,
        in_specs=(split, split, split, split, whole, whole),
        out_specs=(split, split, split, whole, whole),
        check_vma=False,
    )
```

```python
import functools

import jax
import jax.numpy as jnp
from jax import lax
from jax.experimental import pallas as pl
from jax.experimental.pallas import tpu as pltpu
from jax.sharding import PartitionSpec as P

WINDOW = 1024
TILE = 256

score_scale = 168.0 ** (-0.5)
norm_eps = 1e-06
exp2_scale = score_scale * 1.4426950408889634

GROUPS = 3
HEAVY = pl.CostEstimate(flops=10**11, bytes_accessed=10**8, transcendentals=0)
LIGHT = pl.CostEstimate(flops=1000, bytes_accessed=1000, transcendentals=0)

NT = (((1,), (1,)), ((), ()))


def inverse_rms_of(as_float):
    return lax.rsqrt(jnp.mean(as_float * as_float, axis=-1, keepdims=True) + norm_eps)


def norm_back(d_normed, raw, inverse_rms, gain_vec):
    unit_rows = raw * inverse_rms
    d_unit = d_normed * gain_vec
    return inverse_rms * (
        d_unit - unit_rows * jnp.mean(d_unit * unit_rows, axis=-1, keepdims=True)
    )


def heads_kernel(
    shard_ref, q_ref, g_ref, own_ref, near_ref, far_ref, q_gain_ref, k_gain_ref, _,
    dq_ref, d_own_ref, d_near_ref, d_far_ref, gains_ref,
    k_low, k_low_t, k_rms, values, q_low, q_rms, probs_all, d_scores_all,
):
    rows = own_ref.shape[2]
    group = q_ref.shape[1] // rows
    lanes = TILE * group
    blocks = rows // TILE
    tiles = WINDOW // TILE
    q_gain, k_gain = q_gain_ref[...], k_gain_ref[...]
    far_ok = jnp.where(shard_ref[0] >= 2, 1.0, 0.0)
    near_ok = jnp.where(shard_ref[0] >= 1, 1.0, 0.0)
    key_refs = (far_ref, near_ref, own_ref)

    @pl.when(pl.program_id(0) == 0)
    def _():
        gains_ref[...] = jnp.zeros_like(gains_ref)

    for place, ref in enumerate(key_refs):
        raw = ref[0, 0].astype(jnp.float32)
        here = slice(place * rows, (place + 1) * rows)
        inverse_rms = jnp.broadcast_to(inverse_rms_of(raw), raw.shape)
        k_rms[here, :] = inverse_rms
        k_low[here, :] = (raw * inverse_rms * k_gain).astype(jnp.bfloat16)
        values[here, :] = ref[1, 0]
    k_low_t[...] = k_low[...].T
    raw_q = q_ref[0].astype(jnp.float32)
    inverse_rms = jnp.broadcast_to(inverse_rms_of(raw_q), raw_q.shape)
    q_rms[...] = inverse_rms
    q_low[...] = (raw_q * inverse_rms * q_gain).astype(jnp.bfloat16)

    key_ids = lax.broadcasted_iota(jnp.int32, (TILE, lanes), 0)
    token_ids = lax.broadcasted_iota(jnp.int32, (TILE, lanes), 1) // group
    late = key_ids <= token_ids
    edge_ok = jnp.where(late, 1.0, far_ok)
    q_gain_sum = jnp.zeros_like(q_gain)

    for block in range(blocks):
        span = slice(block * TILE, block * TILE + WINDOW + TILE)
        mine = slice(block * lanes, (block + 1) * lanes)
        scores = lax.dot_general(
            k_low[span, :], q_low[mine, :], NT, preferred_element_type=jnp.float32
        )
        scores = jnp.concatenate(
            [jnp.where(late, scores[WINDOW:], scores[:TILE]), scores[TILE:WINDOW]], axis=0
        )
        exp_scores = jnp.exp2(scores * exp2_scale)
        edge = exp_scores[:TILE] * edge_ok
        first_near = (blocks - block) * TILE
        first_own = first_near + rows
        total = jnp.sum(edge, axis=0, keepdims=True)
        for low, high, ok in (
            (TILE, first_near, far_ok),
            (first_near, min(first_own, WINDOW), near_ok),
            (first_own, WINDOW, None),
        ):
            if low < high:
                part = jnp.sum(exp_scores[low:high], axis=0, keepdims=True)
                total = total + (part if ok is None else part * ok)
        inverse = 1.0 / total
        probs = jnp.concatenate([edge, exp_scores[TILE:]], axis=0) * inverse
        d_probs = lax.dot_general(
            values[span, :], g_ref[0, mine, :], NT, preferred_element_type=jnp.float32
        )
        d_probs = jnp.concatenate(
            [jnp.where(late, d_probs[WINDOW:], d_probs[:TILE]), d_probs[TILE:WINDOW]], axis=0
        )
        offset = jnp.sum(probs * d_probs, axis=0, keepdims=True)
        d_scores = probs * (d_probs - offset)
        for whole, held in ((probs, probs_all), (d_scores, d_scores_all)):
            start = block * TILE
            held[start : start + TILE, mine] = jnp.where(late, 0.0, whole[:TILE]).astype(
                jnp.bfloat16
            )
            held[start + TILE : start + WINDOW, mine] = whole[TILE:].astype(jnp.bfloat16)
            held[start + WINDOW : start + WINDOW + TILE, mine] = jnp.where(
                late, whole[:TILE], 0.0
            ).astype(jnp.bfloat16)
        query_grad = score_scale * jnp.dot(
            k_low_t[:, span], d_scores_all[span, mine], preferred_element_type=jnp.float32
        ).T
        raw = q_ref[0, mine, :].astype(jnp.float32)
        inverse_rms = q_rms[mine, :]
        q_gain_sum = q_gain_sum + jnp.sum(query_grad * (raw * inverse_rms), axis=0, keepdims=True)
        query_grad = norm_back(query_grad, raw, inverse_rms, q_gain).astype(dq_ref.dtype)
        dq_ref[start : start + TILE, 0, :, :] = query_grad.reshape(TILE, group, -1)

    pieces = [(tile, tile + 1, 0, tile + 1) for tile in range(blocks - 1)]
    pieces += [(blocks - 1, tiles + 1, 0, blocks)]
    pieces += [(tiles + block, tiles + block + 1, block, blocks) for block in range(1, blocks)]
    k_gain_sum = jnp.zeros_like(k_gain)
    for first, last, low, high in pieces:
        meets = slice(low * lanes, high * lanes)
        keys = slice(first * TILE, last * TILE)
        value_grad = jnp.dot(
            probs_all[keys, meets], g_ref[0, meets, :], preferred_element_type=jnp.float32
        )
        key_grad = score_scale * jnp.dot(
            d_scores_all[keys, meets], q_low[meets, :], preferred_element_type=jnp.float32
        )
        for place, (ref, out) in enumerate(
            zip(key_refs, (d_far_ref, d_near_ref, d_own_ref), strict=True)
        ):
            start = max(first * TILE, place * rows)
            stop = min(last * TILE, (place + 1) * rows)
            if start >= stop:
                continue
            inside = slice(start - place * rows, stop - place * rows)
            here = slice(start - first * TILE, stop - first * TILE)
            unit = ref[0, 0, inside, :].astype(jnp.float32) * k_rms[start:stop, :]
            k_gain_sum = k_gain_sum + jnp.sum(key_grad[here] * unit, axis=0, keepdims=True)
            out[0, 0, inside, :] = key_grad[here].astype(out.dtype)
            out[1, 0, inside, :] = value_grad[here].astype(out.dtype)
    gains_ref[0:1, :] += q_gain_sum
    gains_ref[1:2, :] += k_gain_sum


def closed(shard_ref, own, returned, swapped, kind, head):
    keep = jnp.where(shard_ref[0] % 2 == 1, 0.0, 1.0)
    own, returned, swapped = (
        part[kind, head].astype(jnp.float32) for part in (own, returned, swapped)
    )
    return own + returned + keep * swapped


def close_kernel(shard_ref, own, returned, swapped, raw_ref, k_gain_ref, out):
    for head in range(own.shape[1]):
        grad = closed(shard_ref, own, returned, swapped, 0, head)
        raw = raw_ref[0, head].astype(jnp.float32)
        grad = norm_back(grad, raw, inverse_rms_of(raw), k_gain_ref[...])
        out[0, head] = grad.astype(out.dtype)
        out[1, head] = closed(shard_ref, own, returned, swapped, 1, head).astype(out.dtype)


def finish_kernel(shard_ref, own, returned, swapped, raw_ref, k_gain_ref, *rest):
    *done, key_out, value_out, by_token = rest
    rows, heads, _ = key_out.shape
    before = [(part, head) for part in done for head in range(part.shape[1])]
    for kind, out in ((0, key_out), (1, value_out)):
        for place, (part, head) in enumerate(before):
            by_token[pl.ds(place, rows, stride=heads), :] = part[kind, head].astype(jnp.float32)
        for head in range(own.shape[1]):
            grad = closed(shard_ref, own, returned, swapped, kind, head)
            if kind == 0:
                raw = raw_ref[0, head].astype(jnp.float32)
                grad = norm_back(grad, raw, inverse_rms_of(raw), k_gain_ref[...])
            by_token[pl.ds(len(before) + head, rows, stride=heads), :] = grad
        out[...] = by_token[...].reshape(out.shape).astype(out.dtype)


def choose_kernel(shard_ref, far_ref, own_ref, out_ref):
    odd = shard_ref[0] % 2 == 1

    @pl.when(odd)
    def _():
        out_ref[...] = far_ref[...]

    @pl.when(jnp.logical_not(odd))
    def _():
        out_ref[...] = own_ref[...]


def relay_kernel(shard_ref, far_ref, swapped_ref, out_ref):
    odd = jnp.where(shard_ref[0] % 2 == 1, 1.0, 0.0)
    total = far_ref[...].astype(jnp.float32) + odd * swapped_ref[...].astype(jnp.float32)
    out_ref[...] = total.astype(out_ref.dtype)


def small_call(kernel, shard, *arrays):
    smem, vmem = (pl.BlockSpec(memory_space=space) for space in (pltpu.SMEM, pltpu.VMEM))
    return pl.pallas_call(
        kernel,
        in_specs=[smem] + [vmem] * len(arrays),
        out_specs=vmem,
        out_shape=jax.ShapeDtypeStruct(arrays[0].shape, arrays[0].dtype),
        compiler_params=pltpu.CompilerParams(vmem_limit_bytes=12 * 1024 * 1024),
        cost_estimate=LIGHT,
    )(shard, *arrays)


def later_kernel(corner_ref, in_ref, out_ref):
    if len(in_ref.shape) == 1:
        out_ref[0] = in_ref[0]
    else:
        out_ref[...] = in_ref[...]


def later(array, small):
    vmem = pl.BlockSpec(memory_space=pltpu.VMEM)
    held = pl.BlockSpec(memory_space=pltpu.SMEM if small.ndim == 1 else pltpu.VMEM)
    return pl.pallas_call(
        later_kernel,
        in_specs=[vmem, held],
        out_specs=held,
        out_shape=jax.ShapeDtypeStruct(small.shape, small.dtype),
        compiler_params=pltpu.CompilerParams(vmem_limit_bytes=1024 * 1024),
        cost_estimate=HEAVY,
    )(array[0, 0, :16], small)


def group_grads(shard, first, here, count, queries, grads, own, near, far, q_gain, k_gain, dq):
    _, _, rows, width = own.shape
    query_rows = queries.shape[1]
    span = WINDOW + rows
    group = query_rows // rows
    whole_q = pl.BlockSpec((1, query_rows, width), lambda head: (first + head, 0, 0))
    part = pl.BlockSpec((2, 1, rows, width), lambda head: (0, head, 0, 0))
    held = pl.BlockSpec((2, 1, rows, width), lambda head: (0, here + head, 0, 0))
    gain = pl.BlockSpec((1, width), lambda head: (0, 0))
    shape = (2, count, rows, width)
    return pl.pallas_call(
        heads_kernel,
        grid=(count,),
        in_specs=[
            pl.BlockSpec(memory_space=pltpu.SMEM), whole_q, whole_q, held, held, held, gain, gain,
            pl.BlockSpec(memory_space=pl.ANY),
        ],
        out_specs=[
            pl.BlockSpec((rows, 1, group, width), lambda head: (0, first + head, 0, 0)),
            part,
            part,
            part,
            pl.BlockSpec((2, width), lambda head: (0, 0)),
        ],
        out_shape=[
            jax.ShapeDtypeStruct(dq.shape, dq.dtype),
            jax.ShapeDtypeStruct(shape, jnp.bfloat16),
            jax.ShapeDtypeStruct(shape, jnp.bfloat16),
            jax.ShapeDtypeStruct(shape, jnp.bfloat16),
            jax.ShapeDtypeStruct((2, width), jnp.float32),
        ],
        scratch_shapes=[
            pltpu.VMEM((span, width), jnp.bfloat16),
            pltpu.VMEM((width, span), jnp.bfloat16),
            pltpu.VMEM((span, width), jnp.float32),
            pltpu.VMEM((span, width), jnp.bfloat16),
            pltpu.VMEM((query_rows, width), jnp.bfloat16),
            pltpu.VMEM((query_rows, width), jnp.float32),
            pltpu.VMEM((span, query_rows), jnp.bfloat16),
            pltpu.VMEM((span, query_rows), jnp.bfloat16),
        ],
        input_output_aliases={8: 0},
        compiler_params=pltpu.CompilerParams(vmem_limit_bytes=22 * 1024 * 1024),
        cost_estimate=LIGHT,
    )(shard, queries, grads, own, near, far, q_gain, k_gain, dq)


def close_group(shard, own, returned, swapped, raw, k_gain):
    smem, vmem = (pl.BlockSpec(memory_space=space) for space in (pltpu.SMEM, pltpu.VMEM))
    return pl.pallas_call(
        close_kernel,
        in_specs=[smem] + [vmem] * 5,
        out_specs=vmem,
        out_shape=jax.ShapeDtypeStruct(own.shape, jnp.bfloat16),
        compiler_params=pltpu.CompilerParams(vmem_limit_bytes=12 * 1024 * 1024),
        cost_estimate=LIGHT,
    )(shard, own, returned, swapped, raw, k_gain)


def finish(shard, own, returned, swapped, raw, k_gain, done):
    _, count, rows, width = own.shape
    kv_dev = count + sum(part.shape[1] for part in done)
    shape = (rows, kv_dev, width)
    smem, vmem = (pl.BlockSpec(memory_space=space) for space in (pltpu.SMEM, pltpu.VMEM))
    return pl.pallas_call(
        finish_kernel,
        in_specs=[smem] + [vmem] * (5 + len(done)),
        out_specs=[vmem, vmem],
        out_shape=[jax.ShapeDtypeStruct(shape, jnp.bfloat16)] * 2,
        scratch_shapes=[pltpu.VMEM((rows * kv_dev, width), jnp.float32)],
        compiler_params=pltpu.CompilerParams(vmem_limit_bytes=20 * 1024 * 1024),
    )(shard, own, returned, swapped, raw, k_gain, *done)


def group_sizes(kv_dev):
    count = min(GROUPS, kv_dev)
    return [(kv_dev + count - 1 - place) // count for place in range(count)]


def exchanged(value, *bits):
    count = lax.axis_size(("seq", "head"))
    assert count & (count - 1) == 0
    masks = [1 << bit for bit in bits]
    masks += [sum(masks)] if len(masks) > 1 else []
    return [
        lax.ppermute(value, ("seq", "head"), [(source, source ^ mask) for source in range(count)])
        for mask in masks
    ]


def summed(value, others):
    return value + others[0] if len(others) == 1 else (value + others[0]) + (others[1] + others[2])


def per_device(query, key, value, grad_out, q_gain, k_gain):
    rows, heads, width = query.shape
    kv_dev = key.shape[1]
    group = heads // kv_dev
    count = lax.axis_size("seq")
    assert 2 * rows == WINDOW and rows % TILE == 0 and count % 2 == 0
    shard = lax.axis_index("seq")
    ahead = [(source, source + 2) for source in range(count - 2)]
    back = [(source + 2, source) for source in range(count - 2)]
    swap = [(source, source ^ 1) for source in range(count)]

    def by_head(array):
        split = array.reshape(rows, kv_dev, group, width)
        return jnp.transpose(split, (1, 0, 2, 3)).reshape(kv_dev, rows * group, width)

    sizes = group_sizes(kv_dev)
    starts = [sum(sizes[:place]) for place in range(len(sizes))]
    cuts = [(0, sizes[0])] + ([(sizes[0], kv_dev)] if len(sizes) > 1 else [])
    by_kind = lax.optimization_barrier([jnp.transpose(kind, (1, 0, 2)) for kind in (key, value)])
    owns = [jnp.stack([kind[low:high] for kind in by_kind]) for low, high in cuts]
    fars = [lax.ppermute(own, "seq", ahead) for own in owns]
    queries, grads = by_head(query), by_head(grad_out)
    scalar = shard.astype(jnp.int32).reshape(1)
    q_gain_2d, k_gain_2d = q_gain.reshape(1, width), k_gain.reshape(1, width)

    def split(d_own, d_near, d_far, raw):
        swapped = lax.ppermute(d_near, "seq", swap)
        relayed = small_call(relay_kernel, scalar, d_far, swapped)
        return relayed, (d_own, swapped, raw)

    def close(stays, returned):
        d_own, swapped, raw = stays
        return close_group(scalar, d_own, returned, swapped, raw, k_gain_2d)

    gains, kept, done = [], [], []
    grad_query = jnp.zeros((rows, kv_dev, group, width), query.dtype)
    grads_out = None
    for place, (first, size) in enumerate(zip(starts, sizes, strict=True)):
        if grads_out is not None:
            relayed, stays = split(*grads_out)
        if place < 2:
            own, far, start = owns[place], fars[place], cuts[place][0]
            if place:
                far, gains[0] = lax.optimization_barrier((far, gains[0]))
                gains[0] = later(far, gains[0])
                far, gains[0], relayed = lax.optimization_barrier((far, gains[0], relayed))
            else:
                far, queries, grads, *_ = lax.optimization_barrier(
                    (far, queries, grads, *owns[1:])
                )
            near = lax.ppermute(small_call(choose_kernel, scalar, far, own), "seq", swap)
        scalar_now = scalar
        if grads_out is not None:
            if kept:
                before, returned = kept.pop()
                scalar_now = later(returned, scalar)
                done.append(close(before, returned))
            near, relayed, scalar_now = lax.optimization_barrier((near, relayed, scalar_now))
            kept.append((stays, lax.ppermute(relayed, "seq", back)))
        here = slice(first - start, first - start + size)
        grad_query, *grads_out, gain = group_grads(
            scalar_now, first, first - start, size, queries, grads, own, near, far,
            q_gain_2d, k_gain_2d, grad_query,
        )
        grads_out.append(own[:1, here])
        gains.append(gain)
    relayed, stays = split(*grads_out)
    head_bits, seq_bits = ((lax.axis_size(axis) - 1).bit_length() for axis in ("head", "seq"))
    assert head_bits and seq_bits > 3
    chips = range(head_bits + 1, head_bits + seq_bits)
    gain_sum = sum(gains[1:], gains[0])
    others = exchanged(gain_sum, chips[0])
    if kept:
        before, returned = kept.pop()
        returned, done = lax.optimization_barrier((returned, done))
        gain_sum = later(returned, gain_sum)
        done.append(close(before, returned))
    gain_sum, others = lax.optimization_barrier((gain_sum, others))
    gain_sum = summed(gain_sum, others)
    returned = lax.ppermute(relayed, "seq", back)
    grad_query = grad_query.reshape(rows, heads, width)
    exchanges = [(0, head_bits), *((bit,) for bit in range(1, head_bits))]
    exchanges += [(bit,) for bit in chips[1:-2]]
    for bits in exchanges:
        gain_sum = summed(gain_sum, exchanged(gain_sum, *bits))
    gain_sum, grad_query, done = lax.optimization_barrier((gain_sum, grad_query, done))
    d_own, swapped, raw = stays
    grad_key, grad_value = finish(scalar, d_own, returned, swapped, raw, k_gain_2d, done)
    others, grad_key = lax.optimization_barrier((exchanged(gain_sum, *chips[-2:]), grad_key))
    gain_sum = summed(gain_sum, others)
    return (grad_query, grad_key, grad_value, gain_sum[0], gain_sum[1])


def solution(mesh):
    split, whole = P("seq", "head", None), P()
    return jax.shard_map(
        per_device,
        mesh=mesh,
        in_specs=(split, split, split, split, whole, whole),
        out_specs=(split, split, split, whole, whole),
        check_vma=False,
    )
```

```python
import functools

import jax
import jax.numpy as jnp
from jax import lax
from jax.experimental import pallas as pl
from jax.experimental.pallas import tpu as pltpu
from jax.sharding import PartitionSpec as P

WINDOW = 1024
TILE = 256

score_scale = 168.0 ** (-0.5)
norm_eps = 1e-06
exp2_scale = score_scale * 1.4426950408889634

GROUPS = 3
HEAVY = pl.CostEstimate(flops=10**11, bytes_accessed=10**8, transcendentals=0)
LIGHT = pl.CostEstimate(flops=1000, bytes_accessed=1000, transcendentals=0)

NT = (((1,), (1,)), ((), ()))


def inverse_rms_of(as_float):
    return lax.rsqrt(jnp.mean(as_float * as_float, axis=-1, keepdims=True) + norm_eps)


def norm_back(d_normed, raw, inverse_rms, gain_vec):
    unit_rows = raw * inverse_rms
    d_unit = d_normed * gain_vec
    return inverse_rms * (
        d_unit - unit_rows * jnp.mean(d_unit * unit_rows, axis=-1, keepdims=True)
    )


def heads_kernel(
    shard_ref, q_ref, g_ref, own_ref, near_ref, far_ref, q_gain_ref, k_gain_ref, _,
    dq_ref, d_own_ref, d_near_k_ref, d_near_v_ref, d_far_ref, gains_ref,
    k_low, k_low_t, k_rms, values, q_low, q_rms, probs_all, d_scores_all,
):
    rows = own_ref.shape[2]
    group = q_ref.shape[1] // rows
    lanes = TILE * group
    blocks = rows // TILE
    tiles = WINDOW // TILE
    q_gain, k_gain = q_gain_ref[...], k_gain_ref[...]
    far_ok = jnp.where(shard_ref[0] >= 2, 1.0, 0.0)
    near_ok = jnp.where(shard_ref[0] >= 1, 1.0, 0.0)
    key_refs = (far_ref, near_ref, own_ref)
    grad_refs = (
        (d_far_ref.at[0], d_far_ref.at[1]),
        (d_near_k_ref, d_near_v_ref),
        (d_own_ref.at[0], d_own_ref.at[1]),
    )

    @pl.when(pl.program_id(0) == 0)
    def _():
        gains_ref[...] = jnp.zeros_like(gains_ref)

    for place, ref in enumerate(key_refs):
        raw = ref[0, 0].astype(jnp.float32)
        here = slice(place * rows, (place + 1) * rows)
        inverse_rms = jnp.broadcast_to(inverse_rms_of(raw), raw.shape)
        k_rms[here, :] = inverse_rms
        k_low[here, :] = (raw * inverse_rms * k_gain).astype(jnp.bfloat16)
        values[here, :] = ref[1, 0]
    k_low_t[...] = k_low[...].T
    raw_q = q_ref[0].astype(jnp.float32)
    inverse_rms = jnp.broadcast_to(inverse_rms_of(raw_q), raw_q.shape)
    q_rms[...] = inverse_rms
    q_low[...] = (raw_q * inverse_rms * q_gain).astype(jnp.bfloat16)

    key_ids = lax.broadcasted_iota(jnp.int32, (TILE, lanes), 0)
    token_ids = lax.broadcasted_iota(jnp.int32, (TILE, lanes), 1) // group
    late = key_ids <= token_ids
    edge_ok = jnp.where(late, 1.0, far_ok)
    q_gain_sum = jnp.zeros_like(q_gain)

    for block in range(blocks):
        span = slice(block * TILE, block * TILE + WINDOW + TILE)
        mine = slice(block * lanes, (block + 1) * lanes)
        scores = lax.dot_general(
            k_low[span, :], q_low[mine, :], NT, preferred_element_type=jnp.float32
        )
        scores = jnp.concatenate(
            [jnp.where(late, scores[WINDOW:], scores[:TILE]), scores[TILE:WINDOW]], axis=0
        )
        exp_scores = jnp.exp2(scores * exp2_scale)
        edge = exp_scores[:TILE] * edge_ok
        first_near = (blocks - block) * TILE
        first_own = first_near + rows
        total = jnp.sum(edge, axis=0, keepdims=True)
        for low, high, ok in (
            (TILE, first_near, far_ok),
            (first_near, min(first_own, WINDOW), near_ok),
            (first_own, WINDOW, None),
        ):
            if low < high:
                part = jnp.sum(exp_scores[low:high], axis=0, keepdims=True)
                total = total + (part if ok is None else part * ok)
        inverse = 1.0 / total
        probs = jnp.concatenate([edge, exp_scores[TILE:]], axis=0) * inverse
        d_probs = lax.dot_general(
            values[span, :], g_ref[0, mine, :], NT, preferred_element_type=jnp.float32
        )
        d_probs = jnp.concatenate(
            [jnp.where(late, d_probs[WINDOW:], d_probs[:TILE]), d_probs[TILE:WINDOW]], axis=0
        )
        offset = jnp.sum(probs * d_probs, axis=0, keepdims=True)
        d_scores = probs * (d_probs - offset)
        for whole, held in ((probs, probs_all), (d_scores, d_scores_all)):
            start = block * TILE
            held[start : start + TILE, mine] = jnp.where(late, 0.0, whole[:TILE]).astype(
                jnp.bfloat16
            )
            held[start + TILE : start + WINDOW, mine] = whole[TILE:].astype(jnp.bfloat16)
            held[start + WINDOW : start + WINDOW + TILE, mine] = jnp.where(
                late, whole[:TILE], 0.0
            ).astype(jnp.bfloat16)
        query_grad = score_scale * jnp.dot(
            k_low_t[:, span], d_scores_all[span, mine], preferred_element_type=jnp.float32
        ).T
        raw = q_ref[0, mine, :].astype(jnp.float32)
        inverse_rms = q_rms[mine, :]
        q_gain_sum = q_gain_sum + jnp.sum(query_grad * (raw * inverse_rms), axis=0, keepdims=True)
        query_grad = norm_back(query_grad, raw, inverse_rms, q_gain).astype(dq_ref.dtype)
        dq_ref[start : start + TILE, 0, :, :] = query_grad.reshape(TILE, group, -1)

    pieces = [(tile, tile + 1, 0, tile + 1) for tile in range(blocks - 1)]
    pieces += [(blocks - 1, tiles + 1, 0, blocks)]
    pieces += [(tiles + block, tiles + block + 1, block, blocks) for block in range(1, blocks)]
    k_gain_sum = jnp.zeros_like(k_gain)
    for first, last, low, high in pieces:
        meets = slice(low * lanes, high * lanes)
        keys = slice(first * TILE, last * TILE)
        value_grad = jnp.dot(
            probs_all[keys, meets], g_ref[0, meets, :], preferred_element_type=jnp.float32
        )
        key_grad = score_scale * jnp.dot(
            d_scores_all[keys, meets], q_low[meets, :], preferred_element_type=jnp.float32
        )
        for place, (ref, outs) in enumerate(zip(key_refs, grad_refs, strict=True)):
            start = max(first * TILE, place * rows)
            stop = min(last * TILE, (place + 1) * rows)
            if start >= stop:
                continue
            inside = slice(start - place * rows, stop - place * rows)
            here = slice(start - first * TILE, stop - first * TILE)
            unit = ref[0, 0, inside, :].astype(jnp.float32) * k_rms[start:stop, :]
            k_gain_sum = k_gain_sum + jnp.sum(key_grad[here] * unit, axis=0, keepdims=True)
            outs[0][0, inside, :] = key_grad[here].astype(outs[0].dtype)
            outs[1][0, inside, :] = value_grad[here].astype(outs[1].dtype)
    gains_ref[0:1, :] += q_gain_sum
    gains_ref[1:2, :] += k_gain_sum


def closed(shard_ref, own, returned, swapped, kind, head):
    keep = jnp.where(shard_ref[0] % 2 == 1, 0.0, 1.0)
    own, returned = (part[kind, head].astype(jnp.float32) for part in (own, returned))
    return own + returned + keep * swapped[kind][head].astype(jnp.float32)


def close_kernel(shard_ref, own, returned, swapped_k, swapped_v, raw_ref, k_gain_ref, out):
    swapped = (swapped_k, swapped_v)
    for head in range(own.shape[1]):
        grad = closed(shard_ref, own, returned, swapped, 0, head)
        raw = raw_ref[0, head].astype(jnp.float32)
        grad = norm_back(grad, raw, inverse_rms_of(raw), k_gain_ref[...])
        out[0, head] = grad.astype(out.dtype)
        out[1, head] = closed(shard_ref, own, returned, swapped, 1, head).astype(out.dtype)


def finish_kernel(shard_ref, own, returned, swapped_k, swapped_v, raw_ref, k_gain_ref, *rest):
    swapped = (swapped_k, swapped_v)
    *done, key_out, value_out, by_token = rest
    rows, heads, _ = key_out.shape
    before = [(part, head) for part in done for head in range(part.shape[1])]
    for kind, out in ((0, key_out), (1, value_out)):
        for place, (part, head) in enumerate(before):
            by_token[pl.ds(place, rows, stride=heads), :] = part[kind, head].astype(jnp.float32)
        for head in range(own.shape[1]):
            grad = closed(shard_ref, own, returned, swapped, kind, head)
            if kind == 0:
                raw = raw_ref[0, head].astype(jnp.float32)
                grad = norm_back(grad, raw, inverse_rms_of(raw), k_gain_ref[...])
            by_token[pl.ds(len(before) + head, rows, stride=heads), :] = grad
        out[...] = by_token[...].reshape(out.shape).astype(out.dtype)


def choose_kernel(shard_ref, far_ref, own_ref, out_ref):
    odd = shard_ref[0] % 2 == 1

    @pl.when(odd)
    def _():
        out_ref[...] = far_ref[...]

    @pl.when(jnp.logical_not(odd))
    def _():
        out_ref[...] = own_ref[...]


def relay_kernel(shard_ref, far_ref, swapped_k_ref, swapped_v_ref, out_ref):
    odd = jnp.where(shard_ref[0] % 2 == 1, 1.0, 0.0)
    for kind, ref in enumerate((swapped_k_ref, swapped_v_ref)):
        total = far_ref[kind].astype(jnp.float32) + odd * ref[...].astype(jnp.float32)
        out_ref[kind] = total.astype(out_ref.dtype)


def choose(shard, far, own, here, count):
    _, _, rows, width = own.shape
    held = pl.BlockSpec((2, 1, rows, width), lambda head: (0, here + head, 0, 0))
    return pl.pallas_call(
        choose_kernel,
        grid=(count,),
        in_specs=[pl.BlockSpec(memory_space=pltpu.SMEM), held, held],
        out_specs=pl.BlockSpec((2, 1, rows, width), lambda head: (0, head, 0, 0)),
        out_shape=jax.ShapeDtypeStruct((2, count, rows, width), own.dtype),
        compiler_params=pltpu.CompilerParams(vmem_limit_bytes=8 * 1024 * 1024),
        cost_estimate=LIGHT,
    )(shard, far, own)


def small_call(kernel, shard, *arrays):
    smem, vmem = (pl.BlockSpec(memory_space=space) for space in (pltpu.SMEM, pltpu.VMEM))
    return pl.pallas_call(
        kernel,
        in_specs=[smem] + [vmem] * len(arrays),
        out_specs=vmem,
        out_shape=jax.ShapeDtypeStruct(arrays[0].shape, arrays[0].dtype),
        compiler_params=pltpu.CompilerParams(vmem_limit_bytes=12 * 1024 * 1024),
        cost_estimate=LIGHT,
    )(shard, *arrays)


def later_kernel(corner_ref, in_ref, out_ref):
    if len(in_ref.shape) == 1:
        out_ref[0] = in_ref[0]
    else:
        out_ref[...] = in_ref[...]


def later(array, small, cost=None):
    vmem = pl.BlockSpec(memory_space=pltpu.VMEM)
    held = pl.BlockSpec(memory_space=pltpu.SMEM if small.ndim == 1 else pltpu.VMEM)
    return pl.pallas_call(
        later_kernel,
        in_specs=[vmem, held],
        out_specs=held,
        out_shape=jax.ShapeDtypeStruct(small.shape, small.dtype),
        compiler_params=pltpu.CompilerParams(vmem_limit_bytes=1024 * 1024),
        cost_estimate=cost or HEAVY,
    )(array[0, 0, :16], small)


def group_grads(shard, first, here, count, queries, grads, own, near, far, q_gain, k_gain, dq):
    _, _, rows, width = own.shape
    query_rows = queries.shape[1]
    span = WINDOW + rows
    group = query_rows // rows
    whole_q = pl.BlockSpec((1, query_rows, width), lambda head: (first + head, 0, 0))
    part = pl.BlockSpec((2, 1, rows, width), lambda head: (0, head, 0, 0))
    held = pl.BlockSpec((2, 1, rows, width), lambda head: (0, here + head, 0, 0))
    half = pl.BlockSpec((1, rows, width), lambda head: (head, 0, 0))
    gain = pl.BlockSpec((1, width), lambda head: (0, 0))
    shape = (2, count, rows, width)
    return pl.pallas_call(
        heads_kernel,
        grid=(count,),
        in_specs=[
            pl.BlockSpec(memory_space=pltpu.SMEM), whole_q, whole_q, held, part, held, gain, gain,
            pl.BlockSpec(memory_space=pl.ANY),
        ],
        out_specs=[
            pl.BlockSpec((rows, 1, group, width), lambda head: (0, first + head, 0, 0)),
            part,
            half,
            half,
            part,
            pl.BlockSpec((2, width), lambda head: (0, 0)),
        ],
        out_shape=[
            jax.ShapeDtypeStruct(dq.shape, dq.dtype),
            jax.ShapeDtypeStruct(shape, jnp.bfloat16),
            jax.ShapeDtypeStruct(shape[1:], jnp.bfloat16),
            jax.ShapeDtypeStruct(shape[1:], jnp.bfloat16),
            jax.ShapeDtypeStruct(shape, jnp.bfloat16),
            jax.ShapeDtypeStruct((2, width), jnp.float32),
        ],
        scratch_shapes=[
            pltpu.VMEM((span, width), jnp.bfloat16),
            pltpu.VMEM((width, span), jnp.bfloat16),
            pltpu.VMEM((span, width), jnp.float32),
            pltpu.VMEM((span, width), jnp.bfloat16),
            pltpu.VMEM((query_rows, width), jnp.bfloat16),
            pltpu.VMEM((query_rows, width), jnp.float32),
            pltpu.VMEM((span, query_rows), jnp.bfloat16),
            pltpu.VMEM((span, query_rows), jnp.bfloat16),
        ],
        input_output_aliases={8: 0},
        compiler_params=pltpu.CompilerParams(vmem_limit_bytes=22 * 1024 * 1024),
        cost_estimate=LIGHT,
    )(shard, queries, grads, own, near, far, q_gain, k_gain, dq)


def close_group(shard, own, returned, swapped, raw, k_gain):
    smem, vmem = (pl.BlockSpec(memory_space=space) for space in (pltpu.SMEM, pltpu.VMEM))
    return pl.pallas_call(
        close_kernel,
        in_specs=[smem] + [vmem] * 6,
        out_specs=vmem,
        out_shape=jax.ShapeDtypeStruct(own.shape, jnp.bfloat16),
        compiler_params=pltpu.CompilerParams(vmem_limit_bytes=12 * 1024 * 1024),
        cost_estimate=LIGHT,
    )(shard, own, returned, *swapped, raw, k_gain)


def finish(shard, own, returned, swapped, raw, k_gain, done):
    _, count, rows, width = own.shape
    kv_dev = count + sum(part.shape[1] for part in done)
    shape = (rows, kv_dev, width)
    smem, vmem = (pl.BlockSpec(memory_space=space) for space in (pltpu.SMEM, pltpu.VMEM))
    return pl.pallas_call(
        finish_kernel,
        in_specs=[smem] + [vmem] * (6 + len(done)),
        out_specs=[vmem, vmem],
        out_shape=[jax.ShapeDtypeStruct(shape, jnp.bfloat16)] * 2,
        scratch_shapes=[pltpu.VMEM((rows * kv_dev, width), jnp.float32)],
        compiler_params=pltpu.CompilerParams(vmem_limit_bytes=20 * 1024 * 1024),
    )(shard, own, returned, *swapped, raw, k_gain, *done)


def group_sizes(kv_dev):
    count = min(GROUPS, kv_dev)
    return [(kv_dev + count - 1 - place) // count for place in range(count)]


def exchanged(value, *bits):
    count = lax.axis_size(("seq", "head"))
    assert count & (count - 1) == 0
    masks = [1 << bit for bit in bits]
    masks += [sum(masks)] if len(masks) > 1 else []
    return [
        lax.ppermute(value, ("seq", "head"), [(source, source ^ mask) for source in range(count)])
        for mask in masks
    ]


def summed(value, others):
    return value + others[0] if len(others) == 1 else (value + others[0]) + (others[1] + others[2])


def per_device(query, key, value, grad_out, q_gain, k_gain):
    rows, heads, width = query.shape
    kv_dev = key.shape[1]
    group = heads // kv_dev
    count = lax.axis_size("seq")
    assert 2 * rows == WINDOW and rows % TILE == 0 and count % 2 == 0
    shard = lax.axis_index("seq")
    ahead = [(source, source + 2) for source in range(count - 2)]
    back = [(source + 2, source) for source in range(count - 2)]
    swap = [(source, source ^ 1) for source in range(count)]

    def by_head(array):
        split = array.reshape(rows, kv_dev, group, width)
        return jnp.transpose(split, (1, 0, 2, 3)).reshape(kv_dev, rows * group, width)

    sizes = group_sizes(kv_dev)
    starts = [sum(sizes[:place]) for place in range(len(sizes))]
    cuts = [(0, sizes[0])] + ([(sizes[0], kv_dev)] if len(sizes) > 1 else [])
    by_kind = lax.optimization_barrier([jnp.transpose(kind, (1, 0, 2)) for kind in (key, value)])
    owns = [jnp.stack([kind[low:high] for kind in by_kind]) for low, high in cuts]
    fars = [lax.ppermute(own, "seq", ahead) for own in owns]
    queries, grads = by_head(query), by_head(grad_out)
    scalar = shard.astype(jnp.int32).reshape(1)
    q_gain_2d, k_gain_2d = q_gain.reshape(1, width), k_gain.reshape(1, width)

    def split(d_own, d_near_k, d_near_v, d_far, raw):
        swapped = [lax.ppermute(half, "seq", swap) for half in (d_near_k, d_near_v)]
        relayed = small_call(relay_kernel, scalar, d_far, *swapped)
        return relayed, (d_own, swapped, raw)

    def close(stays, returned):
        d_own, swapped, raw = stays
        return close_group(scalar, d_own, returned, swapped, raw, k_gain_2d)

    gains, kept, done = [], [], []
    grad_query = jnp.zeros((rows, kv_dev, group, width), query.dtype)
    grads_out = None
    for place, (first, size) in enumerate(zip(starts, sizes, strict=True)):
        if grads_out is not None:
            relayed, stays = split(*grads_out)
        if place < 2:
            own, far, start = owns[place], fars[place], cuts[place][0]
            if place:
                far, gains[0] = lax.optimization_barrier((far, gains[0]))
                gains[0] = later(far, gains[0])
                far, gains[0], relayed = lax.optimization_barrier((far, gains[0], relayed))
            else:
                far, queries, grads, *_ = lax.optimization_barrier(
                    (far, queries, grads, *owns[1:])
                )
        elif place:
            far, gains[-1] = lax.optimization_barrier((far, gains[-1]))
        chosen = choose(scalar, far, own, first - start, size)
        near = lax.ppermute(chosen, "seq", swap)
        scalar_now = scalar
        if grads_out is not None:
            if kept:
                before, returned = kept.pop()
                near, returned = lax.optimization_barrier((near, returned))
                scalar_now = later(returned, scalar, LIGHT)
                done.append(close(before, returned))
            kept.append((stays, lax.ppermute(relayed, "seq", back)))
        here = slice(first - start, first - start + size)
        grad_query, *grads_out, gain = group_grads(
            scalar_now, first, first - start, size, queries, grads, own, near, far,
            q_gain_2d, k_gain_2d, grad_query,
        )
        grads_out.append(own[:1, here])
        gains.append(gain)
    relayed, stays = split(*grads_out)
    head_bits, seq_bits = ((lax.axis_size(axis) - 1).bit_length() for axis in ("head", "seq"))
    assert head_bits and seq_bits > 3
    chips = range(head_bits + 1, head_bits + seq_bits)
    gain_sum = sum(gains[1:], gains[0])
    others = exchanged(gain_sum, chips[0])
    if kept:
        before, returned = kept.pop()
        returned, done = lax.optimization_barrier((returned, done))
        gain_sum = later(returned, gain_sum)
        done.append(close(before, returned))
    gain_sum, others = lax.optimization_barrier((gain_sum, others))
    gain_sum = summed(gain_sum, others)
    returned = lax.ppermute(relayed, "seq", back)
    grad_query = grad_query.reshape(rows, heads, width)
    exchanges = [(0, head_bits), *((bit,) for bit in range(1, head_bits))]
    exchanges += [(bit,) for bit in chips[1:-2]]
    for bits in exchanges:
        gain_sum = summed(gain_sum, exchanged(gain_sum, *bits))
    gain_sum, grad_query, done = lax.optimization_barrier((gain_sum, grad_query, done))
    d_own, swapped, raw = stays
    grad_key, grad_value = finish(scalar, d_own, returned, swapped, raw, k_gain_2d, done)
    others, grad_key = lax.optimization_barrier((exchanged(gain_sum, *chips[-2:]), grad_key))
    gain_sum = summed(gain_sum, others)
    return (grad_query, grad_key, grad_value, gain_sum[0], gain_sum[1])


def solution(mesh):
    split, whole = P("seq", "head", None), P()
    return jax.shard_map(
        per_device,
        mesh=mesh,
        in_specs=(split, split, split, split, whole, whole),
        out_specs=(split, split, split, whole, whole),
        check_vma=False,
    )
```

```python
import functools

import jax
import jax.numpy as jnp
from jax import lax
from jax.experimental import pallas as pl
from jax.experimental.pallas import tpu as pltpu
from jax.sharding import PartitionSpec as P

WINDOW = 1024
TILE = 256

score_scale = 168.0 ** (-0.5)
norm_eps = 1e-06
exp2_scale = score_scale * 1.4426950408889634

GROUPS = 3
HEAVY = pl.CostEstimate(flops=10**11, bytes_accessed=10**8, transcendentals=0)
LIGHT = pl.CostEstimate(flops=1000, bytes_accessed=1000, transcendentals=0)

NT = (((1,), (1,)), ((), ()))


def inverse_rms_of(as_float):
    return lax.rsqrt(jnp.mean(as_float * as_float, axis=-1, keepdims=True) + norm_eps)


def norm_back(d_normed, raw, inverse_rms, gain_vec):
    unit_rows = raw * inverse_rms
    d_unit = d_normed * gain_vec
    return inverse_rms * (
        d_unit - unit_rows * jnp.mean(d_unit * unit_rows, axis=-1, keepdims=True)
    )


def heads_kernel(
    shard_ref, q_ref, g_ref, own_ref, near_ref, far_ref, q_gain_ref, k_gain_ref, _,
    dq_ref, d_own_ref, d_near_k_ref, d_near_v_ref, d_far_ref, gains_ref,
    k_low, k_low_t, k_rms, values, q_low, q_rms, key_total, value_total,
):
    rows = own_ref.shape[2]
    group = q_ref.shape[1] // rows
    lanes = TILE * group
    blocks = rows // TILE
    q_gain, k_gain = q_gain_ref[...], k_gain_ref[...]
    far_ok = jnp.where(shard_ref[0] >= 2, 1.0, 0.0)
    near_ok = jnp.where(shard_ref[0] >= 1, 1.0, 0.0)
    key_refs = (far_ref, near_ref, own_ref)
    grad_refs = (
        (d_far_ref.at[0], d_far_ref.at[1]),
        (d_near_k_ref, d_near_v_ref),
        (d_own_ref.at[0], d_own_ref.at[1]),
    )

    @pl.when(pl.program_id(0) == 0)
    def _():
        gains_ref[...] = jnp.zeros_like(gains_ref)

    for place, ref in enumerate(key_refs):
        raw = ref[0, 0].astype(jnp.float32)
        here = slice(place * rows, (place + 1) * rows)
        inverse_rms = jnp.broadcast_to(inverse_rms_of(raw), raw.shape)
        k_rms[here, :] = inverse_rms
        k_low[here, :] = (raw * inverse_rms * k_gain).astype(jnp.bfloat16)
        values[here, :] = ref[1, 0]
    k_low_t[...] = k_low[...].T
    raw_q = q_ref[0].astype(jnp.float32)
    inverse_rms = jnp.broadcast_to(inverse_rms_of(raw_q), raw_q.shape)
    q_rms[...] = inverse_rms
    q_low[...] = (raw_q * inverse_rms * q_gain).astype(jnp.bfloat16)

    key_ids = lax.broadcasted_iota(jnp.int32, (TILE, lanes), 0)
    token_ids = lax.broadcasted_iota(jnp.int32, (TILE, lanes), 1) // group
    late = key_ids <= token_ids
    edge_ok = jnp.where(late, 1.0, far_ok)
    q_gain_sum = jnp.zeros_like(q_gain)

    for block in range(blocks):
        start = block * TILE
        span = slice(start, start + WINDOW + TILE)
        mine = slice(block * lanes, (block + 1) * lanes)
        scores = lax.dot_general(
            k_low[span, :], q_low[mine, :], NT, preferred_element_type=jnp.float32
        )
        scores = jnp.concatenate(
            [jnp.where(late, scores[WINDOW:], scores[:TILE]), scores[TILE:WINDOW]], axis=0
        )
        exp_scores = jnp.exp2(scores * exp2_scale)
        edge = exp_scores[:TILE] * edge_ok
        first_near = (blocks - block) * TILE
        first_own = first_near + rows
        total = jnp.sum(edge, axis=0, keepdims=True)
        for low, high, ok in (
            (TILE, first_near, far_ok),
            (first_near, min(first_own, WINDOW), near_ok),
            (first_own, WINDOW, None),
        ):
            if low < high:
                part = jnp.sum(exp_scores[low:high], axis=0, keepdims=True)
                total = total + (part if ok is None else part * ok)
        inverse = 1.0 / total
        probs = jnp.concatenate([edge, exp_scores[TILE:]], axis=0) * inverse
        d_probs = lax.dot_general(
            values[span, :], g_ref[0, mine, :], NT, preferred_element_type=jnp.float32
        )
        d_probs = jnp.concatenate(
            [jnp.where(late, d_probs[WINDOW:], d_probs[:TILE]), d_probs[TILE:WINDOW]], axis=0
        )
        offset = jnp.sum(probs * d_probs, axis=0, keepdims=True)
        d_scores = probs * (d_probs - offset)
        probs_low, d_scores_low = (
            jnp.concatenate(
                [jnp.where(late, 0.0, whole[:TILE]), whole[TILE:], jnp.where(late, whole[:TILE], 0.0)],
                axis=0,
            ).astype(jnp.bfloat16)
            for whole in (probs, d_scores)
        )
        query_grad = score_scale * jnp.dot(
            k_low_t[:, span], d_scores_low, preferred_element_type=jnp.float32
        ).T
        for held, left, right in (
            (value_total, probs_low, g_ref[0, mine, :]),
            (key_total, d_scores_low, q_low[mine, :]),
        ):
            part = jnp.dot(left, right, preferred_element_type=jnp.float32)
            if block:
                held[start : start + WINDOW, :] += part[:WINDOW]
                held[start + WINDOW : start + WINDOW + TILE, :] = part[WINDOW:]
            else:
                held[span, :] = part
        raw = q_ref[0, mine, :].astype(jnp.float32)
        inverse_rms = q_rms[mine, :]
        q_gain_sum = q_gain_sum + jnp.sum(query_grad * (raw * inverse_rms), axis=0, keepdims=True)
        query_grad = norm_back(query_grad, raw, inverse_rms, q_gain).astype(dq_ref.dtype)
        dq_ref[start : start + TILE, 0, :, :] = query_grad.reshape(TILE, group, -1)

    k_gain_sum = jnp.zeros_like(k_gain)
    for place, (ref, outs) in enumerate(zip(key_refs, grad_refs, strict=True)):
        here = slice(place * rows, (place + 1) * rows)
        key_grad = score_scale * key_total[here, :]
        unit = ref[0, 0].astype(jnp.float32) * k_rms[here, :]
        k_gain_sum = k_gain_sum + jnp.sum(key_grad * unit, axis=0, keepdims=True)
        outs[0][0] = key_grad.astype(outs[0].dtype)
        outs[1][0] = value_total[here, :].astype(outs[1].dtype)
    gains_ref[0:1, :] += q_gain_sum
    gains_ref[1:2, :] += k_gain_sum


def closed(shard_ref, own, returned, swapped, kind, head):
    keep = jnp.where(shard_ref[0] % 2 == 1, 0.0, 1.0)
    own, returned = (part[kind, head].astype(jnp.float32) for part in (own, returned))
    return own + returned + keep * swapped[kind][head].astype(jnp.float32)


def close_kernel(shard_ref, own, returned, swapped_k, swapped_v, raw_ref, k_gain_ref, out):
    swapped = (swapped_k, swapped_v)
    for head in range(own.shape[1]):
        grad = closed(shard_ref, own, returned, swapped, 0, head)
        raw = raw_ref[0, head].astype(jnp.float32)
        grad = norm_back(grad, raw, inverse_rms_of(raw), k_gain_ref[...])
        out[0, head] = grad.astype(out.dtype)
        out[1, head] = closed(shard_ref, own, returned, swapped, 1, head).astype(out.dtype)


def finish_kernel(shard_ref, own, returned, swapped_k, swapped_v, raw_ref, k_gain_ref, *rest):
    swapped = (swapped_k, swapped_v)
    *done, key_out, value_out, by_token = rest
    rows, heads, _ = key_out.shape
    before = [(part, head) for part in done for head in range(part.shape[1])]
    for kind, out in ((0, key_out), (1, value_out)):
        for place, (part, head) in enumerate(before):
            by_token[pl.ds(place, rows, stride=heads), :] = part[kind, head].astype(jnp.float32)
        for head in range(own.shape[1]):
            grad = closed(shard_ref, own, returned, swapped, kind, head)
            if kind == 0:
                raw = raw_ref[0, head].astype(jnp.float32)
                grad = norm_back(grad, raw, inverse_rms_of(raw), k_gain_ref[...])
            by_token[pl.ds(len(before) + head, rows, stride=heads), :] = grad
        out[...] = by_token[...].reshape(out.shape).astype(out.dtype)


def choose_kernel(shard_ref, far_ref, own_ref, out_ref):
    odd = shard_ref[0] % 2 == 1

    @pl.when(odd)
    def _():
        out_ref[...] = far_ref[...]

    @pl.when(jnp.logical_not(odd))
    def _():
        out_ref[...] = own_ref[...]


def relay_kernel(shard_ref, far_ref, swapped_k_ref, swapped_v_ref, out_ref):
    odd = jnp.where(shard_ref[0] % 2 == 1, 1.0, 0.0)
    for kind, ref in enumerate((swapped_k_ref, swapped_v_ref)):
        total = far_ref[kind].astype(jnp.float32) + odd * ref[...].astype(jnp.float32)
        out_ref[kind] = total.astype(out_ref.dtype)


def choose(shard, far, own, here, count):
    _, _, rows, width = own.shape
    held = pl.BlockSpec((2, 1, rows, width), lambda head: (0, here + head, 0, 0))
    return pl.pallas_call(
        choose_kernel,
        grid=(count,),
        in_specs=[pl.BlockSpec(memory_space=pltpu.SMEM), held, held],
        out_specs=pl.BlockSpec((2, 1, rows, width), lambda head: (0, head, 0, 0)),
        out_shape=jax.ShapeDtypeStruct((2, count, rows, width), own.dtype),
        compiler_params=pltpu.CompilerParams(vmem_limit_bytes=8 * 1024 * 1024),
        cost_estimate=LIGHT,
    )(shard, far, own)


def small_call(kernel, shard, *arrays):
    smem, vmem = (pl.BlockSpec(memory_space=space) for space in (pltpu.SMEM, pltpu.VMEM))
    return pl.pallas_call(
        kernel,
        in_specs=[smem] + [vmem] * len(arrays),
        out_specs=vmem,
        out_shape=jax.ShapeDtypeStruct(arrays[0].shape, arrays[0].dtype),
        compiler_params=pltpu.CompilerParams(vmem_limit_bytes=12 * 1024 * 1024),
        cost_estimate=LIGHT,
    )(shard, *arrays)


def later_kernel(corner_ref, in_ref, out_ref):
    if len(in_ref.shape) == 1:
        out_ref[0] = in_ref[0]
    else:
        out_ref[...] = in_ref[...]


def later(array, small, cost=None):
    vmem = pl.BlockSpec(memory_space=pltpu.VMEM)
    held = pl.BlockSpec(memory_space=pltpu.SMEM if small.ndim == 1 else pltpu.VMEM)
    return pl.pallas_call(
        later_kernel,
        in_specs=[vmem, held],
        out_specs=held,
        out_shape=jax.ShapeDtypeStruct(small.shape, small.dtype),
        compiler_params=pltpu.CompilerParams(vmem_limit_bytes=1024 * 1024),
        cost_estimate=cost or HEAVY,
    )(array[0, 0, :16], small)


def group_grads(shard, first, here, count, queries, grads, own, near, far, q_gain, k_gain, dq):
    _, _, rows, width = own.shape
    query_rows = queries.shape[1]
    span = WINDOW + rows
    group = query_rows // rows
    whole_q = pl.BlockSpec((1, query_rows, width), lambda head: (first + head, 0, 0))
    part = pl.BlockSpec((2, 1, rows, width), lambda head: (0, head, 0, 0))
    held = pl.BlockSpec((2, 1, rows, width), lambda head: (0, here + head, 0, 0))
    half = pl.BlockSpec((1, rows, width), lambda head: (head, 0, 0))
    gain = pl.BlockSpec((1, width), lambda head: (0, 0))
    shape = (2, count, rows, width)
    return pl.pallas_call(
        heads_kernel,
        grid=(count,),
        in_specs=[
            pl.BlockSpec(memory_space=pltpu.SMEM), whole_q, whole_q, held, part, held, gain, gain,
            pl.BlockSpec(memory_space=pl.ANY),
        ],
        out_specs=[
            pl.BlockSpec((rows, 1, group, width), lambda head: (0, first + head, 0, 0)),
            part,
            half,
            half,
            part,
            pl.BlockSpec((2, width), lambda head: (0, 0)),
        ],
        out_shape=[
            jax.ShapeDtypeStruct(dq.shape, dq.dtype),
            jax.ShapeDtypeStruct(shape, jnp.bfloat16),
            jax.ShapeDtypeStruct(shape[1:], jnp.bfloat16),
            jax.ShapeDtypeStruct(shape[1:], jnp.bfloat16),
            jax.ShapeDtypeStruct(shape, jnp.bfloat16),
            jax.ShapeDtypeStruct((2, width), jnp.float32),
        ],
        scratch_shapes=[
            pltpu.VMEM((span, width), jnp.bfloat16),
            pltpu.VMEM((width, span), jnp.bfloat16),
            pltpu.VMEM((span, width), jnp.float32),
            pltpu.VMEM((span, width), jnp.bfloat16),
            pltpu.VMEM((query_rows, width), jnp.bfloat16),
            pltpu.VMEM((query_rows, width), jnp.float32),
            pltpu.VMEM((span, width), jnp.float32),
            pltpu.VMEM((span, width), jnp.float32),
        ],
        input_output_aliases={8: 0},
        compiler_params=pltpu.CompilerParams(vmem_limit_bytes=22 * 1024 * 1024),
        cost_estimate=LIGHT,
    )(shard, queries, grads, own, near, far, q_gain, k_gain, dq)


def close_group(shard, own, returned, swapped, raw, k_gain):
    smem, vmem = (pl.BlockSpec(memory_space=space) for space in (pltpu.SMEM, pltpu.VMEM))
    return pl.pallas_call(
        close_kernel,
        in_specs=[smem] + [vmem] * 6,
        out_specs=vmem,
        out_shape=jax.ShapeDtypeStruct(own.shape, jnp.bfloat16),
        compiler_params=pltpu.CompilerParams(vmem_limit_bytes=12 * 1024 * 1024),
        cost_estimate=LIGHT,
    )(shard, own, returned, *swapped, raw, k_gain)


def finish(shard, own, returned, swapped, raw, k_gain, done):
    _, count, rows, width = own.shape
    kv_dev = count + sum(part.shape[1] for part in done)
    shape = (rows, kv_dev, width)
    smem, vmem = (pl.BlockSpec(memory_space=space) for space in (pltpu.SMEM, pltpu.VMEM))
    return pl.pallas_call(
        finish_kernel,
        in_specs=[smem] + [vmem] * (6 + len(done)),
        out_specs=[vmem, vmem],
        out_shape=[jax.ShapeDtypeStruct(shape, jnp.bfloat16)] * 2,
        scratch_shapes=[pltpu.VMEM((rows * kv_dev, width), jnp.float32)],
        compiler_params=pltpu.CompilerParams(vmem_limit_bytes=20 * 1024 * 1024),
    )(shard, own, returned, *swapped, raw, k_gain, *done)


def group_sizes(kv_dev):
    count = min(GROUPS, kv_dev)
    return [(kv_dev + count - 1 - place) // count for place in range(count)]


def exchanged(value, *bits):
    count = lax.axis_size(("seq", "head"))
    assert count & (count - 1) == 0
    masks = [1 << bit for bit in bits]
    masks += [sum(masks)] if len(masks) > 1 else []
    return [
        lax.ppermute(value, ("seq", "head"), [(source, source ^ mask) for source in range(count)])
        for mask in masks
    ]


def summed(value, others):
    return value + others[0] if len(others) == 1 else (value + others[0]) + (others[1] + others[2])


def per_device(query, key, value, grad_out, q_gain, k_gain):
    rows, heads, width = query.shape
    kv_dev = key.shape[1]
    group = heads // kv_dev
    count = lax.axis_size("seq")
    assert 2 * rows == WINDOW and rows % TILE == 0 and count % 2 == 0
    shard = lax.axis_index("seq")
    ahead = [(source, source + 2) for source in range(count - 2)]
    back = [(source + 2, source) for source in range(count - 2)]
    swap = [(source, source ^ 1) for source in range(count)]

    def by_head(array):
        split = array.reshape(rows, kv_dev, group, width)
        return jnp.transpose(split, (1, 0, 2, 3)).reshape(kv_dev, rows * group, width)

    sizes = group_sizes(kv_dev)
    starts = [sum(sizes[:place]) for place in range(len(sizes))]
    cuts = [(0, sizes[0])] + ([(sizes[0], kv_dev)] if len(sizes) > 1 else [])
    by_kind = lax.optimization_barrier([jnp.transpose(kind, (1, 0, 2)) for kind in (key, value)])
    owns = [jnp.stack([kind[low:high] for kind in by_kind]) for low, high in cuts]
    fars = [lax.ppermute(own, "seq", ahead) for own in owns]
    queries, grads = by_head(query), by_head(grad_out)
    scalar = shard.astype(jnp.int32).reshape(1)
    q_gain_2d, k_gain_2d = q_gain.reshape(1, width), k_gain.reshape(1, width)

    def split(d_own, d_near_k, d_near_v, d_far, raw):
        swapped = [lax.ppermute(half, "seq", swap) for half in (d_near_k, d_near_v)]
        relayed = small_call(relay_kernel, scalar, d_far, *swapped)
        return relayed, (d_own, swapped, raw)

    def close(stays, returned):
        d_own, swapped, raw = stays
        return close_group(scalar, d_own, returned, swapped, raw, k_gain_2d)

    gains, kept, done = [], [], []
    grad_query = jnp.zeros((rows, kv_dev, group, width), query.dtype)
    grads_out = None
    for place, (first, size) in enumerate(zip(starts, sizes, strict=True)):
        if grads_out is not None:
            relayed, stays = split(*grads_out)
        if place < 2:
            own, far, start = owns[place], fars[place], cuts[place][0]
            if place:
                far, gains[0] = lax.optimization_barrier((far, gains[0]))
                gains[0] = later(far, gains[0])
                far, gains[0], relayed = lax.optimization_barrier((far, gains[0], relayed))
            else:
                far, queries, grads, *_ = lax.optimization_barrier(
                    (far, queries, grads, *owns[1:])
                )
        elif place:
            far, gains[-1] = lax.optimization_barrier((far, gains[-1]))
        chosen = choose(scalar, far, own, first - start, size)
        near = lax.ppermute(chosen, "seq", swap)
        scalar_now = scalar
        if grads_out is not None:
            if kept:
                before, returned = kept.pop()
                near, returned = lax.optimization_barrier((near, returned))
                scalar_now = later(returned, scalar, LIGHT)
                done.append(close(before, returned))
            kept.append((stays, lax.ppermute(relayed, "seq", back)))
        here = slice(first - start, first - start + size)
        grad_query, *grads_out, gain = group_grads(
            scalar_now, first, first - start, size, queries, grads, own, near, far,
            q_gain_2d, k_gain_2d, grad_query,
        )
        grads_out.append(own[:1, here])
        gains.append(gain)
    relayed, stays = split(*grads_out)
    head_bits, seq_bits = ((lax.axis_size(axis) - 1).bit_length() for axis in ("head", "seq"))
    assert head_bits and seq_bits > 3
    chips = range(head_bits + 1, head_bits + seq_bits)
    gain_sum = sum(gains[1:], gains[0])
    others = exchanged(gain_sum, chips[0])
    if kept:
        before, returned = kept.pop()
        returned, done = lax.optimization_barrier((returned, done))
        gain_sum = later(returned, gain_sum)
        done.append(close(before, returned))
    gain_sum, others = lax.optimization_barrier((gain_sum, others))
    gain_sum = summed(gain_sum, others)
    returned = lax.ppermute(relayed, "seq", back)
    grad_query = grad_query.reshape(rows, heads, width)
    exchanges = [(0, head_bits), *((bit,) for bit in range(1, head_bits))]
    exchanges += [(bit,) for bit in chips[1:-2]]
    for bits in exchanges:
        gain_sum = summed(gain_sum, exchanged(gain_sum, *bits))
    gain_sum, grad_query, done = lax.optimization_barrier((gain_sum, grad_query, done))
    d_own, swapped, raw = stays
    grad_key, grad_value = finish(scalar, d_own, returned, swapped, raw, k_gain_2d, done)
    others, grad_key = lax.optimization_barrier((exchanged(gain_sum, *chips[-2:]), grad_key))
    gain_sum = summed(gain_sum, others)
    return (grad_query, grad_key, grad_value, gain_sum[0], gain_sum[1])


def solution(mesh):
    split, whole = P("seq", "head", None), P()
    return jax.shard_map(
        per_device,
        mesh=mesh,
        in_specs=(split, split, split, split, whole, whole),
        out_specs=(split, split, split, whole, whole),
        check_vma=False,
    )
```

```python
import functools

import jax
import jax.numpy as jnp
from jax import lax
from jax.experimental import pallas as pl
from jax.experimental.pallas import tpu as pltpu
from jax.sharding import PartitionSpec as P

WINDOW = 1024
TILE = 256

score_scale = 168.0 ** (-0.5)
norm_eps = 1e-06
exp2_scale = score_scale * 1.4426950408889634

GROUPS = 3
HEAVY = pl.CostEstimate(flops=10**11, bytes_accessed=10**8, transcendentals=0)
LIGHT = pl.CostEstimate(flops=1000, bytes_accessed=1000, transcendentals=0)

NT = (((1,), (1,)), ((), ()))


def inverse_rms_of(as_float):
    return lax.rsqrt(jnp.mean(as_float * as_float, axis=-1, keepdims=True) + norm_eps)


def norm_back(d_normed, raw, inverse_rms, gain_vec):
    unit_rows = raw * inverse_rms
    d_unit = d_normed * gain_vec
    return inverse_rms * (
        d_unit - unit_rows * jnp.mean(d_unit * unit_rows, axis=-1, keepdims=True)
    )


def heads_kernel(
    shard_ref, q_ref, g_ref, own_ref, near_ref, far_ref, q_gain_ref, k_gain_ref, _,
    dq_ref, d_own_ref, d_near_k_ref, d_near_v_ref, d_far_ref, gains_ref,
    k_low, k_low_t, k_rms, values, q_low, q_rms, key_total, value_total,
):
    rows = own_ref.shape[2]
    group = q_ref.shape[1] // rows
    lanes = TILE * group
    blocks = rows // TILE
    q_gain, k_gain = q_gain_ref[...], k_gain_ref[...]
    far_ok = jnp.where(shard_ref[0] >= 2, 1.0, 0.0)
    near_ok = jnp.where(shard_ref[0] >= 1, 1.0, 0.0)
    key_refs = (far_ref, near_ref, own_ref)
    grad_refs = (
        (d_far_ref.at[0], d_far_ref.at[1]),
        (d_near_k_ref, d_near_v_ref),
        (d_own_ref.at[0], d_own_ref.at[1]),
    )

    @pl.when(pl.program_id(0) == 0)
    def _():
        gains_ref[...] = jnp.zeros_like(gains_ref)

    for place, ref in enumerate(key_refs):
        raw = ref[0, 0].astype(jnp.float32)
        here = slice(place * rows, (place + 1) * rows)
        inverse_rms = jnp.broadcast_to(inverse_rms_of(raw), raw.shape)
        k_rms[here, :] = inverse_rms
        k_low[here, :] = (raw * inverse_rms * k_gain).astype(jnp.bfloat16)
        values[here, :] = ref[1, 0]
    k_low_t[...] = k_low[...].T
    raw_q = q_ref[0].astype(jnp.float32)
    inverse_rms = jnp.broadcast_to(inverse_rms_of(raw_q), raw_q.shape)
    q_rms[...] = inverse_rms
    q_low[...] = (raw_q * inverse_rms * q_gain).astype(jnp.bfloat16)

    key_ids = lax.broadcasted_iota(jnp.int32, (TILE, lanes), 0)
    token_ids = lax.broadcasted_iota(jnp.int32, (TILE, lanes), 1) // group
    late = key_ids <= token_ids
    edge_ok = jnp.where(late, 1.0, far_ok)
    q_gain_sum = jnp.zeros_like(q_gain)

    for block in range(blocks):
        start = block * TILE
        span = slice(start, start + WINDOW + TILE)
        mine = slice(block * lanes, (block + 1) * lanes)
        scores = lax.dot_general(
            k_low[span, :], q_low[mine, :], NT, preferred_element_type=jnp.float32
        )
        scores = jnp.concatenate(
            [jnp.where(late, scores[WINDOW:], scores[:TILE]), scores[TILE:WINDOW]], axis=0
        )
        exp_scores = jnp.exp2(scores * exp2_scale)
        edge = exp_scores[:TILE] * edge_ok
        first_near = (blocks - block) * TILE
        first_own = first_near + rows
        total = jnp.sum(edge, axis=0, keepdims=True)
        for low, high, ok in (
            (TILE, first_near, far_ok),
            (first_near, min(first_own, WINDOW), near_ok),
            (first_own, WINDOW, None),
        ):
            if low < high:
                part = jnp.sum(exp_scores[low:high], axis=0, keepdims=True)
                total = total + (part if ok is None else part * ok)
        inverse = 1.0 / total
        probs = jnp.concatenate([edge, exp_scores[TILE:]], axis=0) * inverse
        d_probs = lax.dot_general(
            values[span, :], g_ref[0, mine, :], NT, preferred_element_type=jnp.float32
        )
        d_probs = jnp.concatenate(
            [jnp.where(late, d_probs[WINDOW:], d_probs[:TILE]), d_probs[TILE:WINDOW]], axis=0
        )
        offset = jnp.sum(probs * d_probs, axis=0, keepdims=True)
        d_scores = probs * (d_probs - offset)
        probs_low, d_scores_low = (
            jnp.concatenate(
                [jnp.where(late, 0.0, whole[:TILE]), whole[TILE:], jnp.where(late, whole[:TILE], 0.0)],
                axis=0,
            ).astype(jnp.bfloat16)
            for whole in (probs, d_scores)
        )
        query_grad = score_scale * jnp.dot(
            k_low_t[:, span], d_scores_low, preferred_element_type=jnp.float32
        ).T
        for held, left, right in (
            (value_total, probs_low, g_ref[0, mine, :]),
            (key_total, d_scores_low, q_low[mine, :]),
        ):
            part = jnp.dot(left, right, preferred_element_type=jnp.float32)
            if block:
                held[start : start + WINDOW, :] += part[:WINDOW]
                held[start + WINDOW : start + WINDOW + TILE, :] = part[WINDOW:]
            else:
                held[span, :] = part
        raw = q_ref[0, mine, :].astype(jnp.float32)
        inverse_rms = q_rms[mine, :]
        q_gain_sum = q_gain_sum + jnp.sum(query_grad * (raw * inverse_rms), axis=0, keepdims=True)
        query_grad = norm_back(query_grad, raw, inverse_rms, q_gain).astype(dq_ref.dtype)
        dq_ref[start : start + TILE, 0, :, :] = query_grad.reshape(TILE, group, -1)

    k_gain_sum = jnp.zeros_like(k_gain)
    for place, (ref, outs) in enumerate(zip(key_refs, grad_refs, strict=True)):
        here = slice(place * rows, (place + 1) * rows)
        key_grad = score_scale * key_total[here, :]
        unit = ref[0, 0].astype(jnp.float32) * k_rms[here, :]
        k_gain_sum = k_gain_sum + jnp.sum(key_grad * unit, axis=0, keepdims=True)
        outs[0][0] = key_grad.astype(outs[0].dtype)
        outs[1][0] = value_total[here, :].astype(outs[1].dtype)
    gains_ref[0:1, :] += q_gain_sum
    gains_ref[1:2, :] += k_gain_sum


def closed(shard_ref, own, returned, swapped, kind, head):
    keep = jnp.where(shard_ref[0] % 2 == 1, 0.0, 1.0)
    own, returned = (part[kind, head].astype(jnp.float32) for part in (own, returned))
    return own + returned + keep * swapped[kind][head].astype(jnp.float32)


def close_kernel(shard_ref, own, returned, swapped_k, swapped_v, raw_ref, k_gain_ref, out):
    swapped = (swapped_k, swapped_v)
    for head in range(own.shape[1]):
        grad = closed(shard_ref, own, returned, swapped, 0, head)
        raw = raw_ref[0, head].astype(jnp.float32)
        grad = norm_back(grad, raw, inverse_rms_of(raw), k_gain_ref[...])
        out[0, head] = grad.astype(out.dtype)
        out[1, head] = closed(shard_ref, own, returned, swapped, 1, head).astype(out.dtype)


def finish_kernel(shard_ref, own, returned, swapped_k, swapped_v, raw_ref, k_gain_ref, *rest):
    swapped = (swapped_k, swapped_v)
    *done, key_out, value_out, by_token = rest
    rows, heads, _ = key_out.shape
    before = [(part, head) for part in done for head in range(part.shape[1])]
    for kind, out in ((0, key_out), (1, value_out)):
        for place, (part, head) in enumerate(before):
            by_token[pl.ds(place, rows, stride=heads), :] = part[kind, head].astype(jnp.float32)
        for head in range(own.shape[1]):
            grad = closed(shard_ref, own, returned, swapped, kind, head)
            if kind == 0:
                raw = raw_ref[0, head].astype(jnp.float32)
                grad = norm_back(grad, raw, inverse_rms_of(raw), k_gain_ref[...])
            by_token[pl.ds(len(before) + head, rows, stride=heads), :] = grad
        out[...] = by_token[...].reshape(out.shape).astype(out.dtype)


def pack_kernel(first, key_ref, value_ref, out_ref, by_token):
    tokens, heads, _ = key_ref.shape
    for kind, ref in enumerate((key_ref, value_ref)):
        by_token[...] = ref[...].astype(jnp.float32).reshape(by_token.shape)
        for head in range(out_ref.shape[1]):
            part = by_token[pl.ds(first + head, tokens, stride=heads), :]
            out_ref[kind, head] = part.astype(out_ref.dtype)


def pack(key, value, first, count):
    rows, heads, width = key.shape
    tokens = rows // 2
    part = pl.BlockSpec((tokens, heads, width), lambda step: (step, 0, 0))
    return pl.pallas_call(
        functools.partial(pack_kernel, first),
        grid=(rows // tokens,),
        in_specs=[part, part],
        out_specs=pl.BlockSpec((2, count, tokens, width), lambda step: (0, 0, step, 0)),
        out_shape=jax.ShapeDtypeStruct((2, count, rows, width), key.dtype),
        scratch_shapes=[pltpu.VMEM((tokens * heads, width), jnp.float32)],
        compiler_params=pltpu.CompilerParams(vmem_limit_bytes=12 * 1024 * 1024),
        cost_estimate=LIGHT,
    )(key, value)


def choose_kernel(shard_ref, far_ref, own_ref, out_ref):
    odd = shard_ref[0] % 2 == 1

    @pl.when(odd)
    def _():
        out_ref[...] = far_ref[...]

    @pl.when(jnp.logical_not(odd))
    def _():
        out_ref[...] = own_ref[...]


def relay_kernel(shard_ref, far_ref, swapped_k_ref, swapped_v_ref, out_ref):
    odd = jnp.where(shard_ref[0] % 2 == 1, 1.0, 0.0)
    for kind, ref in enumerate((swapped_k_ref, swapped_v_ref)):
        total = far_ref[kind].astype(jnp.float32) + odd * ref[...].astype(jnp.float32)
        out_ref[kind] = total.astype(out_ref.dtype)


def choose(shard, far, own, here, count):
    _, _, rows, width = own.shape
    held = pl.BlockSpec((2, 1, rows, width), lambda head: (0, here + head, 0, 0))
    return pl.pallas_call(
        choose_kernel,
        grid=(count,),
        in_specs=[pl.BlockSpec(memory_space=pltpu.SMEM), held, held],
        out_specs=pl.BlockSpec((2, 1, rows, width), lambda head: (0, head, 0, 0)),
        out_shape=jax.ShapeDtypeStruct((2, count, rows, width), own.dtype),
        compiler_params=pltpu.CompilerParams(vmem_limit_bytes=8 * 1024 * 1024),
        cost_estimate=LIGHT,
    )(shard, far, own)


def small_call(kernel, shard, *arrays):
    smem, vmem = (pl.BlockSpec(memory_space=space) for space in (pltpu.SMEM, pltpu.VMEM))
    return pl.pallas_call(
        kernel,
        in_specs=[smem] + [vmem] * len(arrays),
        out_specs=vmem,
        out_shape=jax.ShapeDtypeStruct(arrays[0].shape, arrays[0].dtype),
        compiler_params=pltpu.CompilerParams(vmem_limit_bytes=12 * 1024 * 1024),
        cost_estimate=LIGHT,
    )(shard, *arrays)


def later_kernel(corner_ref, in_ref, out_ref):
    if len(in_ref.shape) == 1:
        out_ref[0] = in_ref[0]
    else:
        out_ref[...] = in_ref[...]


def later(array, small, cost=None):
    vmem = pl.BlockSpec(memory_space=pltpu.VMEM)
    held = pl.BlockSpec(memory_space=pltpu.SMEM if small.ndim == 1 else pltpu.VMEM)
    return pl.pallas_call(
        later_kernel,
        in_specs=[vmem, held],
        out_specs=held,
        out_shape=jax.ShapeDtypeStruct(small.shape, small.dtype),
        compiler_params=pltpu.CompilerParams(vmem_limit_bytes=1024 * 1024),
        cost_estimate=cost or HEAVY,
    )(array[0, 0, :16], small)


def group_grads(shard, first, here, count, queries, grads, own, near, far, q_gain, k_gain, dq):
    _, _, rows, width = own.shape
    query_rows = queries.shape[1]
    span = WINDOW + rows
    group = query_rows // rows
    whole_q = pl.BlockSpec((1, query_rows, width), lambda head: (first + head, 0, 0))
    part = pl.BlockSpec((2, 1, rows, width), lambda head: (0, head, 0, 0))
    held = pl.BlockSpec((2, 1, rows, width), lambda head: (0, here + head, 0, 0))
    half = pl.BlockSpec((1, rows, width), lambda head: (head, 0, 0))
    gain = pl.BlockSpec((1, width), lambda head: (0, 0))
    shape = (2, count, rows, width)
    return pl.pallas_call(
        heads_kernel,
        grid=(count,),
        in_specs=[
            pl.BlockSpec(memory_space=pltpu.SMEM), whole_q, whole_q, held, part, held, gain, gain,
            pl.BlockSpec(memory_space=pl.ANY),
        ],
        out_specs=[
            pl.BlockSpec((rows, 1, group, width), lambda head: (0, first + head, 0, 0)),
            part,
            half,
            half,
            part,
            pl.BlockSpec((2, width), lambda head: (0, 0)),
        ],
        out_shape=[
            jax.ShapeDtypeStruct(dq.shape, dq.dtype),
            jax.ShapeDtypeStruct(shape, jnp.bfloat16),
            jax.ShapeDtypeStruct(shape[1:], jnp.bfloat16),
            jax.ShapeDtypeStruct(shape[1:], jnp.bfloat16),
            jax.ShapeDtypeStruct(shape, jnp.bfloat16),
            jax.ShapeDtypeStruct((2, width), jnp.float32),
        ],
        scratch_shapes=[
            pltpu.VMEM((span, width), jnp.bfloat16),
            pltpu.VMEM((width, span), jnp.bfloat16),
            pltpu.VMEM((span, width), jnp.float32),
            pltpu.VMEM((span, width), jnp.bfloat16),
            pltpu.VMEM((query_rows, width), jnp.bfloat16),
            pltpu.VMEM((query_rows, width), jnp.float32),
            pltpu.VMEM((span, width), jnp.float32),
            pltpu.VMEM((span, width), jnp.float32),
        ],
        input_output_aliases={8: 0},
        compiler_params=pltpu.CompilerParams(vmem_limit_bytes=22 * 1024 * 1024),
        cost_estimate=LIGHT,
    )(shard, queries, grads, own, near, far, q_gain, k_gain, dq)


def close_group(shard, own, returned, swapped, raw, k_gain):
    smem, vmem = (pl.BlockSpec(memory_space=space) for space in (pltpu.SMEM, pltpu.VMEM))
    return pl.pallas_call(
        close_kernel,
        in_specs=[smem] + [vmem] * 6,
        out_specs=vmem,
        out_shape=jax.ShapeDtypeStruct(own.shape, jnp.bfloat16),
        compiler_params=pltpu.CompilerParams(vmem_limit_bytes=12 * 1024 * 1024),
        cost_estimate=LIGHT,
    )(shard, own, returned, *swapped, raw, k_gain)


def finish(shard, own, returned, swapped, raw, k_gain, done):
    _, count, rows, width = own.shape
    kv_dev = count + sum(part.shape[1] for part in done)
    shape = (rows, kv_dev, width)
    smem, vmem = (pl.BlockSpec(memory_space=space) for space in (pltpu.SMEM, pltpu.VMEM))
    return pl.pallas_call(
        finish_kernel,
        in_specs=[smem] + [vmem] * (6 + len(done)),
        out_specs=[vmem, vmem],
        out_shape=[jax.ShapeDtypeStruct(shape, jnp.bfloat16)] * 2,
        scratch_shapes=[pltpu.VMEM((rows * kv_dev, width), jnp.float32)],
        compiler_params=pltpu.CompilerParams(vmem_limit_bytes=20 * 1024 * 1024),
    )(shard, own, returned, *swapped, raw, k_gain, *done)


def group_sizes(kv_dev):
    count = min(GROUPS, kv_dev)
    return [(kv_dev + count - 1 - place) // count for place in range(count)]


def exchanged(value, *bits):
    count = lax.axis_size(("seq", "head"))
    assert count & (count - 1) == 0
    masks = [1 << bit for bit in bits]
    masks += [sum(masks)] if len(masks) > 1 else []
    return [
        lax.ppermute(value, ("seq", "head"), [(source, source ^ mask) for source in range(count)])
        for mask in masks
    ]


def summed(value, others):
    return value + others[0] if len(others) == 1 else (value + others[0]) + (others[1] + others[2])


def per_device(query, key, value, grad_out, q_gain, k_gain):
    rows, heads, width = query.shape
    kv_dev = key.shape[1]
    group = heads // kv_dev
    count = lax.axis_size("seq")
    assert 2 * rows == WINDOW and rows % TILE == 0 and count % 2 == 0
    shard = lax.axis_index("seq")
    ahead = [(source, source + 2) for source in range(count - 2)]
    back = [(source + 2, source) for source in range(count - 2)]
    swap = [(source, source ^ 1) for source in range(count)]

    def by_head(array):
        split = array.reshape(rows, kv_dev, group, width)
        return jnp.transpose(split, (1, 0, 2, 3)).reshape(kv_dev, rows * group, width)

    sizes = group_sizes(kv_dev)
    starts = [sum(sizes[:place]) for place in range(len(sizes))]
    cuts = [(0, sizes[0])] + ([(sizes[0], kv_dev)] if len(sizes) > 1 else [])
    owns = [pack(key, value, low, high - low) for low, high in cuts]
    fars = [lax.ppermute(own, "seq", ahead) for own in owns]
    queries, grads = by_head(query), by_head(grad_out)
    scalar = shard.astype(jnp.int32).reshape(1)
    q_gain_2d, k_gain_2d = q_gain.reshape(1, width), k_gain.reshape(1, width)

    def split(d_own, d_near_k, d_near_v, d_far, raw):
        swapped = [lax.ppermute(half, "seq", swap) for half in (d_near_k, d_near_v)]
        relayed = small_call(relay_kernel, scalar, d_far, *swapped)
        return relayed, (d_own, swapped, raw)

    def close(stays, returned):
        d_own, swapped, raw = stays
        return close_group(scalar, d_own, returned, swapped, raw, k_gain_2d)

    gains, kept, done = [], [], []
    grad_query = jnp.zeros((rows, kv_dev, group, width), query.dtype)
    grads_out = None
    for place, (first, size) in enumerate(zip(starts, sizes, strict=True)):
        if grads_out is not None:
            relayed, stays = split(*grads_out)
        if place < 2:
            own, far, start = owns[place], fars[place], cuts[place][0]
            if place:
                far, gains[0], relayed = lax.optimization_barrier((far, gains[0], relayed))
            else:
                far, queries, grads, *_ = lax.optimization_barrier(
                    (far, queries, grads, *owns[1:])
                )
        elif place:
            far, gains[-1] = lax.optimization_barrier((far, gains[-1]))
        chosen = choose(scalar, far, own, first - start, size)
        near = lax.ppermute(chosen, "seq", swap)
        scalar_now = scalar
        if grads_out is not None:
            if kept:
                before, returned = kept.pop()
                near, returned = lax.optimization_barrier((near, returned))
                scalar_now = later(returned, scalar, LIGHT)
                done.append(close(before, returned))
            kept.append((stays, lax.ppermute(relayed, "seq", back)))
        here = slice(first - start, first - start + size)
        grad_query, *grads_out, gain = group_grads(
            scalar_now, first, first - start, size, queries, grads, own, near, far,
            q_gain_2d, k_gain_2d, grad_query,
        )
        grads_out.append(own[:1, here])
        gains.append(gain)
    relayed, stays = split(*grads_out)
    head_bits, seq_bits = ((lax.axis_size(axis) - 1).bit_length() for axis in ("head", "seq"))
    assert head_bits and seq_bits > 3
    chips = range(head_bits + 1, head_bits + seq_bits)
    gain_sum = sum(gains[1:], gains[0])
    others = exchanged(gain_sum, chips[0])
    if kept:
        before, returned = kept.pop()
        returned, done = lax.optimization_barrier((returned, done))
        gain_sum = later(returned, gain_sum)
        done.append(close(before, returned))
    gain_sum, others = lax.optimization_barrier((gain_sum, others))
    gain_sum = summed(gain_sum, others)
    returned = lax.ppermute(relayed, "seq", back)
    grad_query = grad_query.reshape(rows, heads, width)
    exchanges = [(0, head_bits), *((bit,) for bit in range(1, head_bits))]
    exchanges += [(bit,) for bit in chips[1:-2]]
    for bits in exchanges:
        gain_sum = summed(gain_sum, exchanged(gain_sum, *bits))
    gain_sum, grad_query, done = lax.optimization_barrier((gain_sum, grad_query, done))
    d_own, swapped, raw = stays
    grad_key, grad_value = finish(scalar, d_own, returned, swapped, raw, k_gain_2d, done)
    others, grad_key = lax.optimization_barrier((exchanged(gain_sum, *chips[-2:]), grad_key))
    gain_sum = summed(gain_sum, others)
    return (grad_query, grad_key, grad_value, gain_sum[0], gain_sum[1])


def solution(mesh):
    split, whole = P("seq", "head", None), P()
    return jax.shard_map(
        per_device,
        mesh=mesh,
        in_specs=(split, split, split, split, whole, whole),
        out_specs=(split, split, split, whole, whole),
        check_vma=False,
    )
```

```python
import functools

import jax
import jax.numpy as jnp
from jax import lax
from jax.experimental import pallas as pl
from jax.experimental.pallas import tpu as pltpu
from jax.sharding import PartitionSpec as P

WINDOW = 1024
TILE = 256

score_scale = 168.0 ** (-0.5)
norm_eps = 1e-06
exp2_scale = score_scale * 1.4426950408889634

GROUPS = 3
HEAVY = pl.CostEstimate(flops=10**11, bytes_accessed=10**8, transcendentals=0)
LIGHT = pl.CostEstimate(flops=1000, bytes_accessed=1000, transcendentals=0)

NT = (((1,), (1,)), ((), ()))


def inverse_rms_of(as_float):
    return lax.rsqrt(jnp.mean(as_float * as_float, axis=-1, keepdims=True) + norm_eps)


def norm_back(d_normed, raw, inverse_rms, gain_vec):
    unit_rows = raw * inverse_rms
    d_unit = d_normed * gain_vec
    return inverse_rms * (
        d_unit - unit_rows * jnp.mean(d_unit * unit_rows, axis=-1, keepdims=True)
    )


def heads_kernel(
    shard_ref, q_ref, g_ref, own_ref, near_ref, far_ref, q_gain_ref, k_gain_ref, _,
    dq_ref, d_own_ref, d_near_k_ref, d_near_v_ref, d_far_ref, gains_ref,
    k_low, k_low_t, k_rms, values, q_low, q_rms, key_total, value_total,
):
    rows = own_ref.shape[2]
    group = q_ref.shape[1] // rows
    lanes = TILE * group
    blocks = rows // TILE
    q_gain, k_gain = q_gain_ref[...], k_gain_ref[...]
    far_ok = jnp.where(shard_ref[0] >= 2, 1.0, 0.0)
    near_ok = jnp.where(shard_ref[0] >= 1, 1.0, 0.0)
    key_refs = (far_ref, near_ref, own_ref)
    grad_refs = (
        (d_far_ref.at[0], d_far_ref.at[1]),
        (d_near_k_ref, d_near_v_ref),
        (d_own_ref.at[0], d_own_ref.at[1]),
    )

    @pl.when(pl.program_id(0) == 0)
    def _():
        gains_ref[...] = jnp.zeros_like(gains_ref)

    for place, ref in enumerate(key_refs):
        raw = ref[0, 0].astype(jnp.float32)
        here = slice(place * rows, (place + 1) * rows)
        inverse_rms = jnp.broadcast_to(inverse_rms_of(raw), raw.shape)
        k_rms[here, :] = inverse_rms
        k_low[here, :] = (raw * inverse_rms * k_gain).astype(jnp.bfloat16)
        values[here, :] = ref[1, 0]
    k_low_t[...] = k_low[...].T
    raw_q = q_ref[0].astype(jnp.float32)
    inverse_rms = jnp.broadcast_to(inverse_rms_of(raw_q), raw_q.shape)
    q_rms[...] = inverse_rms
    q_low[...] = (raw_q * inverse_rms * q_gain).astype(jnp.bfloat16)

    key_ids = lax.broadcasted_iota(jnp.int32, (TILE, lanes), 0)
    token_ids = lax.broadcasted_iota(jnp.int32, (TILE, lanes), 1) // group
    late = key_ids <= token_ids
    edge_ok = jnp.where(late, 1.0, far_ok)
    q_gain_sum = jnp.zeros_like(q_gain)

    for block in range(blocks):
        start = block * TILE
        span = slice(start, start + WINDOW + TILE)
        mine = slice(block * lanes, (block + 1) * lanes)
        scores = lax.dot_general(
            k_low[span, :], q_low[mine, :], NT, preferred_element_type=jnp.float32
        )
        scores = jnp.concatenate(
            [jnp.where(late, scores[WINDOW:], scores[:TILE]), scores[TILE:WINDOW]], axis=0
        )
        exp_scores = jnp.exp2(scores * exp2_scale)
        edge = exp_scores[:TILE] * edge_ok
        first_near = (blocks - block) * TILE
        first_own = first_near + rows
        total = jnp.sum(edge, axis=0, keepdims=True)
        for low, high, ok in (
            (TILE, first_near, far_ok),
            (first_near, min(first_own, WINDOW), near_ok),
            (first_own, WINDOW, None),
        ):
            if low < high:
                part = jnp.sum(exp_scores[low:high], axis=0, keepdims=True)
                total = total + (part if ok is None else part * ok)
        inverse = 1.0 / total
        probs = jnp.concatenate([edge, exp_scores[TILE:]], axis=0) * inverse
        d_probs = lax.dot_general(
            values[span, :], g_ref[0, mine, :], NT, preferred_element_type=jnp.float32
        )
        d_probs = jnp.concatenate(
            [jnp.where(late, d_probs[WINDOW:], d_probs[:TILE]), d_probs[TILE:WINDOW]], axis=0
        )
        offset = jnp.sum(probs * d_probs, axis=0, keepdims=True)
        d_scores = probs * (d_probs - offset)
        probs_low, d_scores_low = (
            jnp.concatenate(
                [jnp.where(late, 0.0, whole[:TILE]), whole[TILE:], jnp.where(late, whole[:TILE], 0.0)],
                axis=0,
            ).astype(jnp.bfloat16)
            for whole in (probs, d_scores)
        )
        query_grad = score_scale * jnp.dot(
            k_low_t[:, span], d_scores_low, preferred_element_type=jnp.float32
        ).T
        for held, left, right in (
            (value_total, probs_low, g_ref[0, mine, :]),
            (key_total, d_scores_low, q_low[mine, :]),
        ):
            part = jnp.dot(left, right, preferred_element_type=jnp.float32)
            if block:
                held[start : start + WINDOW, :] += part[:WINDOW]
                held[start + WINDOW : start + WINDOW + TILE, :] = part[WINDOW:]
            else:
                held[span, :] = part
        raw = q_ref[0, mine, :].astype(jnp.float32)
        inverse_rms = q_rms[mine, :]
        q_gain_sum = q_gain_sum + jnp.sum(query_grad * (raw * inverse_rms), axis=0, keepdims=True)
        query_grad = norm_back(query_grad, raw, inverse_rms, q_gain).astype(dq_ref.dtype)
        dq_ref[start : start + TILE, 0, :, :] = query_grad.reshape(TILE, group, -1)

    k_gain_sum = jnp.zeros_like(k_gain)
    for place, (ref, outs) in enumerate(zip(key_refs, grad_refs, strict=True)):
        here = slice(place * rows, (place + 1) * rows)
        key_grad = score_scale * key_total[here, :]
        unit = ref[0, 0].astype(jnp.float32) * k_rms[here, :]
        k_gain_sum = k_gain_sum + jnp.sum(key_grad * unit, axis=0, keepdims=True)
        outs[0][0] = key_grad.astype(outs[0].dtype)
        outs[1][0] = value_total[here, :].astype(outs[1].dtype)
    gains_ref[0:1, :] += q_gain_sum
    gains_ref[1:2, :] += k_gain_sum


def closed(shard_ref, own, returned, swapped, kind, head):
    keep = jnp.where(shard_ref[0] % 2 == 1, 0.0, 1.0)
    own, returned = (part[kind, head].astype(jnp.float32) for part in (own, returned))
    return own + returned + keep * swapped[kind][head].astype(jnp.float32)


def close_kernel(shard_ref, own, returned, swapped_k, swapped_v, raw_ref, k_gain_ref, out):
    swapped = (swapped_k, swapped_v)
    for head in range(own.shape[1]):
        grad = closed(shard_ref, own, returned, swapped, 0, head)
        raw = raw_ref[0, head].astype(jnp.float32)
        grad = norm_back(grad, raw, inverse_rms_of(raw), k_gain_ref[...])
        out[0, head] = grad.astype(out.dtype)
        out[1, head] = closed(shard_ref, own, returned, swapped, 1, head).astype(out.dtype)


def finish_kernel(shard_ref, own, returned, swapped_k, swapped_v, raw_ref, k_gain_ref, *rest):
    swapped = (swapped_k, swapped_v)
    *done, key_out, value_out, by_token = rest
    rows, heads, _ = key_out.shape
    before = [(part, head) for part in done for head in range(part.shape[1])]
    for kind, out in ((0, key_out), (1, value_out)):
        for place, (part, head) in enumerate(before):
            by_token[pl.ds(place, rows, stride=heads), :] = part[kind, head].astype(jnp.float32)
        for head in range(own.shape[1]):
            grad = closed(shard_ref, own, returned, swapped, kind, head)
            if kind == 0:
                raw = raw_ref[0, head].astype(jnp.float32)
                grad = norm_back(grad, raw, inverse_rms_of(raw), k_gain_ref[...])
            by_token[pl.ds(len(before) + head, rows, stride=heads), :] = grad
        out[...] = by_token[...].reshape(out.shape).astype(out.dtype)


def choose_kernel(shard_ref, far_ref, own_ref, out_ref):
    odd = shard_ref[0] % 2 == 1

    @pl.when(odd)
    def _():
        out_ref[...] = far_ref[...]

    @pl.when(jnp.logical_not(odd))
    def _():
        out_ref[...] = own_ref[...]


def relay_kernel(shard_ref, far_ref, swapped_k_ref, swapped_v_ref, out_ref):
    odd = jnp.where(shard_ref[0] % 2 == 1, 1.0, 0.0)
    for kind, ref in enumerate((swapped_k_ref, swapped_v_ref)):
        total = far_ref[kind].astype(jnp.float32) + odd * ref[...].astype(jnp.float32)
        out_ref[kind] = total.astype(out_ref.dtype)


def choose(shard, far, own, here, count):
    _, _, rows, width = own.shape
    held = pl.BlockSpec((2, 1, rows, width), lambda head: (0, here + head, 0, 0))
    return pl.pallas_call(
        choose_kernel,
        grid=(count,),
        in_specs=[pl.BlockSpec(memory_space=pltpu.SMEM), held, held],
        out_specs=pl.BlockSpec((2, 1, rows, width), lambda head: (0, head, 0, 0)),
        out_shape=jax.ShapeDtypeStruct((2, count, rows, width), own.dtype),
        compiler_params=pltpu.CompilerParams(vmem_limit_bytes=8 * 1024 * 1024),
        cost_estimate=LIGHT,
    )(shard, far, own)


def small_call(kernel, shard, *arrays):
    smem, vmem = (pl.BlockSpec(memory_space=space) for space in (pltpu.SMEM, pltpu.VMEM))
    return pl.pallas_call(
        kernel,
        in_specs=[smem] + [vmem] * len(arrays),
        out_specs=vmem,
        out_shape=jax.ShapeDtypeStruct(arrays[0].shape, arrays[0].dtype),
        compiler_params=pltpu.CompilerParams(vmem_limit_bytes=12 * 1024 * 1024),
        cost_estimate=LIGHT,
    )(shard, *arrays)


def later_kernel(corner_ref, in_ref, out_ref):
    if len(in_ref.shape) == 1:
        out_ref[0] = in_ref[0]
    else:
        out_ref[...] = in_ref[...]


def later(array, small, cost=None):
    vmem = pl.BlockSpec(memory_space=pltpu.VMEM)
    held = pl.BlockSpec(memory_space=pltpu.SMEM if small.ndim == 1 else pltpu.VMEM)
    return pl.pallas_call(
        later_kernel,
        in_specs=[vmem, held],
        out_specs=held,
        out_shape=jax.ShapeDtypeStruct(small.shape, small.dtype),
        compiler_params=pltpu.CompilerParams(vmem_limit_bytes=1024 * 1024),
        cost_estimate=cost or HEAVY,
    )(array[0, 0, :16], small)


def group_grads(shard, first, here, count, queries, grads, own, near, far, q_gain, k_gain, dq):
    _, _, rows, width = own.shape
    query_rows = queries.shape[1]
    span = WINDOW + rows
    group = query_rows // rows
    whole_q = pl.BlockSpec((1, query_rows, width), lambda head: (first + head, 0, 0))
    part = pl.BlockSpec((2, 1, rows, width), lambda head: (0, head, 0, 0))
    held = pl.BlockSpec((2, 1, rows, width), lambda head: (0, here + head, 0, 0))
    half = pl.BlockSpec((1, rows, width), lambda head: (head, 0, 0))
    gain = pl.BlockSpec((1, width), lambda head: (0, 0))
    shape = (2, count, rows, width)
    return pl.pallas_call(
        heads_kernel,
        grid=(count,),
        in_specs=[
            pl.BlockSpec(memory_space=pltpu.SMEM), whole_q, whole_q, held, part, held, gain, gain,
            pl.BlockSpec(memory_space=pl.ANY),
        ],
        out_specs=[
            pl.BlockSpec((rows, 1, group, width), lambda head: (0, first + head, 0, 0)),
            part,
            half,
            half,
            part,
            pl.BlockSpec((2, width), lambda head: (0, 0)),
        ],
        out_shape=[
            jax.ShapeDtypeStruct(dq.shape, dq.dtype),
            jax.ShapeDtypeStruct(shape, jnp.bfloat16),
            jax.ShapeDtypeStruct(shape[1:], jnp.bfloat16),
            jax.ShapeDtypeStruct(shape[1:], jnp.bfloat16),
            jax.ShapeDtypeStruct(shape, jnp.bfloat16),
            jax.ShapeDtypeStruct((2, width), jnp.float32),
        ],
        scratch_shapes=[
            pltpu.VMEM((span, width), jnp.bfloat16),
            pltpu.VMEM((width, span), jnp.bfloat16),
            pltpu.VMEM((span, width), jnp.float32),
            pltpu.VMEM((span, width), jnp.bfloat16),
            pltpu.VMEM((query_rows, width), jnp.bfloat16),
            pltpu.VMEM((query_rows, width), jnp.float32),
            pltpu.VMEM((span, width), jnp.float32),
            pltpu.VMEM((span, width), jnp.float32),
        ],
        input_output_aliases={8: 0},
        compiler_params=pltpu.CompilerParams(vmem_limit_bytes=22 * 1024 * 1024),
        cost_estimate=LIGHT,
    )(shard, queries, grads, own, near, far, q_gain, k_gain, dq)


def close_group(shard, own, returned, swapped, raw, k_gain):
    smem, vmem = (pl.BlockSpec(memory_space=space) for space in (pltpu.SMEM, pltpu.VMEM))
    return pl.pallas_call(
        close_kernel,
        in_specs=[smem] + [vmem] * 6,
        out_specs=vmem,
        out_shape=jax.ShapeDtypeStruct(own.shape, jnp.bfloat16),
        compiler_params=pltpu.CompilerParams(vmem_limit_bytes=12 * 1024 * 1024),
        cost_estimate=LIGHT,
    )(shard, own, returned, *swapped, raw, k_gain)


def finish(shard, own, returned, swapped, raw, k_gain, done):
    _, count, rows, width = own.shape
    kv_dev = count + sum(part.shape[1] for part in done)
    shape = (rows, kv_dev, width)
    smem, vmem = (pl.BlockSpec(memory_space=space) for space in (pltpu.SMEM, pltpu.VMEM))
    return pl.pallas_call(
        finish_kernel,
        in_specs=[smem] + [vmem] * (6 + len(done)),
        out_specs=[vmem, vmem],
        out_shape=[jax.ShapeDtypeStruct(shape, jnp.bfloat16)] * 2,
        scratch_shapes=[pltpu.VMEM((rows * kv_dev, width), jnp.float32)],
        compiler_params=pltpu.CompilerParams(vmem_limit_bytes=20 * 1024 * 1024),
    )(shard, own, returned, *swapped, raw, k_gain, *done)


def group_sizes(kv_dev):
    count = min(GROUPS, kv_dev)
    return [(kv_dev + count - 1 - place) // count for place in range(count)]


def exchanged(value, *bits):
    count = lax.axis_size(("seq", "head"))
    assert count & (count - 1) == 0
    masks = [1 << bit for bit in bits]
    masks += [sum(masks)] if len(masks) > 1 else []
    return [
        lax.ppermute(value, ("seq", "head"), [(source, source ^ mask) for source in range(count)])
        for mask in masks
    ]


def summed(value, others):
    return value + others[0] if len(others) == 1 else (value + others[0]) + (others[1] + others[2])


def per_device(query, key, value, grad_out, q_gain, k_gain):
    rows, heads, width = query.shape
    kv_dev = key.shape[1]
    group = heads // kv_dev
    count = lax.axis_size("seq")
    assert 2 * rows == WINDOW and rows % TILE == 0 and count % 2 == 0
    shard = lax.axis_index("seq")
    ahead = [(source, source + 2) for source in range(count - 2)]
    back = [(source + 2, source) for source in range(count - 2)]
    swap = [(source, source ^ 1) for source in range(count)]

    def by_head(array):
        split = array.reshape(rows, kv_dev, group, width)
        return jnp.transpose(split, (1, 0, 2, 3)).reshape(kv_dev, rows * group, width)

    sizes = group_sizes(kv_dev)
    starts = [sum(sizes[:place]) for place in range(len(sizes))]
    cuts = [(0, sizes[0])] + ([(sizes[0], kv_dev)] if len(sizes) > 1 else [])
    by_kind = lax.optimization_barrier([jnp.transpose(kind, (1, 0, 2)) for kind in (key, value)])
    owns = [jnp.stack([kind[low:high] for kind in by_kind]) for low, high in cuts]
    fars = [lax.ppermute(own, "seq", ahead) for own in owns]
    queries, grads = by_head(query), by_head(grad_out)
    scalar = shard.astype(jnp.int32).reshape(1)
    q_gain_2d, k_gain_2d = q_gain.reshape(1, width), k_gain.reshape(1, width)

    def split(d_own, d_near_k, d_near_v, d_far, raw):
        swapped = [lax.ppermute(half, "seq", swap) for half in (d_near_k, d_near_v)]
        relayed = small_call(relay_kernel, scalar, d_far, *swapped)
        return relayed, (d_own, swapped, raw)

    def close(stays, returned):
        d_own, swapped, raw = stays
        return close_group(scalar, d_own, returned, swapped, raw, k_gain_2d)

    gains, kept, done = [], [], []
    grad_query = jnp.zeros((rows, kv_dev, group, width), query.dtype)
    grads_out = None
    for place, (first, size) in enumerate(zip(starts, sizes, strict=True)):
        if grads_out is not None:
            relayed, stays = split(*grads_out)
        if place < 2:
            own, far, start = owns[place], fars[place], cuts[place][0]
            if place:
                far, gains[0], relayed = lax.optimization_barrier((far, gains[0], relayed))
            else:
                far, queries, grads, *_ = lax.optimization_barrier(
                    (far, queries, grads, *owns[1:])
                )
        elif place:
            far, gains[-1] = lax.optimization_barrier((far, gains[-1]))
        chosen = choose(scalar, far, own, first - start, size)
        near = lax.ppermute(chosen, "seq", swap)
        scalar_now = scalar
        if grads_out is not None:
            if kept:
                before, returned = kept.pop()
                near, returned = lax.optimization_barrier((near, returned))
                scalar_now = later(returned, scalar, LIGHT)
                done.append(close(before, returned))
            kept.append((stays, lax.ppermute(relayed, "seq", back)))
        here = slice(first - start, first - start + size)
        grad_query, *grads_out, gain = group_grads(
            scalar_now, first, first - start, size, queries, grads, own, near, far,
            q_gain_2d, k_gain_2d, grad_query,
        )
        grads_out.append(own[:1, here])
        gains.append(gain)
    relayed, stays = split(*grads_out)
    head_bits, seq_bits = ((lax.axis_size(axis) - 1).bit_length() for axis in ("head", "seq"))
    assert head_bits and seq_bits > 3
    chips = range(head_bits + 1, head_bits + seq_bits)
    gain_sum = sum(gains[1:], gains[0])
    others = exchanged(gain_sum, chips[0])
    if kept:
        before, returned = kept.pop()
        returned, done = lax.optimization_barrier((returned, done))
        gain_sum = later(returned, gain_sum)
        done.append(close(before, returned))
    gain_sum, others = lax.optimization_barrier((gain_sum, others))
    gain_sum = summed(gain_sum, others)
    returned = lax.ppermute(relayed, "seq", back)
    grad_query = grad_query.reshape(rows, heads, width)
    exchanges = [(0, head_bits), *((bit,) for bit in range(1, head_bits))]
    exchanges += [(bit,) for bit in chips[1:-2]]
    for bits in exchanges:
        gain_sum = summed(gain_sum, exchanged(gain_sum, *bits))
    gain_sum, grad_query, done = lax.optimization_barrier((gain_sum, grad_query, done))
    d_own, swapped, raw = stays
    grad_key, grad_value = finish(scalar, d_own, returned, swapped, raw, k_gain_2d, done)
    others, grad_key = lax.optimization_barrier((exchanged(gain_sum, *chips[-2:]), grad_key))
    gain_sum = summed(gain_sum, others)
    return (grad_query, grad_key, grad_value, gain_sum[0], gain_sum[1])


def solution(mesh):
    split, whole = P("seq", "head", None), P()
    return jax.shard_map(
        per_device,
        mesh=mesh,
        in_specs=(split, split, split, split, whole, whole),
        out_specs=(split, split, split, whole, whole),
        check_vma=False,
    )
```

```python
import functools

import jax
import jax.numpy as jnp
from jax import lax
from jax.experimental import pallas as pl
from jax.experimental.pallas import tpu as pltpu
from jax.sharding import PartitionSpec as P

WINDOW = 1024
TILE = 256

score_scale = 168.0 ** (-0.5)
norm_eps = 1e-06
exp2_scale = score_scale * 1.4426950408889634

GROUPS = 3
HEAVY = pl.CostEstimate(flops=10**11, bytes_accessed=10**8, transcendentals=0)
LIGHT = pl.CostEstimate(flops=1000, bytes_accessed=1000, transcendentals=0)

NT = (((1,), (1,)), ((), ()))


def inverse_rms_of(as_float):
    return lax.rsqrt(jnp.mean(as_float * as_float, axis=-1, keepdims=True) + norm_eps)


def norm_back(d_normed, raw, inverse_rms, gain_vec):
    unit_rows = raw * inverse_rms
    d_unit = d_normed * gain_vec
    return inverse_rms * (
        d_unit - unit_rows * jnp.mean(d_unit * unit_rows, axis=-1, keepdims=True)
    )


def heads_kernel(
    shard_ref, q_ref, g_ref, own_ref, near_ref, far_ref, q_gain_ref, k_gain_ref, _,
    dq_ref, d_own_ref, d_near_k_ref, d_near_v_ref, d_far_ref, gains_ref,
    k_low, k_low_t, k_rms, values, q_low, q_rms, key_total, value_total,
):
    rows = own_ref.shape[2]
    group = q_ref.shape[1] // rows
    lanes = TILE * group
    blocks = rows // TILE
    q_gain, k_gain = q_gain_ref[...], k_gain_ref[...]
    far_ok = jnp.where(shard_ref[0] >= 2, 1.0, 0.0)
    near_ok = jnp.where(shard_ref[0] >= 1, 1.0, 0.0)
    key_refs = (far_ref, near_ref, own_ref)
    grad_refs = (
        (d_far_ref.at[0], d_far_ref.at[1]),
        (d_near_k_ref, d_near_v_ref),
        (d_own_ref.at[0], d_own_ref.at[1]),
    )

    @pl.when(pl.program_id(0) == 0)
    def _():
        gains_ref[...] = jnp.zeros_like(gains_ref)

    for place, ref in enumerate(key_refs):
        raw = ref[0, 0].astype(jnp.float32)
        here = slice(place * rows, (place + 1) * rows)
        inverse_rms = jnp.broadcast_to(inverse_rms_of(raw), raw.shape)
        k_rms[here, :] = inverse_rms
        k_low[here, :] = (raw * inverse_rms * k_gain).astype(jnp.bfloat16)
        values[here, :] = ref[1, 0]
    k_low_t[...] = k_low[...].T
    raw_q = q_ref[0].astype(jnp.float32)
    inverse_rms = jnp.broadcast_to(inverse_rms_of(raw_q), raw_q.shape)
    q_rms[...] = inverse_rms
    q_low[...] = (raw_q * inverse_rms * q_gain).astype(jnp.bfloat16)

    key_ids = lax.broadcasted_iota(jnp.int32, (TILE, lanes), 0)
    token_ids = lax.broadcasted_iota(jnp.int32, (TILE, lanes), 1) // group
    late = key_ids <= token_ids
    edge_ok = jnp.where(late, 1.0, far_ok)
    q_gain_sum = jnp.zeros_like(q_gain)

    for block in range(blocks):
        start = block * TILE
        span = slice(start, start + WINDOW + TILE)
        mine = slice(block * lanes, (block + 1) * lanes)
        scores = lax.dot_general(
            k_low[span, :], q_low[mine, :], NT, preferred_element_type=jnp.float32
        )
        scores = jnp.concatenate(
            [jnp.where(late, scores[WINDOW:], scores[:TILE]), scores[TILE:WINDOW]], axis=0
        )
        exp_scores = jnp.exp2(scores * exp2_scale)
        edge = exp_scores[:TILE] * edge_ok
        first_near = (blocks - block) * TILE
        first_own = first_near + rows
        total = jnp.sum(edge, axis=0, keepdims=True)
        for low, high, ok in (
            (TILE, first_near, far_ok),
            (first_near, min(first_own, WINDOW), near_ok),
            (first_own, WINDOW, None),
        ):
            if low < high:
                part = jnp.sum(exp_scores[low:high], axis=0, keepdims=True)
                total = total + (part if ok is None else part * ok)
        inverse = 1.0 / total
        probs = jnp.concatenate([edge, exp_scores[TILE:]], axis=0) * inverse
        d_probs = lax.dot_general(
            values[span, :], g_ref[0, mine, :], NT, preferred_element_type=jnp.float32
        )
        d_probs = jnp.concatenate(
            [jnp.where(late, d_probs[WINDOW:], d_probs[:TILE]), d_probs[TILE:WINDOW]], axis=0
        )
        offset = jnp.sum(probs * d_probs, axis=0, keepdims=True)
        d_scores = probs * (d_probs - offset)
        probs_low, d_scores_low = (
            jnp.concatenate(
                [jnp.where(late, 0.0, whole[:TILE]), whole[TILE:], jnp.where(late, whole[:TILE], 0.0)],
                axis=0,
            ).astype(jnp.bfloat16)
            for whole in (probs, d_scores)
        )
        query_grad = score_scale * jnp.dot(
            k_low_t[:, span], d_scores_low, preferred_element_type=jnp.float32
        ).T
        for held, left, right in (
            (value_total, probs_low, g_ref[0, mine, :]),
            (key_total, d_scores_low, q_low[mine, :]),
        ):
            part = jnp.dot(left, right, preferred_element_type=jnp.float32)
            if block:
                held[start : start + WINDOW, :] += part[:WINDOW]
                held[start + WINDOW : start + WINDOW + TILE, :] = part[WINDOW:]
            else:
                held[span, :] = part
        raw = q_ref[0, mine, :].astype(jnp.float32)
        inverse_rms = q_rms[mine, :]
        q_gain_sum = q_gain_sum + jnp.sum(query_grad * (raw * inverse_rms), axis=0, keepdims=True)
        query_grad = norm_back(query_grad, raw, inverse_rms, q_gain).astype(dq_ref.dtype)
        dq_ref[start : start + TILE, 0, :, :] = query_grad.reshape(TILE, group, -1)

    k_gain_sum = jnp.zeros_like(k_gain)
    for place, (ref, outs) in enumerate(zip(key_refs, grad_refs, strict=True)):
        here = slice(place * rows, (place + 1) * rows)
        key_grad = score_scale * key_total[here, :]
        unit = ref[0, 0].astype(jnp.float32) * k_rms[here, :]
        k_gain_sum = k_gain_sum + jnp.sum(key_grad * unit, axis=0, keepdims=True)
        outs[0][0] = key_grad.astype(outs[0].dtype)
        outs[1][0] = value_total[here, :].astype(outs[1].dtype)
    gains_ref[0:1, :] += q_gain_sum
    gains_ref[1:2, :] += k_gain_sum


def closed(shard_ref, own, returned, swapped, kind, head):
    keep = jnp.where(shard_ref[0] % 2 == 1, 0.0, 1.0)
    own, returned = (part[kind, head].astype(jnp.float32) for part in (own, returned))
    return own + returned + keep * swapped[kind][head].astype(jnp.float32)


def close_kernel(shard_ref, own, returned, swapped_k, swapped_v, raw_ref, k_gain_ref, out):
    swapped = (swapped_k, swapped_v)
    for head in range(own.shape[1]):
        grad = closed(shard_ref, own, returned, swapped, 0, head)
        raw = raw_ref[0, head].astype(jnp.float32)
        grad = norm_back(grad, raw, inverse_rms_of(raw), k_gain_ref[...])
        out[0, head] = grad.astype(out.dtype)
        out[1, head] = closed(shard_ref, own, returned, swapped, 1, head).astype(out.dtype)


def finish_kernel(shard_ref, own, returned, swapped_k, swapped_v, raw_ref, k_gain_ref, *rest):
    swapped = (swapped_k, swapped_v)
    *done, key_out, value_out, by_token = rest
    rows, heads, _ = key_out.shape
    before = [(part, head) for part in done for head in range(part.shape[1])]
    for kind, out in ((0, key_out), (1, value_out)):
        for place, (part, head) in enumerate(before):
            by_token[pl.ds(place, rows, stride=heads), :] = part[kind, head].astype(jnp.float32)
        for head in range(own.shape[1]):
            grad = closed(shard_ref, own, returned, swapped, kind, head)
            if kind == 0:
                raw = raw_ref[0, head].astype(jnp.float32)
                grad = norm_back(grad, raw, inverse_rms_of(raw), k_gain_ref[...])
            by_token[pl.ds(len(before) + head, rows, stride=heads), :] = grad
        out[...] = by_token[...].reshape(out.shape).astype(out.dtype)


def choose_kernel(shard_ref, far_ref, own_ref, out_ref):
    odd = shard_ref[0] % 2 == 1

    @pl.when(odd)
    def _():
        out_ref[...] = far_ref[...]

    @pl.when(jnp.logical_not(odd))
    def _():
        out_ref[...] = own_ref[...]


def relay_kernel(shard_ref, far_ref, swapped_k_ref, swapped_v_ref, out_ref):
    odd = jnp.where(shard_ref[0] % 2 == 1, 1.0, 0.0)
    for kind, ref in enumerate((swapped_k_ref, swapped_v_ref)):
        total = far_ref[kind].astype(jnp.float32) + odd * ref[...].astype(jnp.float32)
        out_ref[kind] = total.astype(out_ref.dtype)


def choose(shard, far, own, here, count):
    _, _, rows, width = own.shape
    held = pl.BlockSpec((2, 1, rows, width), lambda head: (0, here + head, 0, 0))
    return pl.pallas_call(
        choose_kernel,
        grid=(count,),
        in_specs=[pl.BlockSpec(memory_space=pltpu.SMEM), held, held],
        out_specs=pl.BlockSpec((2, 1, rows, width), lambda head: (0, head, 0, 0)),
        out_shape=jax.ShapeDtypeStruct((2, count, rows, width), own.dtype),
        compiler_params=pltpu.CompilerParams(vmem_limit_bytes=8 * 1024 * 1024),
        cost_estimate=LIGHT,
    )(shard, far, own)


def small_call(kernel, shard, *arrays):
    smem, vmem = (pl.BlockSpec(memory_space=space) for space in (pltpu.SMEM, pltpu.VMEM))
    return pl.pallas_call(
        kernel,
        in_specs=[smem] + [vmem] * len(arrays),
        out_specs=vmem,
        out_shape=jax.ShapeDtypeStruct(arrays[0].shape, arrays[0].dtype),
        compiler_params=pltpu.CompilerParams(vmem_limit_bytes=12 * 1024 * 1024),
        cost_estimate=LIGHT,
    )(shard, *arrays)


def later_kernel(corner_ref, in_ref, out_ref):
    if len(in_ref.shape) == 1:
        out_ref[0] = in_ref[0]
    else:
        out_ref[...] = in_ref[...]


def later(array, small, cost=None):
    vmem = pl.BlockSpec(memory_space=pltpu.VMEM)
    held = pl.BlockSpec(memory_space=pltpu.SMEM if small.ndim == 1 else pltpu.VMEM)
    return pl.pallas_call(
        later_kernel,
        in_specs=[vmem, held],
        out_specs=held,
        out_shape=jax.ShapeDtypeStruct(small.shape, small.dtype),
        compiler_params=pltpu.CompilerParams(vmem_limit_bytes=1024 * 1024),
        cost_estimate=cost or HEAVY,
    )(array[0, 0, :16], small)


def group_grads(shard, first, here, count, queries, grads, own, near, far, q_gain, k_gain, dq):
    _, _, rows, width = own.shape
    query_rows = queries.shape[1]
    span = WINDOW + rows
    group = query_rows // rows
    whole_q = pl.BlockSpec((1, query_rows, width), lambda head: (first + head, 0, 0))
    part = pl.BlockSpec((2, 1, rows, width), lambda head: (0, head, 0, 0))
    held = pl.BlockSpec((2, 1, rows, width), lambda head: (0, here + head, 0, 0))
    half = pl.BlockSpec((1, rows, width), lambda head: (head, 0, 0))
    gain = pl.BlockSpec((1, width), lambda head: (0, 0))
    shape = (2, count, rows, width)
    return pl.pallas_call(
        heads_kernel,
        grid=(count,),
        in_specs=[
            pl.BlockSpec(memory_space=pltpu.SMEM), whole_q, whole_q, held, part, held, gain, gain,
            pl.BlockSpec(memory_space=pl.ANY),
        ],
        out_specs=[
            pl.BlockSpec((rows, 1, group, width), lambda head: (0, first + head, 0, 0)),
            part,
            half,
            half,
            part,
            pl.BlockSpec((2, width), lambda head: (0, 0)),
        ],
        out_shape=[
            jax.ShapeDtypeStruct(dq.shape, dq.dtype),
            jax.ShapeDtypeStruct(shape, jnp.bfloat16),
            jax.ShapeDtypeStruct(shape[1:], jnp.bfloat16),
            jax.ShapeDtypeStruct(shape[1:], jnp.bfloat16),
            jax.ShapeDtypeStruct(shape, jnp.bfloat16),
            jax.ShapeDtypeStruct((2, width), jnp.float32),
        ],
        scratch_shapes=[
            pltpu.VMEM((span, width), jnp.bfloat16),
            pltpu.VMEM((width, span), jnp.bfloat16),
            pltpu.VMEM((span, width), jnp.float32),
            pltpu.VMEM((span, width), jnp.bfloat16),
            pltpu.VMEM((query_rows, width), jnp.bfloat16),
            pltpu.VMEM((query_rows, width), jnp.float32),
            pltpu.VMEM((span, width), jnp.float32),
            pltpu.VMEM((span, width), jnp.float32),
        ],
        input_output_aliases={8: 0},
        compiler_params=pltpu.CompilerParams(vmem_limit_bytes=22 * 1024 * 1024),
        cost_estimate=LIGHT,
    )(shard, queries, grads, own, near, far, q_gain, k_gain, dq)


def close_group(shard, own, returned, swapped, raw, k_gain):
    smem, vmem = (pl.BlockSpec(memory_space=space) for space in (pltpu.SMEM, pltpu.VMEM))
    return pl.pallas_call(
        close_kernel,
        in_specs=[smem] + [vmem] * 6,
        out_specs=vmem,
        out_shape=jax.ShapeDtypeStruct(own.shape, jnp.bfloat16),
        compiler_params=pltpu.CompilerParams(vmem_limit_bytes=12 * 1024 * 1024),
        cost_estimate=LIGHT,
    )(shard, own, returned, *swapped, raw, k_gain)


def finish(shard, own, returned, swapped, raw, k_gain, done):
    _, count, rows, width = own.shape
    kv_dev = count + sum(part.shape[1] for part in done)
    shape = (rows, kv_dev, width)
    smem, vmem = (pl.BlockSpec(memory_space=space) for space in (pltpu.SMEM, pltpu.VMEM))
    return pl.pallas_call(
        finish_kernel,
        in_specs=[smem] + [vmem] * (6 + len(done)),
        out_specs=[vmem, vmem],
        out_shape=[jax.ShapeDtypeStruct(shape, jnp.bfloat16)] * 2,
        scratch_shapes=[pltpu.VMEM((rows * kv_dev, width), jnp.float32)],
        compiler_params=pltpu.CompilerParams(vmem_limit_bytes=20 * 1024 * 1024),
    )(shard, own, returned, *swapped, raw, k_gain, *done)


def group_sizes(kv_dev):
    count = min(GROUPS, kv_dev)
    return [(kv_dev + count - 1 - place) // count for place in range(count)]


def exchanged(value, *bits):
    count = lax.axis_size(("seq", "head"))
    assert count & (count - 1) == 0
    masks = [1 << bit for bit in bits]
    masks += [sum(masks)] if len(masks) > 1 else []
    return [
        lax.ppermute(value, ("seq", "head"), [(source, source ^ mask) for source in range(count)])
        for mask in masks
    ]


def summed(value, others):
    return value + others[0] if len(others) == 1 else (value + others[0]) + (others[1] + others[2])


def per_device(query, key, value, grad_out, q_gain, k_gain):
    rows, heads, width = query.shape
    kv_dev = key.shape[1]
    group = heads // kv_dev
    count = lax.axis_size("seq")
    assert 2 * rows == WINDOW and rows % TILE == 0 and count % 2 == 0
    shard = lax.axis_index("seq")
    ahead = [(source, source + 2) for source in range(count - 2)]
    back = [(source + 2, source) for source in range(count - 2)]
    swap = [(source, source ^ 1) for source in range(count)]

    def by_head(array):
        split = array.reshape(rows, kv_dev, group, width)
        return jnp.transpose(split, (1, 0, 2, 3)).reshape(kv_dev, rows * group, width)

    sizes = group_sizes(kv_dev)
    starts = [sum(sizes[:place]) for place in range(len(sizes))]
    cuts = [(0, sizes[0])] + ([(sizes[0], kv_dev)] if len(sizes) > 1 else [])
    by_kind = lax.optimization_barrier([jnp.transpose(kind, (1, 0, 2)) for kind in (key, value)])
    owns = [jnp.stack([kind[low:high] for kind in by_kind]) for low, high in cuts]
    fars = [lax.ppermute(own, "seq", ahead) for own in owns]
    queries, grads = by_head(query), by_head(grad_out)
    scalar = shard.astype(jnp.int32).reshape(1)
    q_gain_2d, k_gain_2d = q_gain.reshape(1, width), k_gain.reshape(1, width)

    def split(d_own, d_near_k, d_near_v, d_far, raw):
        swapped = [lax.ppermute(half, "seq", swap) for half in (d_near_k, d_near_v)]
        relayed = small_call(relay_kernel, scalar, d_far, *swapped)
        return relayed, (d_own, swapped, raw)

    def close(stays, returned):
        d_own, swapped, raw = stays
        return close_group(scalar, d_own, returned, swapped, raw, k_gain_2d)

    gains, kept, done = [], [], []
    grad_query = jnp.zeros((rows, kv_dev, group, width), query.dtype)
    grads_out = None
    for place, (first, size) in enumerate(zip(starts, sizes, strict=True)):
        if grads_out is not None:
            relayed, stays = split(*grads_out)
        if place < 2:
            own, far, start = owns[place], fars[place], cuts[place][0]
            if place:
                far, gains[0], relayed = lax.optimization_barrier((far, gains[0], relayed))
            else:
                far, queries, grads, *_ = lax.optimization_barrier(
                    (far, queries, grads, *owns[1:])
                )
        elif place:
            far, gains[-1] = lax.optimization_barrier((far, gains[-1]))
        chosen = choose(scalar, far, own, first - start, size)
        near = lax.ppermute(chosen, "seq", swap)
        scalar_now = scalar
        if grads_out is not None:
            if kept:
                before, returned = kept.pop()
                near, returned = lax.optimization_barrier((near, returned))
                scalar_now = later(returned, scalar, LIGHT)
                done.append(close(before, returned))
            kept.append((stays, lax.ppermute(relayed, "seq", back)))
        here = slice(first - start, first - start + size)
        grad_query, *grads_out, gain = group_grads(
            scalar_now, first, first - start, size, queries, grads, own, near, far,
            q_gain_2d, k_gain_2d, grad_query,
        )
        grads_out.append(own[:1, here])
        gains.append(gain)
    relayed, stays = split(*grads_out)
    head_bits, seq_bits = ((lax.axis_size(axis) - 1).bit_length() for axis in ("head", "seq"))
    assert head_bits and seq_bits > 3
    chips = range(head_bits + 1, head_bits + seq_bits)
    gain_sum = sum(gains[1:], gains[0])
    others = exchanged(gain_sum, chips[0])
    if kept:
        before, returned = kept.pop()
        returned, done = lax.optimization_barrier((returned, done))
        gain_sum = later(returned, gain_sum)
        done.append(close(before, returned))
    gain_sum, others = lax.optimization_barrier((gain_sum, others))
    gain_sum = summed(gain_sum, others)
    returned = lax.ppermute(relayed, "seq", back)
    grad_query = grad_query.reshape(rows, heads, width)
    exchanges = [(0, head_bits), *((bit,) for bit in range(1, head_bits))]
    exchanges += [(bit,) for bit in chips[1:-1]]
    for bits in exchanges:
        gain_sum = summed(gain_sum, exchanged(gain_sum, *bits))
    gain_sum, grad_query, done = lax.optimization_barrier((gain_sum, grad_query, done))
    d_own, swapped, raw = stays
    grad_key, grad_value = finish(scalar, d_own, returned, swapped, raw, k_gain_2d, done)
    others, grad_key = lax.optimization_barrier((exchanged(gain_sum, chips[-1]), grad_key))
    gain_sum = summed(gain_sum, others)
    return (grad_query, grad_key, grad_value, gain_sum[0], gain_sum[1])


def solution(mesh):
    split, whole = P("seq", "head", None), P()
    return jax.shard_map(
        per_device,
        mesh=mesh,
        in_specs=(split, split, split, split, whole, whole),
        out_specs=(split, split, split, whole, whole),
        check_vma=False,
    )
```

```python
import functools

import jax
import jax.numpy as jnp
from jax import lax
from jax.experimental import pallas as pl
from jax.experimental.pallas import tpu as pltpu
from jax.sharding import PartitionSpec as P

WINDOW = 1024
TILE = 256

score_scale = 168.0 ** (-0.5)
norm_eps = 1e-06
exp2_scale = score_scale * 1.4426950408889634

GROUPS = 3
HEAVY = pl.CostEstimate(flops=10**11, bytes_accessed=10**8, transcendentals=0)
LIGHT = pl.CostEstimate(flops=1000, bytes_accessed=1000, transcendentals=0)

NT = (((1,), (1,)), ((), ()))


def inverse_rms_of(as_float):
    return lax.rsqrt(jnp.mean(as_float * as_float, axis=-1, keepdims=True) + norm_eps)


def norm_back(d_normed, raw, inverse_rms, gain_vec):
    unit_rows = raw * inverse_rms
    d_unit = d_normed * gain_vec
    return inverse_rms * (
        d_unit - unit_rows * jnp.mean(d_unit * unit_rows, axis=-1, keepdims=True)
    )


def heads_kernel(
    shard_ref, q_ref, g_ref, own_ref, near_ref, far_ref, q_gain_ref, k_gain_ref, _,
    dq_ref, d_own_ref, d_near_k_ref, d_near_v_ref, d_far_ref, gains_ref,
    k_low, k_low_t, k_rms, values, q_low, q_rms, key_total, value_total,
):
    rows = own_ref.shape[2]
    group = q_ref.shape[1] // rows
    lanes = TILE * group
    blocks = rows // TILE
    q_gain, k_gain = q_gain_ref[...], k_gain_ref[...]
    far_ok = jnp.where(shard_ref[0] >= 2, 1.0, 0.0)
    near_ok = jnp.where(shard_ref[0] >= 1, 1.0, 0.0)
    key_refs = (far_ref, near_ref, own_ref)
    grad_refs = (
        (d_far_ref.at[0], d_far_ref.at[1]),
        (d_near_k_ref, d_near_v_ref),
        (d_own_ref.at[0], d_own_ref.at[1]),
    )

    @pl.when(pl.program_id(0) == 0)
    def _():
        gains_ref[...] = jnp.zeros_like(gains_ref)

    for place, ref in enumerate(key_refs):
        raw = ref[0, 0].astype(jnp.float32)
        here = slice(place * rows, (place + 1) * rows)
        inverse_rms = jnp.broadcast_to(inverse_rms_of(raw), raw.shape)
        k_rms[here, :] = inverse_rms
        k_low[here, :] = (raw * inverse_rms * k_gain).astype(jnp.bfloat16)
        values[here, :] = ref[1, 0]
    k_low_t[...] = k_low[...].T
    raw_q = q_ref[0].astype(jnp.float32)
    inverse_rms = jnp.broadcast_to(inverse_rms_of(raw_q), raw_q.shape)
    q_rms[...] = inverse_rms
    q_low[...] = (raw_q * inverse_rms * q_gain).astype(jnp.bfloat16)

    key_ids = lax.broadcasted_iota(jnp.int32, (TILE, lanes), 0)
    token_ids = lax.broadcasted_iota(jnp.int32, (TILE, lanes), 1) // group
    late = key_ids <= token_ids
    edge_ok = jnp.where(late, 1.0, far_ok)
    q_gain_sum = jnp.zeros_like(q_gain)

    for block in range(blocks):
        start = block * TILE
        span = slice(start, start + WINDOW + TILE)
        mine = slice(block * lanes, (block + 1) * lanes)
        scores = lax.dot_general(
            k_low[span, :], q_low[mine, :], NT, preferred_element_type=jnp.float32
        )
        scores = jnp.concatenate(
            [jnp.where(late, scores[WINDOW:], scores[:TILE]), scores[TILE:WINDOW]], axis=0
        )
        exp_scores = jnp.exp2(scores * exp2_scale)
        edge = exp_scores[:TILE] * edge_ok
        first_near = (blocks - block) * TILE
        first_own = first_near + rows
        total = jnp.sum(edge, axis=0, keepdims=True)
        for low, high, ok in (
            (TILE, first_near, far_ok),
            (first_near, min(first_own, WINDOW), near_ok),
            (first_own, WINDOW, None),
        ):
            if low < high:
                part = jnp.sum(exp_scores[low:high], axis=0, keepdims=True)
                total = total + (part if ok is None else part * ok)
        inverse = 1.0 / total
        probs = jnp.concatenate([edge, exp_scores[TILE:]], axis=0) * inverse
        d_probs = lax.dot_general(
            values[span, :], g_ref[0, mine, :], NT, preferred_element_type=jnp.float32
        )
        d_probs = jnp.concatenate(
            [jnp.where(late, d_probs[WINDOW:], d_probs[:TILE]), d_probs[TILE:WINDOW]], axis=0
        )
        offset = jnp.sum(probs * d_probs, axis=0, keepdims=True)
        d_scores = probs * (d_probs - offset)
        probs_low, d_scores_low = (
            jnp.concatenate(
                [jnp.where(late, 0.0, whole[:TILE]), whole[TILE:], jnp.where(late, whole[:TILE], 0.0)],
                axis=0,
            ).astype(jnp.bfloat16)
            for whole in (probs, d_scores)
        )
        query_grad = score_scale * jnp.dot(
            k_low_t[:, span], d_scores_low, preferred_element_type=jnp.float32
        ).T
        for held, left, right in (
            (value_total, probs_low, g_ref[0, mine, :]),
            (key_total, d_scores_low, q_low[mine, :]),
        ):
            part = jnp.dot(left, right, preferred_element_type=jnp.float32)
            if block:
                held[start : start + WINDOW, :] += part[:WINDOW]
                held[start + WINDOW : start + WINDOW + TILE, :] = part[WINDOW:]
            else:
                held[span, :] = part
        raw = q_ref[0, mine, :].astype(jnp.float32)
        inverse_rms = q_rms[mine, :]
        q_gain_sum = q_gain_sum + jnp.sum(query_grad * (raw * inverse_rms), axis=0, keepdims=True)
        query_grad = norm_back(query_grad, raw, inverse_rms, q_gain).astype(dq_ref.dtype)
        dq_ref[start : start + TILE, 0, :, :] = query_grad.reshape(TILE, group, -1)

    k_gain_sum = jnp.zeros_like(k_gain)
    for place, (ref, outs) in enumerate(zip(key_refs, grad_refs, strict=True)):
        here = slice(place * rows, (place + 1) * rows)
        key_grad = score_scale * key_total[here, :]
        unit = ref[0, 0].astype(jnp.float32) * k_rms[here, :]
        k_gain_sum = k_gain_sum + jnp.sum(key_grad * unit, axis=0, keepdims=True)
        outs[0][0] = key_grad.astype(outs[0].dtype)
        outs[1][0] = value_total[here, :].astype(outs[1].dtype)
    gains_ref[0:1, :] += q_gain_sum
    gains_ref[1:2, :] += k_gain_sum


def closed(shard_ref, own, returned, swapped, kind, head):
    keep = jnp.where(shard_ref[0] % 2 == 1, 0.0, 1.0)
    own, returned = (part[kind, head].astype(jnp.float32) for part in (own, returned))
    return own + returned + keep * swapped[kind][head].astype(jnp.float32)


def close_kernel(shard_ref, own, returned, swapped_k, swapped_v, raw_ref, k_gain_ref, out):
    swapped = (swapped_k, swapped_v)
    for head in range(own.shape[1]):
        grad = closed(shard_ref, own, returned, swapped, 0, head)
        raw = raw_ref[0, head].astype(jnp.float32)
        grad = norm_back(grad, raw, inverse_rms_of(raw), k_gain_ref[...])
        out[0, head] = grad.astype(out.dtype)
        out[1, head] = closed(shard_ref, own, returned, swapped, 1, head).astype(out.dtype)


def finish_kernel(shard_ref, own, returned, swapped_k, swapped_v, raw_ref, k_gain_ref, *rest):
    swapped = (swapped_k, swapped_v)
    *done, key_out, value_out, by_token = rest
    rows, heads, _ = key_out.shape
    before = [(part, head) for part in done for head in range(part.shape[1])]
    for kind, out in ((0, key_out), (1, value_out)):
        for place, (part, head) in enumerate(before):
            by_token[pl.ds(place, rows, stride=heads), :] = part[kind, head].astype(jnp.float32)
        for head in range(own.shape[1]):
            grad = closed(shard_ref, own, returned, swapped, kind, head)
            if kind == 0:
                raw = raw_ref[0, head].astype(jnp.float32)
                grad = norm_back(grad, raw, inverse_rms_of(raw), k_gain_ref[...])
            by_token[pl.ds(len(before) + head, rows, stride=heads), :] = grad
        out[...] = by_token[...].reshape(out.shape).astype(out.dtype)


def pack_kernel(first, key_ref, value_ref, out_ref, by_token):
    tokens, heads, _ = key_ref.shape
    for kind, ref in enumerate((key_ref, value_ref)):
        by_token[...] = ref[...].astype(jnp.float32).reshape(by_token.shape)
        for head in range(out_ref.shape[1]):
            part = by_token[pl.ds(first + head, tokens, stride=heads), :]
            out_ref[kind, head] = part.astype(out_ref.dtype)


def pack(key, value, first, count):
    rows, heads, width = key.shape
    tokens = rows // 2
    part = pl.BlockSpec((tokens, heads, width), lambda step: (step, 0, 0))
    return pl.pallas_call(
        functools.partial(pack_kernel, first),
        grid=(rows // tokens,),
        in_specs=[part, part],
        out_specs=pl.BlockSpec((2, count, tokens, width), lambda step: (0, 0, step, 0)),
        out_shape=jax.ShapeDtypeStruct((2, count, rows, width), key.dtype),
        scratch_shapes=[pltpu.VMEM((tokens * heads, width), jnp.float32)],
        compiler_params=pltpu.CompilerParams(vmem_limit_bytes=56 * 1024 * 1024),
        cost_estimate=LIGHT,
    )(key, value)


def choose_kernel(shard_ref, far_ref, own_ref, out_ref):
    odd = shard_ref[0] % 2 == 1

    @pl.when(odd)
    def _():
        out_ref[...] = far_ref[...]

    @pl.when(jnp.logical_not(odd))
    def _():
        out_ref[...] = own_ref[...]


def relay_kernel(shard_ref, far_ref, swapped_k_ref, swapped_v_ref, out_ref):
    odd = jnp.where(shard_ref[0] % 2 == 1, 1.0, 0.0)
    for kind, ref in enumerate((swapped_k_ref, swapped_v_ref)):
        total = far_ref[kind].astype(jnp.float32) + odd * ref[...].astype(jnp.float32)
        out_ref[kind] = total.astype(out_ref.dtype)


def choose(shard, far, own, here, count):
    _, _, rows, width = own.shape
    held = pl.BlockSpec((2, 1, rows, width), lambda head: (0, here + head, 0, 0))
    return pl.pallas_call(
        choose_kernel,
        grid=(count,),
        in_specs=[pl.BlockSpec(memory_space=pltpu.SMEM), held, held],
        out_specs=pl.BlockSpec((2, 1, rows, width), lambda head: (0, head, 0, 0)),
        out_shape=jax.ShapeDtypeStruct((2, count, rows, width), own.dtype),
        compiler_params=pltpu.CompilerParams(vmem_limit_bytes=8 * 1024 * 1024),
        cost_estimate=LIGHT,
    )(shard, far, own)


def small_call(kernel, shard, *arrays):
    smem, vmem = (pl.BlockSpec(memory_space=space) for space in (pltpu.SMEM, pltpu.VMEM))
    return pl.pallas_call(
        kernel,
        in_specs=[smem] + [vmem] * len(arrays),
        out_specs=vmem,
        out_shape=jax.ShapeDtypeStruct(arrays[0].shape, arrays[0].dtype),
        compiler_params=pltpu.CompilerParams(vmem_limit_bytes=12 * 1024 * 1024),
        cost_estimate=LIGHT,
    )(shard, *arrays)


def later_kernel(corner_ref, in_ref, out_ref):
    if len(in_ref.shape) == 1:
        out_ref[0] = in_ref[0]
    else:
        out_ref[...] = in_ref[...]


def later(array, small, cost=None):
    vmem = pl.BlockSpec(memory_space=pltpu.VMEM)
    held = pl.BlockSpec(memory_space=pltpu.SMEM if small.ndim == 1 else pltpu.VMEM)
    return pl.pallas_call(
        later_kernel,
        in_specs=[vmem, held],
        out_specs=held,
        out_shape=jax.ShapeDtypeStruct(small.shape, small.dtype),
        compiler_params=pltpu.CompilerParams(vmem_limit_bytes=1024 * 1024),
        cost_estimate=cost or HEAVY,
    )(array[0, 0, :16], small)


def group_grads(shard, first, here, count, queries, grads, own, near, far, q_gain, k_gain, dq):
    _, _, rows, width = own.shape
    query_rows = queries.shape[1]
    span = WINDOW + rows
    group = query_rows // rows
    whole_q = pl.BlockSpec((1, query_rows, width), lambda head: (first + head, 0, 0))
    part = pl.BlockSpec((2, 1, rows, width), lambda head: (0, head, 0, 0))
    held = pl.BlockSpec((2, 1, rows, width), lambda head: (0, here + head, 0, 0))
    half = pl.BlockSpec((1, rows, width), lambda head: (head, 0, 0))
    gain = pl.BlockSpec((1, width), lambda head: (0, 0))
    shape = (2, count, rows, width)
    return pl.pallas_call(
        heads_kernel,
        grid=(count,),
        in_specs=[
            pl.BlockSpec(memory_space=pltpu.SMEM), whole_q, whole_q, held, part, held, gain, gain,
            pl.BlockSpec(memory_space=pl.ANY),
        ],
        out_specs=[
            pl.BlockSpec((rows, 1, group, width), lambda head: (0, first + head, 0, 0)),
            part,
            half,
            half,
            part,
            pl.BlockSpec((2, width), lambda head: (0, 0)),
        ],
        out_shape=[
            jax.ShapeDtypeStruct(dq.shape, dq.dtype),
            jax.ShapeDtypeStruct(shape, jnp.bfloat16),
            jax.ShapeDtypeStruct(shape[1:], jnp.bfloat16),
            jax.ShapeDtypeStruct(shape[1:], jnp.bfloat16),
            jax.ShapeDtypeStruct(shape, jnp.bfloat16),
            jax.ShapeDtypeStruct((2, width), jnp.float32),
        ],
        scratch_shapes=[
            pltpu.VMEM((span, width), jnp.bfloat16),
            pltpu.VMEM((width, span), jnp.bfloat16),
            pltpu.VMEM((span, width), jnp.float32),
            pltpu.VMEM((span, width), jnp.bfloat16),
            pltpu.VMEM((query_rows, width), jnp.bfloat16),
            pltpu.VMEM((query_rows, width), jnp.float32),
            pltpu.VMEM((span, width), jnp.float32),
            pltpu.VMEM((span, width), jnp.float32),
        ],
        input_output_aliases={8: 0},
        compiler_params=pltpu.CompilerParams(vmem_limit_bytes=22 * 1024 * 1024),
        cost_estimate=LIGHT,
    )(shard, queries, grads, own, near, far, q_gain, k_gain, dq)


def close_group(shard, own, returned, swapped, raw, k_gain):
    smem, vmem = (pl.BlockSpec(memory_space=space) for space in (pltpu.SMEM, pltpu.VMEM))
    return pl.pallas_call(
        close_kernel,
        in_specs=[smem] + [vmem] * 6,
        out_specs=vmem,
        out_shape=jax.ShapeDtypeStruct(own.shape, jnp.bfloat16),
        compiler_params=pltpu.CompilerParams(vmem_limit_bytes=12 * 1024 * 1024),
        cost_estimate=LIGHT,
    )(shard, own, returned, *swapped, raw, k_gain)


def finish(shard, own, returned, swapped, raw, k_gain, done):
    _, count, rows, width = own.shape
    kv_dev = count + sum(part.shape[1] for part in done)
    shape = (rows, kv_dev, width)
    smem, vmem = (pl.BlockSpec(memory_space=space) for space in (pltpu.SMEM, pltpu.VMEM))
    return pl.pallas_call(
        finish_kernel,
        in_specs=[smem] + [vmem] * (6 + len(done)),
        out_specs=[vmem, vmem],
        out_shape=[jax.ShapeDtypeStruct(shape, jnp.bfloat16)] * 2,
        scratch_shapes=[pltpu.VMEM((rows * kv_dev, width), jnp.float32)],
        compiler_params=pltpu.CompilerParams(vmem_limit_bytes=20 * 1024 * 1024),
    )(shard, own, returned, *swapped, raw, k_gain, *done)


def group_sizes(kv_dev):
    count = min(GROUPS, kv_dev)
    return [(kv_dev + count - 1 - place) // count for place in range(count)]


def exchanged(value, *bits):
    count = lax.axis_size(("seq", "head"))
    assert count & (count - 1) == 0
    masks = [1 << bit for bit in bits]
    masks += [sum(masks)] if len(masks) > 1 else []
    return [
        lax.ppermute(value, ("seq", "head"), [(source, source ^ mask) for source in range(count)])
        for mask in masks
    ]


def summed(value, others):
    return value + others[0] if len(others) == 1 else (value + others[0]) + (others[1] + others[2])


def per_device(query, key, value, grad_out, q_gain, k_gain):
    rows, heads, width = query.shape
    kv_dev = key.shape[1]
    group = heads // kv_dev
    count = lax.axis_size("seq")
    assert 2 * rows == WINDOW and rows % TILE == 0 and count % 2 == 0
    shard = lax.axis_index("seq")
    ahead = [(source, source + 2) for source in range(count - 2)]
    back = [(source + 2, source) for source in range(count - 2)]
    swap = [(source, source ^ 1) for source in range(count)]

    def by_head(array):
        split = array.reshape(rows, kv_dev, group, width)
        return jnp.transpose(split, (1, 0, 2, 3)).reshape(kv_dev, rows * group, width)

    sizes = group_sizes(kv_dev)
    starts = [sum(sizes[:place]) for place in range(len(sizes))]
    cuts = [(0, sizes[0])] + ([(sizes[0], kv_dev)] if len(sizes) > 1 else [])
    owns = [pack(key, value, low, high - low) for low, high in cuts]
    fars = [lax.ppermute(own, "seq", ahead) for own in owns]
    queries, grads = by_head(query), by_head(grad_out)
    scalar = shard.astype(jnp.int32).reshape(1)
    q_gain_2d, k_gain_2d = q_gain.reshape(1, width), k_gain.reshape(1, width)

    def split(d_own, d_near_k, d_near_v, d_far, raw):
        swapped = [lax.ppermute(half, "seq", swap) for half in (d_near_k, d_near_v)]
        relayed = small_call(relay_kernel, scalar, d_far, *swapped)
        return relayed, (d_own, swapped, raw)

    def close(stays, returned):
        d_own, swapped, raw = stays
        return close_group(scalar, d_own, returned, swapped, raw, k_gain_2d)

    gains, kept, done = [], [], []
    grad_query = jnp.zeros((rows, kv_dev, group, width), query.dtype)
    grads_out = None
    for place, (first, size) in enumerate(zip(starts, sizes, strict=True)):
        if grads_out is not None:
            relayed, stays = split(*grads_out)
        if place < 2:
            own, far, start = owns[place], fars[place], cuts[place][0]
            if place:
                far, gains[0], relayed = lax.optimization_barrier((far, gains[0], relayed))
            else:
                far, queries, grads, *_ = lax.optimization_barrier(
                    (far, queries, grads, *owns[1:])
                )
        elif place:
            far, gains[-1] = lax.optimization_barrier((far, gains[-1]))
        chosen = choose(scalar, far, own, first - start, size)
        near = lax.ppermute(chosen, "seq", swap)
        scalar_now = scalar
        if grads_out is not None:
            if kept:
                before, returned = kept.pop()
                near, returned = lax.optimization_barrier((near, returned))
                scalar_now = later(returned, scalar, LIGHT)
                done.append(close(before, returned))
            kept.append((stays, lax.ppermute(relayed, "seq", back)))
        here = slice(first - start, first - start + size)
        grad_query, *grads_out, gain = group_grads(
            scalar_now, first, first - start, size, queries, grads, own, near, far,
            q_gain_2d, k_gain_2d, grad_query,
        )
        grads_out.append(own[:1, here])
        gains.append(gain)
    relayed, stays = split(*grads_out)
    head_bits, seq_bits = ((lax.axis_size(axis) - 1).bit_length() for axis in ("head", "seq"))
    assert head_bits and seq_bits > 3
    chips = range(head_bits + 1, head_bits + seq_bits)
    gain_sum = sum(gains[1:], gains[0])
    others = exchanged(gain_sum, chips[0])
    if kept:
        before, returned = kept.pop()
        returned, done = lax.optimization_barrier((returned, done))
        gain_sum = later(returned, gain_sum)
        done.append(close(before, returned))
    gain_sum, others = lax.optimization_barrier((gain_sum, others))
    gain_sum = summed(gain_sum, others)
    returned = lax.ppermute(relayed, "seq", back)
    grad_query = grad_query.reshape(rows, heads, width)
    exchanges = [(0, head_bits), *((bit,) for bit in range(1, head_bits))]
    exchanges += [(bit,) for bit in chips[1:-2]]
    for bits in exchanges:
        gain_sum = summed(gain_sum, exchanged(gain_sum, *bits))
    gain_sum, grad_query, done = lax.optimization_barrier((gain_sum, grad_query, done))
    d_own, swapped, raw = stays
    grad_key, grad_value = finish(scalar, d_own, returned, swapped, raw, k_gain_2d, done)
    others, grad_key = lax.optimization_barrier((exchanged(gain_sum, *chips[-2:]), grad_key))
    gain_sum = summed(gain_sum, others)
    return (grad_query, grad_key, grad_value, gain_sum[0], gain_sum[1])


def solution(mesh):
    split, whole = P("seq", "head", None), P()
    return jax.shard_map(
        per_device,
        mesh=mesh,
        in_specs=(split, split, split, split, whole, whole),
        out_specs=(split, split, split, whole, whole),
        check_vma=False,
    )
```
